32 devices in a mesh: section: 2 (over core), dp: 4 (over y, x), mp: 4 (over z).
Axes of the slice: x: 2, y: 2, z: 4, core: 2. Of those that a mesh axis runs over, the one named last changes fastest.
Arguments:
- segment_input: bfloat16 [2, 4, 256, 2048], P(None, 'dp', None, 'mp'), may hold values from -6 to 6
- out_grad: bfloat16 [2, 4, 256, 2048], P(None, 'dp', None, 'mp'), may hold values from -6 to 6
- pool_tokens: bfloat16 [16, 4, 128, 896], P('section', 'dp'), may hold values from -6 to 6
- neighbour_ids: int32 [2, 4, 4, 4], P(None, 'dp'), may hold values from 0 to 15, as said below
- neighbour_counts: int32 [2, 4, 4], P(None, 'dp'), may hold values from 1 to 4
- enc_gain: float32 [896], replicated, may hold values from 0.5 to 1.5
- enc_up: bfloat16 [896, 1024], P(None, 'mp'), may hold values from -0.1875 to 0.1875
- enc_down: bfloat16 [1024, 896], P(None, 'mp'), may hold values from -0.1875 to 0.1875
- norm_gain: float32 [2, 2048], P('section'), may hold values from 0.5 to 1.5
- w_query: bfloat16 [2, 2048, 1024], P('section', None, 'mp'), may hold values from -0.125 to 0.125
- w_key: bfloat16 [2, 896, 1024], P('section', None, 'mp'), may hold values from -0.1875 to 0.1875
- w_value: bfloat16 [2, 896, 1024], P('section', None, 'mp'), may hold values from -0.1875 to 0.1875
- w_out: bfloat16 [2, 1024, 2048], P('section', None, 'mp'), may hold values from -0.1875 to 0.1875
Outputs:
- grad_key: bfloat16 [2, 896, 1024], P('section', None, 'mp')
- grad_value: bfloat16 [2, 896, 1024], P('section', None, 'mp')
The draws below stay inside these ranges and needn't reach their ends.
Inputs may be any that keep to these rules, and one draw needn't show every extreme that they name: `neighbour_ids`: the 4 slots of one stretch name distinct pool stretches.
All inputs are finite; a program needn't handle non-finite values.
Results may differ from the reference program's by a relative error of at most 0.025.
Values may be sent and summed in bfloat16 or wider, within the bound.
No kernel may reach another device: no remote copies, remote signals or barrier semaphores. Data moves between devices by JAX's collectives and lax.ppermute only.
A program may use at most 128 MiB of HBM per device.

```python
import jax
import jax.numpy as jnp
from jax import lax

D = 2048
HEAD = 128
ENC = 896
STRETCH = 64
NT = 128
KMAX = 4
MB = 2
CPM = 4
HEADS = 8
HQ = 1024
ENC_FF = 1024
RM = 256
POOL = 16
GROUPS = 4
SECTIONS = 2
N_MP = 4


def draw_neighbour_counts(key, part):
    base = jax.random.randint(jax.random.fold_in(key, 11), (MB * GROUPS * CPM,), 1, KMAX + 1)
    total_count = MB * GROUPS * CPM
    full_place = jax.random.randint(jax.random.fold_in(key, 12), (), 0, total_count)
    low_place = (full_place + 1) % total_count
    positions = jnp.arange(total_count)
    base = jnp.where(positions == full_place, KMAX, base)
    base = jnp.where(positions == low_place, 1, base)
    return base.reshape(MB, GROUPS, CPM).astype(jnp.int32)


def draw_neighbour_ids(key, part):
    total_count = MB * GROUPS * CPM
    row_keys = jax.random.split(jax.random.fold_in(key, 21), total_count)
    picks = jax.vmap(lambda row_key: jax.random.permutation(row_key, POOL)[:KMAX])(row_keys)
    top_place = jax.random.randint(jax.random.fold_in(key, 22), (), 0, total_count)
    bottom_place = (top_place + 1) % total_count
    positions = jnp.arange(total_count)[:, None]
    slot_index = jnp.arange(KMAX)[None, :]
    picks = jnp.where(positions == top_place, POOL - 1 - slot_index, picks)
    picks = jnp.where(positions == bottom_place, slot_index, picks)
    return picks.reshape(MB, GROUPS, CPM, KMAX).astype(jnp.int32)


def level_of(stream_key, shape, pieces, low, high):
    def one(dim, shards_of):
        draws = jax.random.uniform(jax.random.fold_in(jax.random.fold_in(stream_key, 6), dim), (shards_of,), jnp.float32, low / len(pieces), high / len(pieces))
        return jnp.repeat(jnp.exp(draws), shape[dim] // shards_of).reshape((-1,) + (1,) * (len(shape) - dim - 1))

    loudness = one(*pieces[0])
    for cut in pieces[1:]:
        loudness = loudness * one(*cut)
    return loudness


def scatter_about(stream_key, shape, spread, most, cuts=(), kind=jnp.bfloat16):
    entries = spread * jax.random.normal(stream_key, shape, jnp.float32)
    if cuts:
        entries = entries * level_of(stream_key, shape, cuts, -0.22, 0.18)
    return jnp.clip(entries, -most, most).astype(kind)


def setup_inputs(seed: int = 0) -> dict:
    splits = jax.random.split(jax.random.key(seed), 14)
    return {
        "segment_input": scatter_about(splits[0], (MB, GROUPS, RM, D), 1.0, 6.0, ((1, 4), (3, 4))),
        "out_grad": scatter_about(splits[1], (MB, GROUPS, RM, D), 1.0, 6.0, ((1, 4), (3, 4))),
        "pool_tokens": scatter_about(splits[2], (POOL, GROUPS, NT, ENC), 1.0, 6.0, ((0, 2), (1, 4))),
        "neighbour_ids": draw_neighbour_ids(jax.random.fold_in(splits[13], 71), 0),
        "neighbour_counts": draw_neighbour_counts(jax.random.fold_in(splits[13], 71), 0),
        "enc_gain": jnp.clip(1.0 + 0.1 * jax.random.normal(splits[5], (ENC,), jnp.float32), 0.5, 1.5),
        "enc_up": scatter_about(splits[6], (ENC, ENC_FF), ENC ** -0.5, 0.1875, ((1, 4),)),
        "enc_down": scatter_about(splits[7], (ENC_FF, ENC), ENC_FF ** -0.5, 0.1875, ((1, 4),)),
        "norm_gain": jnp.clip(1.0 + 0.1 * jax.random.normal(splits[8], (SECTIONS, D), jnp.float32), 0.5, 1.5),
        "w_query": scatter_about(splits[9], (SECTIONS, D, HQ), D ** -0.5, 0.125, ((0, 2), (2, 4))),
        "w_key": scatter_about(splits[10], (SECTIONS, ENC, HQ), ENC ** -0.5, 0.1875, ((0, 2), (2, 4))),
        "w_value": scatter_about(splits[11], (SECTIONS, ENC, HQ), ENC ** -0.5, 0.1875, ((0, 2), (2, 4))),
        "w_out": scatter_about(splits[12], (SECTIONS, HQ, D), HQ ** -0.5, 0.1875, ((0, 2), (2, 4))),
    }


EPSILON = 1e-05

def to_bf16(values):
    return lax.optimization_barrier(values.astype(jnp.bfloat16))

def rms_scale(values):
    return lax.rsqrt(lax.optimization_barrier(jnp.mean(values * values, axis=-1, keepdims=True)) + EPSILON)

def encode_pool(raw_rows, enc_gain, enc_up, enc_down):
    raw_wide = raw_rows.astype(jnp.float32)
    normed = to_bf16(raw_wide * rms_scale(raw_wide) * enc_gain)
    hidden = to_bf16(jax.nn.gelu(jnp.dot(normed, enc_up, preferred_element_type=jnp.float32)))
    return (raw_wide + jnp.dot(hidden, enc_down, preferred_element_type=jnp.float32)).astype(jnp.bfloat16)

def attend(queries, key_block, value_block, usable):
    scores = jnp.einsum('cqhe,ckhe->chqk', queries.astype(jnp.float32), key_block.astype(jnp.float32))
    scores = jnp.where(usable[:, None, None, :], scores, -1e+30)
    weights = jax.nn.softmax(scores, axis=-1)
    weights_bf = to_bf16(weights)
    attended = jnp.einsum('chqk,ckhe->cqhe', weights_bf.astype(jnp.float32), value_block.astype(jnp.float32))
    return (weights, weights_bf, attended.astype(jnp.bfloat16))

def attend_back(queries, key_block, value_block, weights, weights_bf, grad_attended):
    grad_wide = grad_attended.astype(jnp.float32)
    grad_weights = jnp.einsum('cqhe,ckhe->chqk', grad_wide, value_block.astype(jnp.float32))
    grad_scores = weights * (grad_weights - lax.optimization_barrier(jnp.sum(weights * grad_weights, axis=-1, keepdims=True)))
    grad_values = jnp.einsum('chqk,cqhe->ckhe', weights_bf.astype(jnp.float32), grad_wide).astype(jnp.bfloat16)
    grad_keys = jnp.einsum('chqk,cqhe->ckhe', grad_scores, queries.astype(jnp.float32)).astype(jnp.bfloat16)
    grad_queries = jnp.einsum('chqk,ckhe->cqhe', grad_scores, key_block.astype(jnp.float32))
    return (grad_keys, grad_values, grad_queries)

def reference(segment_input, out_grad, pool_tokens, neighbour_ids, neighbour_counts, enc_gain, enc_up, enc_down, norm_gain, w_query, w_key, w_value, w_out):
    head_scale = HEAD ** (-0.5)
    key_span = KMAX * NT
    segment_params = (norm_gain, w_query, w_key, w_value, w_out)
    contract = (((0,), (0,)), ((), ()))

    def front(rows_in, gain, query_w, key_block, value_block, usable):
        rows_wide = rows_in.astype(jnp.float32)
        inv_rms = rms_scale(rows_wide)
        normed = to_bf16(rows_wide * inv_rms * gain)
        query_raw = jnp.dot(normed, query_w, preferred_element_type=jnp.float32)
        queries = to_bf16(query_raw * head_scale).reshape(CPM, STRETCH, HEADS, HEAD)
        weights, weights_bf, attended = attend(queries, key_block, value_block, usable)
        return (inv_rms, query_raw, queries, weights, weights_bf, attended)

    def one_group(totals, group_data):
        inputs_g, grads_g, raw_g, ids_g, counts_g = group_data
        encoded = encode_pool(raw_g.reshape(POOL * NT, ENC), enc_gain, enc_up, enc_down).reshape(POOL, NT, ENC)
        sum_keys, sum_values = totals
        for micro_index in range(MB):
            neighbours = encoded[ids_g[micro_index]].reshape(CPM * key_span, ENC)
            usable = (jnp.arange(key_span, dtype=jnp.int32) // NT)[None, :] < counts_g[micro_index][:, None]

            def project(weight):
                projected = jnp.dot(neighbours, weight, preferred_element_type=jnp.float32).astype(jnp.bfloat16)
                return projected.reshape(CPM, key_span, HEADS, HEAD)

            def forward(rows_in, params):
                gain, query_w, key_w, value_w, out_w = params
                outputs = front(rows_in, gain, query_w, project(key_w), project(value_w), usable)
                attended = outputs[5].reshape(CPM * STRETCH, HQ)
                result = rows_in.astype(jnp.float32) + jnp.dot(attended, out_w, preferred_element_type=jnp.float32)
                return (result.astype(jnp.bfloat16), rows_in)
            _, saved = lax.scan(forward, inputs_g[micro_index], segment_params)

            def backward(grad_rows, packed):
                rows_in, gain, query_w, key_w, value_w, out_w = packed
                key_block = project(key_w)
                value_block = project(value_w)
                inv_rms, query_raw, queries, weights, weights_bf, _ = front(rows_in, gain, query_w, key_block, value_block, usable)
                grad_att = to_bf16(jnp.dot(grad_rows, out_w.T, preferred_element_type=jnp.float32)).reshape(CPM, STRETCH, HEADS, HEAD)
                grad_keys, grad_values, grad_queries = attend_back(queries, key_block, value_block, weights, weights_bf, grad_att)
                grad_scaled = to_bf16((grad_queries * head_scale).reshape(CPM * STRETCH, HQ))
                part_totals = lax.optimization_barrier(jnp.sum((grad_scaled.astype(jnp.float32) * query_raw).reshape(CPM * STRETCH, N_MP, HQ // N_MP), axis=2))
                row_total = lax.optimization_barrier(jnp.sum(to_bf16(part_totals).astype(jnp.float32), axis=1, keepdims=True))
                grad_normed = jnp.dot(grad_scaled, query_w.T, preferred_element_type=jnp.float32)
                rows_wide = rows_in.astype(jnp.float32)
                grad_in = grad_rows.astype(jnp.float32) + inv_rms * gain * grad_normed - rows_wide * inv_rms * inv_rms * row_total / D
                key_grad = lax.dot_general(neighbours, grad_keys.reshape(CPM * key_span, HQ), contract, preferred_element_type=jnp.float32)
                value_grad = lax.dot_general(neighbours, grad_values.reshape(CPM * key_span, HQ), contract, preferred_element_type=jnp.float32)
                return (grad_in.astype(jnp.bfloat16), (key_grad, value_grad))
            _, (key_grads, value_grads) = lax.scan(backward, grads_g[micro_index], (saved,) + segment_params, reverse=True)
            sum_keys = sum_keys + key_grads
            sum_values = sum_values + value_grads
        return ((sum_keys, sum_values), None)
    group_data = (jnp.moveaxis(segment_input, 1, 0), jnp.moveaxis(out_grad, 1, 0), jnp.moveaxis(pool_tokens, 1, 0), jnp.moveaxis(neighbour_ids, 1, 0), jnp.moveaxis(neighbour_counts, 1, 0))
    start_totals = (jnp.zeros((SECTIONS, ENC, HQ), jnp.float32), jnp.zeros((SECTIONS, ENC, HQ), jnp.float32))
    (sum_keys, sum_values), _ = lax.scan(one_group, start_totals, group_data)
    return (sum_keys.astype(jnp.bfloat16), sum_values.astype(jnp.bfloat16))
```

```python
import functools

import jax
import jax.numpy as jnp
from jax import lax
from jax.experimental import pallas as pl
from jax.experimental.pallas import tpu as pltpu
from jax.sharding import PartitionSpec as P

HEAD = 128
NT = 128
EPSILON = 1e-05
SCALE = HEAD ** (-0.5)
PAD = 16
VMEM_LIMIT = 56 * 1024 * 1024

BF16 = jnp.bfloat16
F32 = jnp.float32
NN = (((1,), (0,)), ((), ()))
NTR = (((1,), (1,)), ((), ()))
TNR = (((0,), (0,)), ((), ()))


def mm(a, b, dims=NN):
    return lax.dot_general(a, b, dims, preferred_element_type=F32)


def xor_move(value, axis, by):
    count = lax.axis_size(axis)
    return lax.ppermute(value, axis, [(i, i ^ by) for i in range(count)])


def swap(value):
    return xor_move(value, "section", 1)


def after(value, *others):
    return lax.optimization_barrier((value,) + others)[0]


def vm():
    return pl.BlockSpec(memory_space=pltpu.VMEM)


def hbm():
    return pl.BlockSpec(memory_space=pl.ANY)


def smem():
    return pl.BlockSpec(memory_space=pltpu.SMEM)


def call(body, outs, specs, scratch=(), flops=0):
    nbytes = sum(o.size * o.dtype.itemsize for o in outs)
    return pl.pallas_call(
        body,
        out_shape=outs,
        in_specs=specs,
        out_specs=[vm() for _ in outs],
        scratch_shapes=list(scratch),
        compiler_params=pltpu.CompilerParams(vmem_limit_bytes=VMEM_LIMIT),
        cost_estimate=pl.CostEstimate(
            flops=flops, bytes_accessed=2 * nbytes, transcendentals=0
        ),
    )


def shape(dims, dtype=BF16):
    return jax.ShapeDtypeStruct(dims, dtype)


def to_row(column):
    rows = column.shape[0]
    here = lax.broadcasted_iota(jnp.int32, (rows, rows), 0)
    there = lax.broadcasted_iota(jnp.int32, (rows, rows), 1)
    return jnp.sum(jnp.where(here == there, column, 0.0), axis=0, keepdims=True)


def to_column(row):
    rows = row.shape[1]
    here = lax.broadcasted_iota(jnp.int32, (rows, rows), 0)
    there = lax.broadcasted_iota(jnp.int32, (rows, rows), 1)
    return jnp.sum(jnp.where(here == there, row, 0.0), axis=1, keepdims=True)


def load_pool(own, other, pool, sems):
    half = own.shape[0]
    s = lax.axis_index("section")
    copies = [
        pltpu.make_async_copy(own, pool.at[pl.ds(s * half, half)], sems.at[0]),
        pltpu.make_async_copy(other, pool.at[pl.ds((1 - s) * half, half)], sems.at[1]),
    ]
    for copy in copies:
        copy.start()
    return copies


def hidden_body(n, parts, gathered, *refs):
    pool_ref, gain_ref = refs[:2]
    if gathered:
        up, out_ref = refs[2:4]
    else:
        pieces, (out_ref, up, sems) = refs[2 : 2 + parts], refs[2 + parts :]
        s, g, m = (lax.axis_index(a) for a in ("section", "dp", "mp"))
        copies = []
        for i, piece in enumerate(pieces):
            half, dg = divmod(i, parts // 2)
            place = (s ^ half) * (parts // 2) + (g ^ dg)
            for dz in range(n):
                copies.append(
                    pltpu.make_async_copy(piece.at[dz], up.at[m ^ dz, place], sems.at[i * n + dz])
                )
        for copy in copies:
            copy.start()
        for copy in copies:
            copy.wait()
    rows, width = pool_ref.shape
    cols = up.shape[-1]
    chunk = 256

    def step(i, _):
        here = pl.ds(pl.multiple_of(i * chunk, chunk), chunk)
        wide = pool_ref[here, :].astype(F32)
        scale = lax.rsqrt(jnp.mean(wide * wide, axis=-1, keepdims=True) + EPSILON)
        normed = (wide * scale * gain_ref[...]).astype(BF16)
        for k in range(n):
            weight = up[k].reshape(width, cols)
            out_ref[here, k * cols : (k + 1) * cols] = jax.nn.gelu(mm(normed, weight)).astype(BF16)
        return 0

    lax.fori_loop(0, rows // chunk, step, 0)


def encoded_body(n, parts, gathered, *refs):
    pool_ref, hidden_ref, kv0_ref, kv1_ref = refs[:4]
    if gathered:
        down, enc_ref, out0_ref, out1_ref = refs[4:]
        weight = down[...]
    else:
        pieces = refs[4 : 4 + parts]
        enc_ref, out0_ref, out1_ref, down, sems = refs[4 + parts :]
        cols = pieces[0].shape[-1]
        s, g, m = (lax.axis_index(a) for a in ("section", "dp", "mp"))
        copies = []
        for i, piece in enumerate(pieces):
            half, dg = divmod(i, parts // 2)
            place = (s ^ half) * (parts // 2) + (g ^ dg)
            where = pl.ds(pl.multiple_of(place * cols, cols), cols)
            for dz in range(n):
                copies.append(
                    pltpu.make_async_copy(
                        piece.at[dz], down.at[m ^ dz, :, where], sems.at[i * n + dz]
                    )
                )
        for copy in copies:
            copy.start()
        for copy in copies:
            copy.wait()
    count, length, width = enc_ref.shape
    group = 2

    def step(i, _):
        here = pl.ds(pl.multiple_of(i * group * length, group * length), group * length)
        there = pl.ds(i * group, group)
        weight = down[...].reshape(width, hidden_ref.shape[1])
        enc = pool_ref[here, :].astype(F32) + mm(hidden_ref[here, :], weight, NTR)
        enc = enc.astype(BF16)
        enc_ref[there] = enc.reshape(group, length, width)
        out0_ref[there] = mm(enc, kv0_ref[...]).astype(BF16).reshape(group, length, -1)
        out1_ref[there] = mm(enc, kv1_ref[...]).astype(BF16).reshape(group, length, -1)
        return 0

    lax.fori_loop(0, count // group, step, 0)


def gather_slots(pool, ids_ref, micro, tract, slots, block):
    for k in range(slots):
        block[k * NT : (k + 1) * NT, :] = pool[ids_ref[micro, tract, k]]


def probabilities(queries, keys, used):
    scores = mm(queries, keys, NTR)
    lane = lax.broadcasted_iota(jnp.int32, scores.shape, 1)
    scores = jnp.where(lane < used * NT, scores, -1e30)
    powers = jnp.exp(scores - jnp.max(scores, axis=-1, keepdims=True))
    return powers / jnp.sum(powers, axis=-1, keepdims=True)


def first_layer_body(n, tracts, slots, *refs):
    ids_ref, counts_ref, gain_ref, wq_ref = refs[:4]
    pieces, (own, other) = refs[4 : 4 + n], refs[4 + n : 6 + n]
    att_ref, query_ref, probs_ref, pool, block, sems = refs[6 + n :]
    copies = load_pool(own, other, pool, sems)
    s, m = lax.axis_index("section"), lax.axis_index("mp")
    rows, feats = pieces[0].shape
    cols = wq_ref.shape[1]
    total = jnp.zeros((rows, 1), F32)
    for d in range(n):
        wide = pieces[d][...].astype(F32)
        total = total + jnp.sum(wide * wide, axis=-1, keepdims=True)
    scale = lax.rsqrt(total / (n * feats) + EPSILON)
    raw = jnp.zeros((rows, cols), F32)
    for d in range(n):
        source = m ^ d
        normed = (pieces[d][...].astype(F32) * scale * gain_ref[source]).astype(BF16)
        here = pl.ds(pl.multiple_of(source * feats, feats), feats)
        raw = raw + mm(normed, wq_ref[here, :])
    query_ref[...] = (raw * SCALE).astype(BF16)
    for copy in copies:
        copy.wait()
    length = rows // tracts
    heads = cols // HEAD
    for c in range(tracts):
        gather_slots(pool, ids_ref, s, c, slots, block)
        here = slice(c * length, (c + 1) * length)
        for h in range(heads):
            there = slice(h * HEAD, (h + 1) * HEAD)
            probs = probabilities(query_ref[here, there], block[:, there], counts_ref[s, c])
            probs_ref[c * heads + h] = probs
            vals = block[:, cols + h * HEAD : cols + (h + 1) * HEAD]
            att_ref[here, there] = mm(probs.astype(BF16), vals).astype(BF16)


def between_body(n, *refs):
    gain_ref, own_ref, wout_ref, wq_ref = refs[:4]
    pieces = refs[4 : 4 + n]
    rows_ref, messages = refs[4 + n], refs[5 + n :]
    m = lax.axis_index("mp")
    cols = pieces[0].shape[1]
    rows = own_ref.shape[0]
    wide = own_ref[...].astype(F32)
    for d in range(n):
        here = pl.ds(pl.multiple_of((m ^ d) * cols, cols), cols)
        wide = wide + mm(pieces[d][...], wout_ref[here, :])
    rounded = wide.astype(BF16)
    rows_ref[...] = rounded
    wide = rounded.astype(F32)
    square = to_row(jnp.sum(wide * wide, axis=-1, keepdims=True))
    high = square.astype(BF16).astype(F32)
    index = lax.broadcasted_iota(jnp.int32, (PAD, rows), 0)
    extra = jnp.where(index == 0, high, jnp.where(index == 1, square - high, 0.0)).astype(BF16)
    gained = (wide * gain_ref[m]).astype(BF16)
    for d in range(n):
        messages[d][:rows, :] = mm(gained, wq_ref[d]).astype(BF16)
        messages[d][rows:, :] = extra


def last_layer_body(n, width, tracts, slots, *refs):
    ids_ref, counts_ref = refs[:2]
    messages, grads = refs[2 : 2 + n], refs[2 + n : 2 + 2 * n]
    own, other, dkv_ref, out_ref, scale_ref, raw_ref, query_ref, att_ref, pool, block, sems = refs[
        2 + 2 * n :
    ]
    copies = load_pool(own, other, pool, sems)
    s = lax.axis_index("section")
    rows, cols = grads[0].shape
    raw = jnp.zeros((rows, cols), F32)
    square = jnp.zeros((1, rows), F32)
    grad = jnp.zeros((rows, cols), F32)
    for d in range(n):
        raw = raw + messages[d][:rows, :].astype(F32)
        extra = messages[d][rows:, :].astype(F32)
        square = square + extra[0:1, :] + extra[1:2, :]
        grad = grad + grads[d][...].astype(F32)
    scale = lax.rsqrt(to_column(square) / width + EPSILON)
    scale_ref[...] = jnp.broadcast_to(scale, scale_ref.shape)
    raw = raw * scale
    raw_ref[...] = raw
    query_ref[...] = (raw * SCALE).astype(BF16)
    att_ref[...] = grad.astype(BF16)
    for copy in copies:
        copy.wait()
    length = rows // tracts
    heads = cols // HEAD
    for c in range(tracts):
        gather_slots(pool, ids_ref, s, c, slots, block)
        here = slice(c * length, (c + 1) * length)
        slot_rows = slice(c * slots * NT, (c + 1) * slots * NT)
        for h in range(heads):
            there = slice(h * HEAD, (h + 1) * HEAD)
            beyond = slice(cols + h * HEAD, cols + (h + 1) * HEAD)
            queries, keys = query_ref[here, there], block[:, there]
            probs = probabilities(queries, keys, counts_ref[s, c])
            grad_att = att_ref[here, there]
            grad_probs = mm(grad_att, block[:, beyond], NTR)
            inner = jnp.sum(probs * grad_probs, axis=-1, keepdims=True)
            scores = (probs * (grad_probs - inner)).astype(BF16)
            dkv_ref[slot_rows, there] = mm(scores, queries, TNR).astype(BF16)
            dkv_ref[slot_rows, beyond] = mm(probs.astype(BF16), grad_att, TNR).astype(BF16)
            out_ref[here, there] = (mm(scores, keys) * SCALE).astype(BF16)
    part = jnp.sum(out_ref[:rows, :].astype(F32) * raw_ref[...], axis=-1, keepdims=True)
    index = lax.broadcasted_iota(jnp.int32, (PAD, rows), 0)
    out_ref[rows:, :] = jnp.where(index == 0, to_row(part), 0.0).astype(BF16)


def weight_grads(enc_ref, dkv_ref, key_ref, value_ref):
    cols = key_ref.shape[1]
    for r in range(0, enc_ref.shape[0], NT):
        total = mm(enc_ref[r : r + NT, :], dkv_ref[...])
        key_ref[r : r + NT, :] = total[:, :cols].astype(BF16)
        value_ref[r : r + NT, :] = total[:, cols:].astype(BF16)


def last_grads_body(tracts, slots, ids_ref, dkv_ref, own, other, enc_ref, key_ref, value_ref, pool, sems):
    copies = load_pool(own, other, pool, sems)
    s = lax.axis_index("section")
    for copy in copies:
        copy.wait()
    for c in range(tracts):
        for k in range(slots):
            place = (c * slots + k) * NT
            enc_ref[:, place : place + NT] = pool[ids_ref[s, c, k]].T
    weight_grads(enc_ref, dkv_ref, key_ref, value_ref)


def back_between_body(n, width, *refs):
    gain_ref, rows_ref, og_ref, scale_ref, wq_ref, wout_ref = refs[:6]
    pieces, messages = refs[6 : 6 + n], refs[6 + n :]
    s, m = lax.axis_index("section"), lax.axis_index("mp")
    rows, feats = rows_ref.shape
    cols = pieces[0].shape[1]
    normed = jnp.zeros((rows, feats), F32)
    total = jnp.zeros((1, rows), F32)
    for d in range(n):
        normed = normed + mm(pieces[d][:rows, :], wq_ref[d], NTR)
        total = total + pieces[d][rows:, :].astype(F32)[0:1, :]
    scale = scale_ref[:, 0:1]
    wide = rows_ref[...].astype(F32)
    grad = og_ref[s].astype(F32) + scale * gain_ref[m] * normed
    grad = grad - wide * (scale * scale * (to_column(total) / width))
    grad = grad.astype(BF16)
    for d in range(n):
        here = pl.ds(pl.multiple_of((m ^ d) * cols, cols), cols)
        messages[d][...] = mm(grad, wout_ref[here, :], NTR).astype(BF16)


def out_grad_body(n, *refs):
    og_ref, wout_ref = refs[:2]
    messages = refs[2:]
    s, m = lax.axis_index("section"), lax.axis_index("mp")
    cols = messages[0].shape[1]
    for d in range(n):
        here = pl.ds(pl.multiple_of((m ^ d) * cols, cols), cols)
        messages[d][...] = mm(og_ref[s], wout_ref[here, :], NTR).astype(BF16)


def first_back_body(n, tracts, slots, *refs):
    ids_ref, query_ref, probs_ref, enc_ref = refs[:4]
    grads = refs[4 : 4 + n]
    own, other, key_ref, value_ref, att_ref, dkv_ref, pool, block, sems = refs[4 + n :]
    copies = load_pool(own, other, pool, sems)
    s = lax.axis_index("section")
    rows, cols = query_ref.shape
    grad = jnp.zeros((rows, cols), F32)
    for d in range(n):
        grad = grad + grads[d][...].astype(F32)
    att_ref[...] = grad.astype(BF16)
    for copy in copies:
        copy.wait()
    length = rows // tracts
    heads = cols // HEAD
    for c in range(tracts):
        gather_slots(pool, ids_ref, s, c, slots, block)
        here = slice(c * length, (c + 1) * length)
        slot_rows = slice(c * slots * NT, (c + 1) * slots * NT)
        for h in range(heads):
            there = slice(h * HEAD, (h + 1) * HEAD)
            beyond = slice(cols + h * HEAD, cols + (h + 1) * HEAD)
            probs = probs_ref[c * heads + h]
            grad_att = att_ref[here, there]
            grad_probs = mm(grad_att, block[:, beyond], NTR)
            inner = jnp.sum(probs * grad_probs, axis=-1, keepdims=True)
            scores = (probs * (grad_probs - inner)).astype(BF16)
            dkv_ref[slot_rows, there] = mm(scores, query_ref[here, there], TNR).astype(BF16)
            dkv_ref[slot_rows, beyond] = mm(probs.astype(BF16), grad_att, TNR).astype(BF16)
    weight_grads(enc_ref, dkv_ref, key_ref, value_ref)


def along_mp(value, n):
    return [value] + [xor_move(value, "mp", d) for d in range(1, n)]


def scattered(messages):
    return [messages[0]] + [xor_move(messages[d], "mp", d) for d in range(1, len(messages))]


def over_dp(value, dp):
    if dp != 4:
        return lax.psum(value, "dp")
    half = value.shape[0] // 2
    parts = [value[:half], value[half:]]
    for order in ((1, 2), (2, 1)):
        moved = [xor_move(part, "dp", by) for part, by in zip(parts, order)]
        parts = [
            (a.astype(F32) + b.astype(F32)).astype(BF16) for a, b in zip(parts, moved)
        ]
    return jnp.concatenate(parts, axis=0)


def spread(along, dp):
    planes = [along] + [xor_move(along, "dp", d) for d in range(1, dp)]
    return planes + [swap(plane) for plane in planes]


def on_device(
    segment_input,
    out_grad,
    pool_tokens,
    neighbour_ids,
    neighbour_counts,
    enc_gain,
    enc_up,
    enc_down,
    norm_gain,
    w_query,
    w_key,
    w_value,
    w_out,
):
    n, dp = lax.axis_size("mp"), lax.axis_size("dp")
    s, g = lax.axis_index("section"), lax.axis_index("dp")
    m = lax.axis_index("mp")
    _, _, rows, feats = segment_input.shape
    width = n * feats
    cols = w_query.shape[2]
    half, _, length, enc_width = pool_tokens.shape
    tracts, slots = neighbour_ids.shape[2:]
    ids, counts = neighbour_ids[:, 0], neighbour_counts[:, 0]
    ff = enc_down.shape[0]
    first = s == 0

    def by_layer(own):
        other = swap(own)
        return jnp.where(first, own, other), jnp.where(first, other, own)

    down_t = enc_down.T
    parts = 2 * dp
    shares = (enc_width // n) % 16 == 0 and (enc_width // parts) % 16 == 0 and ff // parts == 128
    if shares:
        place = s * dp + g
        up_rows, down_cols = enc_width // parts, ff // parts
        up_piece = lax.dynamic_slice_in_dim(enc_up, place * up_rows, up_rows, 0)
        down_piece = lax.dynamic_slice_in_dim(down_t, place * down_cols, down_cols, 1)
        up_line = jnp.stack(along_mp(up_piece, n))
        down_piece = after(down_piece, up_line)
        down_line = jnp.stack(along_mp(down_piece, n))
        ups = spread(up_line, dp)
        downs = spread(down_line, dp)
        z_done = down_line
        up_scratch = [
            pltpu.VMEM((n, parts, up_rows, enc_up.shape[1]), BF16),
            pltpu.SemaphoreType.DMA((parts * n,)),
        ]
        down_scratch = [
            pltpu.VMEM((n, enc_width // n, ff), BF16),
            pltpu.SemaphoreType.DMA((parts * n,)),
        ]
        spec = [hbm()] * parts
    else:
        ups = [lax.all_gather(enc_up, "mp", axis=0)]
        downs = [lax.all_gather(down_t, "mp", axis=0, tiled=True)]
        z_done = enc_gain
        up_scratch = down_scratch = []
        spec = [vm()]

    wq0, wq1 = by_layer(w_query[0])
    wout0, wout1 = by_layer(w_out[0])
    kv0, kv1 = by_layer(jnp.concatenate([w_key[0], w_value[0]], axis=1))
    gain0, gain1 = by_layer(norm_gain.reshape(n, 1, feats))

    own_rows = lax.dynamic_index_in_dim(segment_input[:, 0], s, 0, keepdims=False)
    own_rows = after(own_rows, z_done)
    row_pieces = along_mp(own_rows, n)

    half_feats = feats // 2

    def query_share(d):
        start = (m ^ d) * feats + s * half_feats
        return lax.dynamic_slice_in_dim(wq1, start, half_feats, 0)

    shares_out = [query_share(d) for d in range(n)]
    shares_out = list(lax.optimization_barrier(tuple(shares_out) + tuple(row_pieces[1:])))[:n]
    mine = jnp.stack(scattered(shares_out))
    others = swap(mine)
    wq1_rows = jnp.where(
        first, jnp.concatenate([mine, others], 1), jnp.concatenate([others, mine], 1)
    )

    grad_messages = call(
        functools.partial(out_grad_body, n),
        [shape((rows, cols))] * n,
        [vm()] * 2,
        flops=2 * rows * width * cols,
    )(out_grad[:, 0], wout1)
    grad_messages = list(lax.optimization_barrier(tuple(grad_messages) + (mine,)))[:n]
    grad_pieces = scattered(grad_messages)

    pool_rows = pool_tokens[:, 0].reshape(half * length, enc_width)
    hidden = call(
        functools.partial(hidden_body, n, parts, not shares),
        [shape((half * length, ff))],
        [vm(), vm()] + spec,
        up_scratch,
        flops=2 * half * length * enc_width * ff,
    )(pool_rows, enc_gain[None, :], *ups)[0]
    enc_own, pool0_own, pool1_own = call(
        functools.partial(encoded_body, n, parts, not shares),
        [
            shape((half, length, enc_width)),
            shape((half, length, 2 * cols)),
            shape((half, length, 2 * cols)),
        ],
        [vm()] * 4 + spec,
        down_scratch,
        flops=4 * half * length * enc_width * ff,
    )(pool_rows, hidden, kv0, kv1, *downs)
    pool0_other = swap(pool0_own)
    pool1_other = swap(after(pool1_own, pool0_other))
    enc_other = swap(after(enc_own, pool0_other))
    pool_scratch = pltpu.VMEM((2 * half, length, 2 * cols), BF16)
    block_scratch = pltpu.VMEM((slots * NT, 2 * cols), BF16)
    pair = pltpu.SemaphoreType.DMA((2,))
    heads = cols // HEAD
    chunk = rows // tracts
    attention_flops = 2 * rows * slots * NT * cols

    att, query0, probs0 = call(
        functools.partial(first_layer_body, n, tracts, slots),
        [
            shape((rows, cols)),
            shape((rows, cols)),
            shape((tracts * heads, chunk, slots * NT), F32),
        ],
        [smem(), smem(), vm(), vm()] + [vm()] * n + [hbm(), hbm()],
        [pool_scratch, block_scratch, pair],
        flops=2 * rows * width * cols + 2 * attention_flops,
    )(ids, counts, gain0, wq0, *row_pieces, pool0_own, pool0_other)
    att_pieces = along_mp(att, n)
    rows1, *messages = call(
        functools.partial(between_body, n),
        [shape((rows, feats))] + [shape((rows + PAD, cols))] * n,
        [vm()] * (4 + n),
        flops=4 * rows * feats * n * cols,
    )(gain1, own_rows, wout0, wq1_rows, *att_pieces)
    query_pieces = scattered(messages)
    slot_rows = tracts * slots * NT
    dkv1, grad_query, scale1 = call(
        functools.partial(last_layer_body, n, width, tracts, slots),
        [shape((slot_rows, 2 * cols)), shape((rows + PAD, cols)), shape((rows, HEAD), F32)],
        [smem(), smem()] + [vm()] * (2 * n) + [hbm(), hbm()],
        [
            pltpu.VMEM((rows, cols), F32),
            pltpu.VMEM((rows, cols), BF16),
            pltpu.VMEM((rows, cols), BF16),
            pool_scratch,
            block_scratch,
            pair,
        ],
        flops=5 * attention_flops,
    )(ids, counts, *query_pieces, *grad_pieces, pool1_own, pool1_other)
    query_grads = along_mp(grad_query, n)
    enc_slots, key1, value1 = call(
        functools.partial(last_grads_body, tracts, slots),
        [shape((enc_width, slot_rows)), shape((enc_width, cols)), shape((enc_width, cols))],
        [smem(), vm(), hbm(), hbm()],
        [pltpu.VMEM((2 * half, length, enc_width), BF16), pair],
        flops=4 * enc_width * slot_rows * cols,
    )(ids, dkv1, enc_own, enc_other)
    messages = call(
        functools.partial(back_between_body, n, width),
        [shape((rows, cols))] * n,
        [vm()] * (6 + n),
        flops=4 * rows * feats * n * cols,
    )(gain1, rows1, out_grad[:, 0], scale1, wq1_rows, wout0, *query_grads)
    grad_pieces0 = scattered(messages)

    def over_cores(key_part, value_part):
        kept = jnp.where(first, key_part, value_part)
        other = swap(jnp.where(first, value_part, key_part))
        return (kept.astype(F32) + other.astype(F32)).astype(BF16)

    sum1 = over_dp(over_cores(key1, value1), dp)
    key0, value0 = call(
        functools.partial(first_back_body, n, tracts, slots),
        [shape((enc_width, cols)), shape((enc_width, cols))],
        [smem(), vm(), vm(), vm()] + [vm()] * n + [hbm(), hbm()],
        [
            pltpu.VMEM((rows, cols), BF16),
            pltpu.VMEM((slot_rows, 2 * cols), BF16),
            pool_scratch,
            block_scratch,
            pair,
        ],
        flops=3 * attention_flops + 4 * enc_width * slot_rows * cols,
    )(ids, query0, probs0, enc_slots, *grad_pieces0, pool0_own, pool0_other)
    sum0 = over_dp(over_cores(key0, value0), dp)
    received = swap(jnp.where(first, sum1, sum0))
    key_total = jnp.where(first, sum0, received)
    value_total = jnp.where(first, received, sum1)
    return (key_total[None], value_total[None])


def solution(mesh):
    placed = (
        P(None, "dp", None, "mp"),
        P(None, "dp", None, "mp"),
        P("section", "dp", None, None),
        P(None, "dp", None, None),
        P(None, "dp", None),
        P(),
        P(None, "mp"),
        P(None, "mp"),
        P("section", None),
        P("section", None, "mp"),
        P("section", None, "mp"),
        P("section", None, "mp"),
        P("section", None, "mp"),
    )
    return jax.shard_map(
        on_device,
        mesh=mesh,
        in_specs=placed,
        out_specs=(P("section", None, "mp"), P("section", None, "mp")),
        check_vma=False,
    )
```

```python
import functools

import jax
import jax.numpy as jnp
from jax import lax
from jax.experimental import pallas as pl
from jax.experimental.pallas import tpu as pltpu
from jax.sharding import PartitionSpec as P

HEAD = 128
NT = 128
EPSILON = 1e-05
SCALE = HEAD ** (-0.5)
PAD = 16
VMEM_LIMIT = 20 * 1024 * 1024
ENCODER_LIMIT = 32 * 1024 * 1024

BF16 = jnp.bfloat16
F32 = jnp.float32
NN = (((1,), (0,)), ((), ()))
NTR = (((1,), (1,)), ((), ()))
TNR = (((0,), (0,)), ((), ()))


def mm(a, b, dims=NN):
    return lax.dot_general(a, b, dims, preferred_element_type=F32)


def xor_move(value, axis, by):
    count = lax.axis_size(axis)
    return lax.ppermute(value, axis, [(i, i ^ by) for i in range(count)])


def swap(value):
    return xor_move(value, "section", 1)


def vm():
    return pl.BlockSpec(memory_space=pltpu.VMEM)


def hbm():
    return pl.BlockSpec(memory_space=pl.ANY)


def hbm_only():
    return pl.BlockSpec(memory_space=pltpu.HBM)


def smem():
    return pl.BlockSpec(memory_space=pltpu.SMEM)


def call(body, outs, specs, scratch=(), flops=0, limit=VMEM_LIMIT, deps=(), passing=()):
    count, more, kept, results = len(specs), len(deps), len(passing), len(outs)
    nbytes = sum(o.size * o.dtype.itemsize for o in outs)
    start = count + more + kept

    def kernel(*refs):
        body(*refs[:count], *refs[start : start + results], *refs[start + results + kept :])

    def run(*args):
        return pl.pallas_call(
            kernel,
            out_shape=list(outs) + [shape(x.shape, x.dtype) for x in passing],
            in_specs=list(specs) + [hbm()] * (more + kept),
            out_specs=[vm() for _ in outs] + [hbm()] * kept,
            scratch_shapes=list(scratch),
            input_output_aliases={count + more + i: results + i for i in range(kept)},
            compiler_params=pltpu.CompilerParams(vmem_limit_bytes=limit),
            cost_estimate=pl.CostEstimate(
                flops=flops // 1000, bytes_accessed=nbytes // 1000, transcendentals=0
            ),
        )(*args, *deps, *passing)

    return run


def shape(dims, dtype=BF16):
    return jax.ShapeDtypeStruct(dims, dtype)


def to_row(column):
    rows = column.shape[0]
    here = lax.broadcasted_iota(jnp.int32, (rows, rows), 0)
    there = lax.broadcasted_iota(jnp.int32, (rows, rows), 1)
    return jnp.sum(jnp.where(here == there, column, 0.0), axis=0, keepdims=True)


def to_column(row):
    rows = row.shape[1]
    here = lax.broadcasted_iota(jnp.int32, (rows, rows), 0)
    there = lax.broadcasted_iota(jnp.int32, (rows, rows), 1)
    return jnp.sum(jnp.where(here == there, row, 0.0), axis=1, keepdims=True)


def load_slots(own, other, ids_ref, tracts, slots, blocks, sems, start=0):
    half = own.shape[0]
    span = pl.ds(start, blocks.shape[1])
    s = lax.axis_index("section")
    waits = []
    for c in range(tracts):
        for k in range(slots):
            i = c * slots + k
            place = ids_ref[s, c, k]
            here = place // half == s
            target, sem = blocks.at[pl.ds(i * NT, NT)], sems.at[i]

            @pl.when(here)
            def _(target=target, sem=sem, place=place):
                pltpu.make_async_copy(own.at[place - s * half, :, span], target, sem).start()

            @pl.when(jnp.logical_not(here))
            def _(target=target, sem=sem, place=place):
                pltpu.make_async_copy(other.at[place - (1 - s) * half, :, span], target, sem).start()

            waits.append(pltpu.make_async_copy(own.at[0, :, span], target, sem))
    return waits


def of_layer(layer, own_ref, other_ref, *index):
    index = index or (Ellipsis,)
    own = lax.axis_index("section") == layer
    return jnp.where(own, own_ref[index], other_ref[index])


def pack(value, cols):
    rows, feats = value.shape
    if feats >= cols:
        return jnp.concatenate([value[:, i : i + cols] for i in range(0, feats, cols)], axis=0)
    share = rows * feats // cols
    return jnp.concatenate([value[i : i + share] for i in range(0, rows, share)], axis=1)


def unpack(value, rows, feats):
    cols = value.shape[1]
    if feats >= cols:
        return jnp.concatenate(
            [value[i : i + rows] for i in range(0, value.shape[0], rows)], axis=1
        )
    return jnp.concatenate([value[:, i : i + feats] for i in range(0, cols, feats)], axis=0)


def share_body(up_ref, down_ref, out_ref, sems):
    place = lax.axis_index("section") * lax.axis_size("dp") + lax.axis_index("dp")
    tall = out_ref.shape[0] // 2
    rows = pl.ds(pl.multiple_of(place * tall, tall), tall)
    cols = pl.ds(pl.multiple_of(place * HEAD, HEAD), HEAD)
    copies = [pltpu.make_async_copy(up_ref.at[rows], out_ref.at[pl.ds(0, tall)], sems.at[0])]
    for side in range(2):
        copies.append(
            pltpu.make_async_copy(
                down_ref.at[pl.ds(side * tall, tall), cols],
                out_ref.at[pl.ds(tall, tall), pl.ds(side * HEAD, HEAD)],
                sems.at[1 + side],
            )
        )
    for copy in copies:
        copy.start()
    for copy in copies:
        copy.wait()


def line_body(n, *refs):
    tall = refs[0].shape[0] // 2
    for d in range(n):
        refs[n][d] = refs[d][:tall, :]
        refs[n + 1][d] = refs[d][tall:, :]


def pair_body(*refs):
    for i in range(2):
        refs[4 + i][0] = refs[2 * i][...]
        refs[4 + i][1] = refs[2 * i + 1][...]


def gather_body(up, up1, up2, down, down2, down1, out_ref):
    for base, parts in ((0, (up, up1, up2)), (4, (down, down2, down1))):
        near = 1 if base == 0 else 2
        out_ref[base] = parts[0][...]
        out_ref[base + near] = parts[1][...]
        out_ref[base + 3 - near] = parts[2][0]
        out_ref[base + 3] = parts[2][1]


def shares_body(n, wq_own, wq_other, rows_ref, own_ref, *outs):
    s, m = lax.axis_index("section"), lax.axis_index("mp")
    own_ref[...] = pack(rows_ref[s], outs[0].shape[1])
    tall = outs[0].shape[0]
    for d in range(n):
        start = ((m ^ d) * 2 + s) * tall
        here = pl.ds(pl.multiple_of(start, tall), tall)
        outs[d][...] = of_layer(1, wq_own, wq_other, here, slice(None))


def projection_body(n, *refs):
    for d in range(n):
        refs[n][d] = refs[d][...]


def add_body(count, *refs):
    for i in range(count):
        total = refs[i][...].astype(F32) + refs[count + i][...].astype(F32)
        refs[2 * count + i][...] = total.astype(BF16)


def halves_body(kept_ref, other_ref, top_ref, bottom_ref):
    half = top_ref.shape[0]
    for i, out_ref in enumerate((top_ref, bottom_ref)):
        here = slice(i * half, (i + 1) * half)
        total = kept_ref[here, :].astype(F32) + other_ref[here, :].astype(F32)
        out_ref[...] = total.astype(BF16)


def norm_body(pool_ref, gain_ref, out_ref):
    wide = pool_ref[...].astype(F32)
    scale = lax.rsqrt(jnp.mean(wide * wide, axis=-1, keepdims=True) + EPSILON)
    out_ref[...] = (wide * scale * gain_ref[...]).astype(BF16)


def encoder_body(n, parts, gathered, *refs):
    pool_ref, normed_ref = refs[:2]
    pieces, (enc_ref, hidden, up, down, *sems) = refs[2:4], refs[4:]
    m = lax.axis_index("mp")
    if gathered:
        copies = [[pltpu.make_async_copy(pieces[i], (up, down)[i], sems[0].at[i])] for i in range(2)]
        downs = copies[1]
        ups = copies[:1] + [[]] * (n - 1)
        ups[0][0].start()
        downs[0].start()
    else:
        up_sems, down_sems = sems
        s, g = lax.axis_index("section"), lax.axis_index("dp")
        dp, tall, wide = parts // 2, pieces[0].shape[2], HEAD
        ups, downs = [[] for _ in range(n)], []
        for dz in range(n):
            for i in range(parts):
                half, dg = divmod(i, dp)
                place = (s ^ half) * dp + (g ^ dg)
                ups[dz].append(
                    pltpu.make_async_copy(
                        pieces[half].at[dg, dz], up.at[m ^ dz, place], up_sems.at[i * n + dz]
                    )
                )
                where = pl.ds(pl.multiple_of(place * wide, wide), wide)
                for side in range(2):
                    downs.append(
                        pltpu.make_async_copy(
                            pieces[half].at[dp + dg, dz, :, pl.ds(side * wide, wide)],
                            down.at[m ^ dz, pl.ds(side * tall, tall), where],
                            down_sems.at[(i * n + dz) * 2 + side],
                        )
                    )
            for copy in ups[dz]:
                copy.start()
        for copy in downs:
            copy.start()
    rows, width = normed_ref.shape
    cols = up.shape[-1]
    chunk = rows // 2
    for dz in range(n):
        for copy in ups[dz]:
            copy.wait()
        k = dz if gathered else m ^ dz
        there = pl.ds(pl.multiple_of(k * cols, cols), cols)
        weight = up[k].reshape(width, cols)
        for r in range(0, rows, chunk):
            product = mm(normed_ref[r : r + chunk, :], weight)
            hidden[r : r + chunk, there] = jax.nn.gelu(product).astype(BF16)
    for copy in downs:
        copy.wait()
    for r in range(0, rows, chunk):
        weight = down[...].reshape(width, hidden.shape[1])
        enc = pool_ref[r : r + chunk, :].astype(F32) + mm(hidden[r : r + chunk, :], weight, NTR)
        enc_ref[r : r + chunk, :] = enc.astype(BF16)


def projected_body(enc_ref, *refs):
    weights, (enc_kv_ref, out0_ref) = refs[:4], refs[4:]
    count, length, _ = enc_kv_ref.shape
    width, cols = weights[0].shape
    enc = enc_ref[...]
    enc_kv_ref[:, :, :width] = enc.reshape(count, length, width)
    for j in range(4):
        layer, kind = divmod(j, 2)
        weight = of_layer(layer, *weights[2 * kind : 2 * kind + 2])
        out = mm(enc, weight).astype(BF16).reshape(count, length, cols)
        if layer == 0:
            out0_ref[:, :, kind * cols : (kind + 1) * cols] = out
        else:
            start = width + kind * cols
            enc_kv_ref[:, :, start : start + cols] = out


def slot_slice(c, slots):
    return slice(c * slots * NT, (c + 1) * slots * NT)


def softmax_used(scores, used):
    lane = lax.broadcasted_iota(jnp.int32, scores.shape, scores.ndim - 1)
    scores = jnp.where(lane < used * NT, scores, -1e30)
    powers = jnp.exp(scores - jnp.max(scores, axis=-1, keepdims=True))
    return powers / jnp.sum(powers, axis=-1, keepdims=True)


def first_layer_body(
    n, tracts, slots, ids_ref, counts_ref, gain_own, gain_other, wq_own, wq_other, *refs
):
    *pieces, own, other, att_ref, query_ref, probs_ref, blocks, sems = refs
    waits = load_slots(own, other, ids_ref, tracts, slots, blocks, sems)
    s, m = lax.axis_index("section"), lax.axis_index("mp")
    rows, cols = att_ref.shape
    feats = gain_own.shape[-1]

    def piece(k):
        if len(pieces) == n or k < 2:
            return unpack(pieces[k][...], rows, feats).astype(F32)
        inner = jnp.logical_or(m == 1, m == 2)
        inside, outside = pieces[2 * k - 2 : 2 * k]
        return unpack(jnp.where(inner, inside[...], outside[...]), rows, feats).astype(F32)

    total = jnp.zeros((rows, 1), F32)
    for k in range(n):
        wide = piece(k)
        total = total + jnp.sum(wide * wide, axis=-1, keepdims=True)
    scale = lax.rsqrt(total / (n * feats) + EPSILON)
    raw = jnp.zeros((rows, cols), F32)
    for k in range(n):
        wide = piece(k)
        gain = of_layer(0, gain_own, gain_other, m ^ k)
        normed = (wide * scale * gain).astype(BF16)
        here = pl.ds(pl.multiple_of((m ^ k) * feats, feats), feats)
        raw = raw + mm(normed, of_layer(0, wq_own, wq_other, here, slice(None)))
    query_ref[...] = (raw * SCALE).astype(BF16)
    length = rows // tracts
    heads = cols // HEAD
    for copy in waits:
        copy.wait()
    for c in range(tracts):
        here, span = slice(c * length, (c + 1) * length), slot_slice(c, slots)
        for h in range(heads):
            there = slice(h * HEAD, (h + 1) * HEAD)
            probs_ref[c * heads + h] = mm(query_ref[here, there], blocks[span, there], NTR)
    for c in range(tracts):
        both = slice(c * heads, (c + 1) * heads)
        probs_ref[both] = softmax_used(probs_ref[both], counts_ref[s, c])
    for c in range(tracts):
        here, span = slice(c * length, (c + 1) * length), slot_slice(c, slots)
        for h in range(heads):
            there = slice(h * HEAD, (h + 1) * HEAD)
            beyond = slice(cols + h * HEAD, cols + (h + 1) * HEAD)
            probs = probs_ref[c * heads + h].astype(BF16)
            att_ref[here, there] = mm(probs, blocks[span, beyond]).astype(BF16)


def between_body(n, *refs):
    gain_own, gain_other, own_ref, wout_own, wout_other, wq_own, wq_other, og_ref = refs[:8]
    pieces = refs[8 : 8 + n]
    rows_ref, messages = refs[8 + n], refs[9 + n :]
    s, m = lax.axis_index("section"), lax.axis_index("mp")
    rows, cols = pieces[0].shape
    tall = wq_own.shape[1]
    feats = rows_ref.shape[1]
    wide = unpack(own_ref[...], rows, feats).astype(F32)
    for d in range(n):
        here = pl.ds(pl.multiple_of((m ^ d) * cols, cols), cols)
        wide = wide + mm(pieces[d][...], of_layer(0, wout_own, wout_other, here, slice(None)))
    rounded = wide.astype(BF16)
    rows_ref[...] = rounded
    wide = rounded.astype(F32)
    square = to_row(jnp.sum(wide * wide, axis=-1, keepdims=True))
    high = square.astype(BF16).astype(F32)
    index = lax.broadcasted_iota(jnp.int32, (PAD, rows), 0)
    extra = jnp.where(index == 0, high, jnp.where(index == 1, square - high, 0.0)).astype(BF16)
    gained = (wide * of_layer(1, gain_own, gain_other, m)).astype(BF16)
    for d in range(n):
        weight = jnp.concatenate([wq_own[d], wq_other[d]], axis=0)
        flipped = jnp.concatenate([wq_other[d], wq_own[d]], axis=0)
        messages[d][:rows, :] = mm(gained, jnp.where(s == 0, weight, flipped)).astype(BF16)
        messages[d][rows : rows + PAD, :] = extra
        here = pl.ds(pl.multiple_of((m ^ d) * cols, cols), cols)
        weight = of_layer(1, wout_own, wout_other, here, slice(None))
        messages[d][rows + PAD :, :] = mm(og_ref[s], weight, NTR).astype(BF16)


def score_grads(tracts, slots, heads, cols, att_ref, blocks, probs_ref, grads_ref, scores_ref, soft_ref):
    length = att_ref.shape[0] // tracts
    for c in range(tracts):
        here, span = slice(c * length, (c + 1) * length), slot_slice(c, slots)
        for h in range(heads):
            there = slice(h * HEAD, (h + 1) * HEAD)
            beyond = slice(cols + h * HEAD, cols + (h + 1) * HEAD)
            grads_ref[c * heads + h] = mm(att_ref[here, there], blocks[span, beyond], NTR)
    for c in range(tracts):
        both = slice(c * heads, (c + 1) * heads)
        probs, grads = probs_ref[both], grads_ref[both]
        inner = jnp.sum(probs * grads, axis=-1, keepdims=True)
        scores_ref[both] = (probs * (grads - inner)).astype(BF16)
        soft_ref[both] = probs.astype(BF16)


def slot_grads(tracts, slots, heads, cols, query_ref, att_ref, scores_ref, soft_ref, dkv_ref):
    length = att_ref.shape[0] // tracts
    for c in range(tracts):
        here, span = slice(c * length, (c + 1) * length), slot_slice(c, slots)
        for h in range(heads):
            there = slice(h * HEAD, (h + 1) * HEAD)
            beyond = slice(cols + h * HEAD, cols + (h + 1) * HEAD)
            dkv_ref[span, there] = mm(
                scores_ref[c * heads + h], query_ref[here, there], TNR
            ).astype(BF16)
            dkv_ref[span, beyond] = mm(
                soft_ref[c * heads + h], att_ref[here, there], TNR
            ).astype(BF16)


def last_layer_body(n, width, tracts, slots, *refs):
    ids_ref, counts_ref = refs[:2]
    messages = refs[2 : 2 + n]
    own, other, dkv_ref, out_ref, scale_ref = refs[2 + n : 7 + n]
    raw_ref, query_ref, att_ref, probs_ref, grads_ref, scores_ref, soft_ref, blocks, sems = refs[
        7 + n :
    ]
    waits = load_slots(own, other, ids_ref, tracts, slots, blocks, sems, own.shape[2] - blocks.shape[1])
    s = lax.axis_index("section")
    rows, cols = raw_ref.shape
    raw = jnp.zeros((rows, cols), F32)
    square = jnp.zeros((1, rows), F32)
    grad = jnp.zeros((rows, cols), F32)
    for d in range(n):
        raw = raw + messages[d][:rows, :].astype(F32)
        extra = messages[d][rows : rows + PAD, :].astype(F32)
        square = square + extra[0:1, :] + extra[1:2, :]
        grad = grad + messages[d][rows + PAD :, :].astype(F32)
    scale = lax.rsqrt(to_column(square) / width + EPSILON)
    scale_ref[...] = jnp.broadcast_to(scale, scale_ref.shape)
    raw = raw * scale
    raw_ref[...] = raw
    query_ref[...] = (raw * SCALE).astype(BF16)
    att_ref[...] = grad.astype(BF16)
    length = rows // tracts
    heads = cols // HEAD
    for copy in waits:
        copy.wait()
    for c in range(tracts):
        here, span = slice(c * length, (c + 1) * length), slot_slice(c, slots)
        for h in range(heads):
            there = slice(h * HEAD, (h + 1) * HEAD)
            probs_ref[c * heads + h] = mm(query_ref[here, there], blocks[span, there], NTR)
    for c in range(tracts):
        both = slice(c * heads, (c + 1) * heads)
        probs_ref[both] = softmax_used(probs_ref[both], counts_ref[s, c])
    score_grads(
        tracts, slots, heads, cols, att_ref, blocks, probs_ref, grads_ref, scores_ref, soft_ref
    )
    for c in range(tracts):
        here, span = slice(c * length, (c + 1) * length), slot_slice(c, slots)
        for h in range(heads):
            there = slice(h * HEAD, (h + 1) * HEAD)
            grad_query = mm(scores_ref[c * heads + h], blocks[span, there]) * SCALE
            out_ref[here, there] = grad_query.astype(BF16)
    part = jnp.sum(out_ref[:rows, :].astype(F32) * raw_ref[...], axis=-1, keepdims=True)
    index = lax.broadcasted_iota(jnp.int32, (PAD, rows), 0)
    out_ref[rows:, :] = jnp.where(index == 0, to_row(part), 0.0).astype(BF16)
    slot_grads(tracts, slots, heads, cols, query_ref, att_ref, scores_ref, soft_ref, dkv_ref)


def weight_grads(enc_ref, dkv_ref, kept_ref, sent_ref):
    cols = kept_ref.shape[1]
    first = lax.axis_index("section") == 0
    chunk = enc_ref.shape[0] // 2
    for r in range(0, enc_ref.shape[0], chunk):
        total = mm(enc_ref[r : r + chunk, :], dkv_ref[...])
        keys, values = total[:, :cols], total[:, cols:]
        kept_ref[r : r + chunk, :] = jnp.where(first, keys, values).astype(BF16)
        sent_ref[r : r + chunk, :] = jnp.where(first, values, keys).astype(BF16)


def last_grads_body(
    tracts, slots, ids_ref, dkv_ref, own, other, enc_ref, kept_ref, sent_ref, rows_ref, sems
):
    waits = load_slots(own, other, ids_ref, tracts, slots, rows_ref, sems)
    for i, copy in enumerate(waits):
        copy.wait()
        here = slice(i * NT, (i + 1) * NT)
        enc_ref[:, here] = rows_ref[here, :].T
    weight_grads(enc_ref, dkv_ref, kept_ref, sent_ref)


def back_between_body(n, width, *refs):
    gain_own, gain_other, rows_ref, og_ref, scale_ref, wq_own, wq_other = refs[:7]
    wout_own, wout_other = refs[7:9]
    pieces, messages = refs[9 : 9 + n], refs[9 + n :]
    s, m = lax.axis_index("section"), lax.axis_index("mp")
    rows, feats = rows_ref.shape
    cols = pieces[0].shape[1]
    normed = jnp.zeros((rows, feats), F32)
    total = jnp.zeros((1, rows), F32)
    for d in range(n):
        weight = jnp.concatenate([wq_own[d], wq_other[d]], axis=0)
        flipped = jnp.concatenate([wq_other[d], wq_own[d]], axis=0)
        normed = normed + mm(pieces[d][:rows, :], jnp.where(s == 0, weight, flipped), NTR)
        total = total + pieces[d][rows:, :].astype(F32)[0:1, :]
    scale = scale_ref[:, 0:1]
    wide = rows_ref[...].astype(F32)
    gain = of_layer(1, gain_own, gain_other, m)
    grad = og_ref[s].astype(F32) + scale * gain * normed
    grad = grad - wide * (scale * scale * (to_column(total) / width))
    grad = grad.astype(BF16)
    for d in range(n):
        here = pl.ds(pl.multiple_of((m ^ d) * cols, cols), cols)
        weight = of_layer(0, wout_own, wout_other, here, slice(None))
        messages[d][...] = mm(grad, weight, NTR).astype(BF16)


def first_back_body(n, tracts, slots, *refs):
    ids_ref, query_ref, probs_ref = refs[:3]
    grads = refs[3 : 3 + n]
    own, other, dkv_ref = refs[3 + n : 6 + n]
    att_ref, grads_ref, scores_ref, soft_ref, blocks, sems = refs[6 + n :]
    waits = load_slots(own, other, ids_ref, tracts, slots, blocks, sems)
    rows, cols = query_ref.shape
    grad = jnp.zeros((rows, cols), F32)
    for d in range(n):
        grad = grad + grads[d][...].astype(F32)
    att_ref[...] = grad.astype(BF16)
    heads = cols // HEAD
    for copy in waits:
        copy.wait()
    score_grads(
        tracts, slots, heads, cols, att_ref, blocks, probs_ref, grads_ref, scores_ref, soft_ref
    )
    slot_grads(tracts, slots, heads, cols, query_ref, att_ref, scores_ref, soft_ref, dkv_ref)


def along_mp(value, n):
    return [value] + [xor_move(value, "mp", d) for d in range(1, n)]


def scattered(messages):
    return [messages[0]] + [xor_move(messages[d], "mp", d) for d in range(1, len(messages))]


def on_device(
    segment_input,
    out_grad,
    pool_tokens,
    neighbour_ids,
    neighbour_counts,
    enc_gain,
    enc_up,
    enc_down,
    norm_gain,
    w_query,
    w_key,
    w_value,
    w_out,
):
    n, dp = lax.axis_size("mp"), lax.axis_size("dp")
    s = lax.axis_index("section")
    _, _, rows, feats = segment_input.shape
    width = n * feats
    cols = w_query.shape[2]
    half, _, length, enc_width = pool_tokens.shape
    tracts, slots = neighbour_ids.shape[2:]
    ids, counts = neighbour_ids[:, 0], neighbour_counts[:, 0]
    ff = enc_down.shape[0]
    first = s == 0
    gain = norm_gain.reshape(n, 1, feats)
    wq, wk, wv, wout = w_query[0], w_key[0], w_value[0], w_out[0]
    gains, wqs, wks, wvs, wouts = ((w, swap(w)) for w in (gain, wq, wk, wv, wout))

    def share_out(deps):
        return call(
            functools.partial(shares_body, n),
            [shape((rows * feats // cols, cols))] + [shape((feats // 2, cols))] * n,
            [vm()] * 3,
            deps=deps,
        )(*wqs, segment_input[:, 0])

    down_t = enc_down.T
    parts = 2 * dp
    up_rows, down_cols = enc_width // parts, ff // parts
    shares = up_rows % 16 == 0 and enc_width // n == 2 * up_rows and down_cols == HEAD
    shares = shares and enc_up.shape[1] == 2 * down_cols and dp == 4
    if shares:
        share = call(
            share_body,
            [shape((2 * up_rows, 2 * down_cols))],
            [hbm_only(), hbm_only()],
            [pltpu.SemaphoreType.DMA((3,))],
        )(enc_up, down_t)[0]
        line = along_mp(share, n)
        line_done = line[1:]
        piece = (n, up_rows, 2 * down_cols)
        up, down = call(
            functools.partial(line_body, n),
            [shape(piece)] * 2,
            [vm()] * n,
            deps=[wqs[1], wouts[1]],
        )(*line)
        own, *query_shares = share_out(line_done)
        inner, outer = [(1, 2), (2, 1)], [(1, 0), (2, 3)]
        up1, down2 = xor_move(up, "dp", 1), xor_move(down, "dp", 2)
        near, far_inner = xor_move(own, "mp", 1), lax.ppermute(own, "mp", inner)
        ups, downs = call(
            pair_body, [shape((2,) + piece)] * 2, [vm()] * 4, deps=[near, far_inner, wks[1]]
        )(up, up1, down, down2)
        up2, down1 = xor_move(ups, "dp", 2), xor_move(downs, "dp", 1)
        next_outer = lax.ppermute(far_inner, "mp", outer)
        next_inner = lax.ppermute(near, "mp", inner)
        gathered = call(
            gather_body,
            [shape((parts,) + piece)],
            [vm()] * 6,
            deps=[next_outer, next_inner, wvs[1]],
        )(up, up1, up2, down, down2, down1)[0]
        pieces = [gathered, swap(gathered)]
        far_outer = lax.ppermute(next_inner, "mp", outer)
        query_shares = scattered(query_shares)
        row_pieces = [own, near, next_inner, next_outer, far_inner, far_outer]
        before_projected = query_shares[1:] + [far_outer]
        scratch = [
            pltpu.VMEM((n, parts, up_rows, enc_up.shape[1]), BF16),
            pltpu.VMEM((n, enc_width // n, ff), BF16),
            pltpu.SemaphoreType.DMA((parts * n,)),
            pltpu.SemaphoreType.DMA((2 * parts * n,)),
        ]
    else:
        own, *query_shares = share_out([])
        row_pieces, query_shares = along_mp(own, n), scattered(query_shares)
        before_projected = []
        pieces = [
            lax.all_gather(enc_up, "mp", axis=0),
            lax.all_gather(down_t, "mp", axis=0, tiled=True),
        ]
        scratch = [
            pltpu.VMEM((n, enc_width, enc_up.shape[1]), BF16),
            pltpu.VMEM((enc_width, ff), BF16),
            pltpu.SemaphoreType.DMA((2,)),
        ]

    pool_rows = pool_tokens[:, 0].reshape(half * length, enc_width)
    normed = call(
        norm_body, [shape((half * length, enc_width))], [vm(), vm()], flops=half * length * enc_width
    )(pool_rows, enc_gain[None, :])[0]
    enc = call(
        functools.partial(encoder_body, n, parts, not shares),
        [shape((half * length, enc_width))],
        [vm()] * 4 if shares else [vm()] * 2 + [hbm()] * 2,
        [pltpu.VMEM((half * length, ff), BF16)] + scratch,
        flops=4 * half * length * enc_width * ff,
        limit=ENCODER_LIMIT if shares else 48 * 1024 * 1024,
    )(pool_rows, normed, *pieces)[0]
    enc_own, pool0_own = call(
        projected_body,
        [shape((half, length, enc_width + 2 * cols)), shape((half, length, 2 * cols))],
        [vm()] * 5,
        flops=8 * half * length * enc_width * cols,
        deps=before_projected,
    )(enc, *wks, *wvs)
    pool0_other = swap(pool0_own)
    projection = call(
        functools.partial(projection_body, n), [shape((n, feats // 2, cols))], [vm()] * n
    )(*query_shares)[0]
    projections = (projection, swap(projection))

    heads = cols // HEAD
    chunk = rows // tracts
    slot_rows = tracts * slots * NT
    blocks_scratch = pltpu.VMEM((slot_rows, 2 * cols), BF16)
    slot_sems = pltpu.SemaphoreType.DMA((tracts * slots,))
    wide_scores = pltpu.VMEM((tracts * heads, chunk, slots * NT), F32)
    bf_scores = pltpu.VMEM((tracts * heads, chunk, slots * NT), BF16)
    attention_flops = 2 * rows * slots * NT * cols

    att, query0, probs0, enc_own = call(
        functools.partial(first_layer_body, n, tracts, slots),
        [
            shape((rows, cols)),
            shape((rows, cols)),
            shape((tracts * heads, chunk, slots * NT), F32),
        ],
        [smem(), smem()] + [vm()] * (6 + len(row_pieces)),
        [blocks_scratch, slot_sems],
        flops=2 * rows * width * cols + 2 * attention_flops,
        passing=[enc_own],
    )(ids, counts, *gains, *wqs, *row_pieces, pool0_own, pool0_other)
    enc_other = swap(enc_own)
    att_pieces = along_mp(att, n)
    rows1, *messages = call(
        functools.partial(between_body, n),
        [shape((rows, feats))] + [shape((2 * rows + PAD, cols))] * n,
        [vm()] * (8 + n),
        flops=6 * rows * feats * n * cols,
        deps=[enc_other],
    )(*gains, own, *wouts, *projections, out_grad[:, 0], *att_pieces)
    query_pieces = scattered(messages)
    dkv1, grad_query, scale1 = call(
        functools.partial(last_layer_body, n, width, tracts, slots),
        [shape((slot_rows, 2 * cols)), shape((rows + PAD, cols)), shape((rows, HEAD), F32)],
        [smem(), smem()] + [vm()] * (n + 2),
        [
            pltpu.VMEM((rows, cols), F32),
            pltpu.VMEM((rows, cols), BF16),
            pltpu.VMEM((rows, cols), BF16),
            wide_scores,
            wide_scores,
            bf_scores,
            bf_scores,
            blocks_scratch,
            slot_sems,
        ],
        flops=5 * attention_flops,
    )(ids, counts, *query_pieces, enc_own, enc_other)
    query_grads = along_mp(grad_query, n)
    enc_slots, kept1, sent1 = call(
        functools.partial(last_grads_body, tracts, slots),
        [shape((enc_width, slot_rows)), shape((enc_width, cols)), shape((enc_width, cols))],
        [smem(), vm(), hbm(), hbm()],
        [pltpu.VMEM((slot_rows, enc_width), BF16), slot_sems],
        flops=4 * enc_width * slot_rows * cols,
    )(ids, dkv1, enc_own, enc_other)
    half_shape = shape((enc_width // 2, cols))
    *messages, kept1, sent1 = call(
        functools.partial(back_between_body, n, width),
        [shape((rows, cols))] * n,
        [vm()] * (9 + n),
        flops=4 * rows * feats * n * cols,
        passing=[kept1, sent1],
    )(*gains, rows1, out_grad[:, 0], scale1, *projections, *wouts, *query_grads)
    grad_pieces0 = scattered(messages)

    def over_dp(parts, order, deps=()):
        moved = [xor_move(part, "dp", by) for part, by in zip(parts, order)]
        return call(functools.partial(add_body, 2), [half_shape] * 2, [vm()] * 4, deps=deps)(
            *parts, *moved
        )

    def summed(kept, sent, deps=()):
        parts = call(halves_body, [half_shape] * 2, [vm()] * 2)(kept, swap(sent))
        if dp == 4:
            parts = over_dp(over_dp(parts, (1, 2), deps), (2, 1))
        else:
            parts = [lax.psum(part, "dp") for part in parts]
        return jnp.concatenate(parts, axis=0)

    sum1 = summed(kept1, sent1, grad_pieces0[1:])
    dkv0 = call(
        functools.partial(first_back_body, n, tracts, slots),
        [shape((slot_rows, 2 * cols))],
        [smem()] + [vm()] * (n + 4),
        [
            pltpu.VMEM((rows, cols), BF16),
            wide_scores,
            bf_scores,
            bf_scores,
            blocks_scratch,
            slot_sems,
        ],
        flops=3 * attention_flops,
    )(ids, query0, probs0, *grad_pieces0, pool0_own, pool0_other)[0]
    kept0, sent0 = call(
        weight_grads,
        [shape((enc_width, cols)), shape((enc_width, cols))],
        [vm()] * 2,
        flops=4 * enc_width * slot_rows * cols,
        deps=[sum1],
    )(enc_slots, dkv0)
    sum0 = summed(kept0, sent0)
    received = swap(jnp.where(first, sum1, sum0))
    key_total = jnp.where(first, sum0, received)
    value_total = jnp.where(first, received, sum1)
    return (key_total[None], value_total[None])


def solution(mesh):
    placed = (
        P(None, "dp", None, "mp"),
        P(None, "dp", None, "mp"),
        P("section", "dp", None, None),
        P(None, "dp", None, None),
        P(None, "dp", None),
        P(),
        P(None, "mp"),
        P(None, "mp"),
        P("section", None),
        P("section", None, "mp"),
        P("section", None, "mp"),
        P("section", None, "mp"),
        P("section", None, "mp"),
    )
    return jax.shard_map(
        on_device,
        mesh=mesh,
        in_specs=placed,
        out_specs=(P("section", None, "mp"), P("section", None, "mp")),
        check_vma=False,
    )
```

```python
import functools

import jax
import jax.numpy as jnp
from jax import lax
from jax.experimental import pallas as pl
from jax.experimental.pallas import tpu as pltpu
from jax.sharding import PartitionSpec as P

HEAD = 128
NT = 128
EPSILON = 1e-05
SCALE = HEAD ** (-0.5)
PAD = 16
VMEM_LIMIT = 20 * 1024 * 1024
ENCODER_LIMIT = 32 * 1024 * 1024
FIRST_LIMIT = 60 * 1024 * 1024

BF16 = jnp.bfloat16
F32 = jnp.float32
NN = (((1,), (0,)), ((), ()))
NTR = (((1,), (1,)), ((), ()))
TNR = (((0,), (0,)), ((), ()))


def mm(a, b, dims=NN):
    return lax.dot_general(a, b, dims, preferred_element_type=F32)


def xor_move(value, axis, by):
    count = lax.axis_size(axis)
    return lax.ppermute(value, axis, [(i, i ^ by) for i in range(count)])


def places(n):
    return (0, 2, 3, 1) if n == 4 else tuple(range(n))


def swap(value):
    return xor_move(value, "section", 1)


def vm():
    return pl.BlockSpec(memory_space=pltpu.VMEM)


def hbm():
    return pl.BlockSpec(memory_space=pl.ANY)


def hbm_only():
    return pl.BlockSpec(memory_space=pltpu.HBM)


def smem():
    return pl.BlockSpec(memory_space=pltpu.SMEM)


def call(body, outs, specs, scratch=(), flops=0, limit=VMEM_LIMIT, first=(), deps=(), passing=()):
    count, more, kept, results = len(specs), len(deps), len(passing), len(outs)
    nbytes = sum(o.size * o.dtype.itemsize for o in outs)
    begin = len(first)
    start = begin + count + more + kept

    def kernel(*refs):
        given = refs[begin : begin + count]
        body(*given, *refs[start : start + results], *refs[start + results + kept :])

    def run(*args):
        return pl.pallas_call(
            kernel,
            out_shape=list(outs) + [shape(x.shape, x.dtype) for x in passing],
            in_specs=[hbm()] * begin + list(specs) + [hbm()] * (more + kept),
            out_specs=[vm() for _ in outs] + [hbm()] * kept,
            scratch_shapes=list(scratch),
            input_output_aliases={begin + count + more + i: results + i for i in range(kept)},
            compiler_params=pltpu.CompilerParams(vmem_limit_bytes=limit),
            cost_estimate=pl.CostEstimate(
                flops=flops // 1000, bytes_accessed=nbytes // 1000, transcendentals=0
            ),
        )(*first, *args, *deps, *passing)

    return run


def shape(dims, dtype=BF16):
    return jax.ShapeDtypeStruct(dims, dtype)


def to_row(column):
    rows = column.shape[0]
    here = lax.broadcasted_iota(jnp.int32, (rows, rows), 0)
    there = lax.broadcasted_iota(jnp.int32, (rows, rows), 1)
    return jnp.sum(jnp.where(here == there, column, 0.0), axis=0, keepdims=True)


def to_column(row):
    rows = row.shape[1]
    here = lax.broadcasted_iota(jnp.int32, (rows, rows), 0)
    there = lax.broadcasted_iota(jnp.int32, (rows, rows), 1)
    return jnp.sum(jnp.where(here == there, row, 0.0), axis=1, keepdims=True)


def slot_value(own, other, ids_ref, tract, slot, start, size):
    half = own.shape[0]
    s = lax.axis_index("section")
    place = ids_ref[s, tract, slot]
    mine, theirs = place - s * half, place - (1 - s) * half
    here = jnp.logical_and(mine >= 0, mine < half)
    cols = slice(start, start + size)
    return jnp.where(
        here,
        own[jnp.clip(mine, 0, half - 1), :, cols],
        other[jnp.clip(theirs, 0, half - 1), :, cols],
    )


def fill_slots(own, other, ids_ref, tracts, slots, blocks, start=0):
    for c in range(tracts):
        for k in range(slots):
            here = slice((c * slots + k) * NT, (c * slots + k + 1) * NT)
            blocks[here, :] = slot_value(own, other, ids_ref, c, k, start, blocks.shape[1])


def of_layer(layer, own_ref, other_ref, *index):
    index = index or (Ellipsis,)
    own = lax.axis_index("section") == layer
    return jnp.where(own, own_ref[index], other_ref[index])


def pack(value, cols):
    rows, feats = value.shape
    if feats >= cols:
        return jnp.concatenate([value[:, i : i + cols] for i in range(0, feats, cols)], axis=0)
    share = rows * feats // cols
    return jnp.concatenate([value[i : i + share] for i in range(0, rows, share)], axis=1)


def unpack(value, rows, feats):
    cols = value.shape[1]
    if feats >= cols:
        return jnp.concatenate(
            [value[i : i + rows] for i in range(0, value.shape[0], rows)], axis=1
        )
    return jnp.concatenate([value[:, i : i + feats] for i in range(0, cols, feats)], axis=0)


def share_body(n, up_ref, down_ref, wq_own, wq_other, rows_ref, *refs):
    outs, own_ref, sems = refs[:n], refs[n], refs[n + 1]
    s, m = lax.axis_index("section"), lax.axis_index("mp")
    place = s * lax.axis_size("dp") + lax.axis_index("dp")
    parts = 2 * lax.axis_size("dp")
    tall = up_ref.shape[0] // parts
    share = wq_own.shape[0] // (n * parts)
    rows = pl.ds(pl.multiple_of(place * tall, 16), tall)
    cols = pl.ds(pl.multiple_of(place * HEAD, HEAD), HEAD)
    copies = [pltpu.make_async_copy(up_ref.at[rows], outs[0].at[pl.ds(0, tall)], sems.at[0])]
    for side in range(2):
        copies.append(
            pltpu.make_async_copy(
                down_ref.at[pl.ds(side * tall, tall), cols],
                outs[0].at[pl.ds(tall, tall), pl.ds(side * HEAD, HEAD)],
                sems.at[1 + side],
            )
        )
    for copy in copies:
        copy.start()
    for i, d in enumerate(places(n)):
        start = ((m ^ d) * parts + place) * share
        here = pl.ds(pl.multiple_of(start, share), share)
        target = outs[i].at[pl.ds(2 * tall, share)]
        copies.append(pltpu.make_async_copy(wq_own.at[here], target, sems.at[3 + i]))

        @pl.when(s == 1)
        def _(here=here, target=target, i=i):
            pltpu.make_async_copy(wq_own.at[here], target, sems.at[3 + i]).start()

        @pl.when(s != 1)
        def _(here=here, target=target, i=i):
            pltpu.make_async_copy(wq_other.at[here], target, sems.at[3 + i]).start()

    total, length = rows_ref.shape[1], own_ref.shape[1]
    for i in range(own_ref.shape[0] // total):
        source = rows_ref.at[s, :, pl.ds(i * length, length)]
        target = own_ref.at[pl.ds(i * total, total)]
        copies.append(pltpu.make_async_copy(source, target, sems.at[3 + n + i]))
        copies[-1].start()
    for copy in copies:
        copy.wait()
    half = own_ref.shape[0] // 2
    outs[n - 1][2 * tall + share :, :] = own_ref[:half, :]
    for i in range(1, n):
        outs[i][: 2 * tall, :] = outs[0][: 2 * tall, :]


def line_body(n, tall, *refs):
    half = (refs[0].shape[0] - 2 * tall) // 2
    own_ref, far_ref = refs[n], refs[n + 1]
    near_ref, message, kept_ref = refs[n + 4 :]
    kept_ref[...] = own_ref[...]
    near_ref[...] = refs[n - 1][2 * (tall + half) :, :]
    rest = own_ref.shape[0] // 2
    message[:rest, :] = own_ref[rest:, :]
    message[rest:, :] = far_ref[...]
    for i in range(1, n):
        for j in range(2):
            start = 2 * tall + j * half
            refs[n + 2 + j][i - 1, :tall] = refs[i][j * tall : (j + 1) * tall, :]
            refs[n + 2 + j][i - 1, tall:] = refs[i][start : start + half, :]


def pair_body(up, up1, down, down2, near1, moved, far2, far3, ups, downs, message, near):
    for here, there, out_ref in ((up, up1, ups), (down, down2, downs)):
        out_ref[0] = here[...]
        out_ref[1] = there[...]
    first, rest, rows = near.shape[0], near1.shape[0], far2.shape[0]
    near[:rest, :] = near1[...]
    near[rest:, :] = moved[:rest, :]
    message[:first, :] = near[...]
    for i, far in enumerate((far3, far2)):
        start = rest + i * rows
        total = moved[start : start + rows, :].astype(F32) + far[...].astype(F32)
        message[first + i * rows : first + (i + 1) * rows, :] = total.astype(BF16)


def gather_body(
    up, up1, up2, down, down2, down1, moved, close, key_ref, value_ref,
    out_ref, next_ref, grad_ref, key_out, value_out,
):
    key_out[...] = key_ref[...]
    value_out[...] = value_ref[...]
    for base, parts in ((0, (up, up1, up2)), (4, (down, down2, down1))):
        near = 1 if base == 0 else 2
        out_ref[base] = parts[0][...]
        out_ref[base + near] = parts[1][...]
        out_ref[base + 3 - near] = parts[2][0]
        out_ref[base + 3] = parts[2][1]
    first, rows = next_ref.shape[0], grad_ref.shape[0]
    next_ref[...] = moved[:first, :]
    total = moved[first + rows :, :].astype(F32) + close[...].astype(F32)
    grad_ref[...] = total.astype(BF16)


def rows_body(cols, rows_ref, own_ref):
    own_ref[...] = pack(rows_ref[lax.axis_index("section")], cols)


def query_shares_body(n, wq_own, wq_other, *outs):
    m = lax.axis_index("mp")
    tall = outs[0].shape[0]
    for i, d in enumerate(places(n)):
        here = pl.ds(pl.multiple_of((m ^ d) * tall, tall), tall)
        outs[i][...] = of_layer(1, wq_own, wq_other, here, slice(None))


def out_grads_body(n, og_ref, wout_own, wout_other, *outs):
    s, m = lax.axis_index("section"), lax.axis_index("mp")
    cols = outs[0].shape[1]
    rows = og_ref.shape[1]
    for i, d in enumerate(places(n)):
        here = pl.ds(pl.multiple_of((m ^ d) * cols, cols), cols)
        weight = of_layer(1, wout_own, wout_other, here, slice(None))
        outs[i][...] = mm(og_ref[s], weight, NTR).astype(BF16)
    for i, out_ref in enumerate(outs[1:3]):
        if len(outs) > n:
            outs[n][i * rows : (i + 1) * rows, :] = out_ref[...]


def add_body(count, *refs):
    for i in range(count):
        total = refs[i][...].astype(F32) + refs[count + i][...].astype(F32)
        refs[2 * count + i][...] = total.astype(BF16)


def halves_body(kept_ref, other_ref, top_ref, bottom_ref):
    half = top_ref.shape[0]
    for i, out_ref in enumerate((top_ref, bottom_ref)):
        here = slice(i * half, (i + 1) * half)
        total = kept_ref[here, :].astype(F32) + other_ref[here, :].astype(F32)
        out_ref[...] = total.astype(BF16)


def norm_body(pool_ref, gain_ref, out_ref):
    wide = pool_ref[...].astype(F32)
    scale = lax.rsqrt(jnp.mean(wide * wide, axis=-1, keepdims=True) + EPSILON)
    out_ref[...] = (wide * scale * gain_ref[...]).astype(BF16)


def encoder_body(n, parts, gathered, *refs):
    pool_ref, normed_ref = refs[:2]
    if gathered:
        pieces, (enc_ref, hidden, up, down, *sems) = refs[2:4], refs[4:]
    else:
        pieces, (enc_ref, wq_ref, hidden, up, down) = refs[2:4], refs[8:]
        up_ref, down_ref, wq_own, wq_other = refs[4:8]
    m = lax.axis_index("mp")
    if gathered:
        copies = [[pltpu.make_async_copy(pieces[i], (up, down)[i], sems[0].at[i])] for i in range(2)]
        downs = copies[1]
        ups = copies[:1] + [[]] * (n - 1)
        ups[0][0].start()
        downs[0].start()
    else:
        s, g = lax.axis_index("section"), lax.axis_index("dp")
        dp, tall, wide = parts // 2, up.shape[2], HEAD
        share = pieces[0].shape[2] - tall
        ups, downs = [[] for _ in range(n)], []
        up[m] = up_ref[...].reshape(up.shape[1:])
        down[m] = down_ref[...]
        here = pl.ds(pl.multiple_of(m * wq_ref.shape[1], wq_ref.shape[1]), wq_ref.shape[1])
        wq_ref[0] = of_layer(1, wq_own, wq_other, here, slice(None))
        for j, dz in enumerate(places(n)[1:]):
            for i in range(parts):
                half, dg = divmod(i, dp)
                place = (s ^ half) * dp + (g ^ dg)
                for k in range(2):
                    start = pl.multiple_of((2 * place + k) * share, share)
                    wq_ref[j + 1, pl.ds(start, share)] = pieces[half][k * dp + dg, j, tall:]
                up[m ^ dz, place] = pieces[half][dg, j, :tall]
                where = pl.ds(pl.multiple_of(place * wide, wide), wide)
                for side in range(2):
                    rows_of = slice(side * tall, (side + 1) * tall)
                    down[m ^ dz, rows_of, where] = pieces[half][
                        dp + dg, j, :tall, side * wide : (side + 1) * wide
                    ]
    rows, width = normed_ref.shape
    cols = up.shape[-1]
    chunk = rows // 2
    for dz in range(n):
        for copy in ups[dz]:
            copy.wait()
        k = dz if gathered else m ^ dz
        there = pl.ds(pl.multiple_of(k * cols, cols), cols)
        weight = up[k].reshape(width, cols)
        for r in range(0, rows, chunk):
            product = mm(normed_ref[r : r + chunk, :], weight)
            hidden[r : r + chunk, there] = jax.nn.gelu(product).astype(BF16)
    for copy in downs:
        copy.wait()
    for r in range(0, rows, chunk):
        weight = down[...].reshape(width, hidden.shape[1])
        enc = pool_ref[r : r + chunk, :].astype(F32) + mm(hidden[r : r + chunk, :], weight, NTR)
        enc_ref[r : r + chunk, :] = enc.astype(BF16)


def projected_body(enc_ref, *refs):
    weights, (enc_kv_ref, out0_ref) = refs[:4], refs[4:]
    count, length, _ = enc_kv_ref.shape
    width, cols = weights[0].shape
    enc = enc_ref[...]
    enc_kv_ref[:, :, :width] = enc.reshape(count, length, width)
    for j in range(4):
        layer, kind = divmod(j, 2)
        weight = of_layer(layer, *weights[2 * kind : 2 * kind + 2])
        out = mm(enc, weight).astype(BF16).reshape(count, length, cols)
        if layer == 0:
            out0_ref[:, :, kind * cols : (kind + 1) * cols] = out
        else:
            start = width + kind * cols
            enc_kv_ref[:, :, start : start + cols] = out


def slot_slice(c, slots):
    return slice(c * slots * NT, (c + 1) * slots * NT)


def softmax_used(scores, used):
    lane = lax.broadcasted_iota(jnp.int32, scores.shape, scores.ndim - 1)
    scores = jnp.where(lane < used * NT, scores, -1e30)
    powers = jnp.exp(scores - jnp.max(scores, axis=-1, keepdims=True))
    return powers / jnp.sum(powers, axis=-1, keepdims=True)


def first_layer_body(
    n, tracts, slots, ids_ref, counts_ref, gain_own, gain_other, wq_own, wq_other, *refs
):
    *pieces, own, other, att_ref, query_ref, probs_ref, blocks = refs
    fill_slots(own, other, ids_ref, tracts, slots, blocks)
    s, m = lax.axis_index("section"), lax.axis_index("mp")
    rows, cols = query_ref.shape
    feats = gain_own.shape[-1]

    def piece(k):
        if len(pieces) == n or k < 2:
            return unpack(pieces[k][...], rows, feats).astype(F32)
        inner = jnp.logical_or(m == 1, m == 2)
        inside, outside = pieces[2 * k - 2 : 2 * k]
        return unpack(jnp.where(inner, inside[...], outside[...]), rows, feats).astype(F32)

    total = jnp.zeros((rows, 1), F32)
    for k in range(n):
        wide = piece(k)
        total = total + jnp.sum(wide * wide, axis=-1, keepdims=True)
    scale = lax.rsqrt(total / (n * feats) + EPSILON)
    raw = jnp.zeros((rows, cols), F32)
    for k in range(n):
        wide = piece(k)
        gain = of_layer(0, gain_own, gain_other, m ^ k)
        normed = (wide * scale * gain).astype(BF16)
        here = pl.ds(pl.multiple_of((m ^ k) * feats, feats), feats)
        raw = raw + mm(normed, of_layer(0, wq_own, wq_other, here, slice(None)))
    query_ref[...] = (raw * SCALE).astype(BF16)
    length = rows // tracts
    heads = cols // HEAD
    for c in range(tracts):
        here, span = slice(c * length, (c + 1) * length), slot_slice(c, slots)
        for h in range(heads):
            there = slice(h * HEAD, (h + 1) * HEAD)
            probs_ref[c * heads + h] = mm(query_ref[here, there], blocks[span, there], NTR)
    for c in range(tracts):
        both = slice(c * heads, (c + 1) * heads)
        probs_ref[both] = softmax_used(probs_ref[both], counts_ref[s, c])
    for c in range(tracts):
        here, span = slice(c * length, (c + 1) * length), slot_slice(c, slots)
        for h in range(heads):
            there = slice(h * HEAD, (h + 1) * HEAD)
            beyond = slice(cols + h * HEAD, cols + (h + 1) * HEAD)
            probs = probs_ref[c * heads + h].astype(BF16)
            att_ref[here, there] = mm(probs, blocks[span, beyond]).astype(BF16)


def between_body(n, *refs):
    gain_own, gain_other, own_ref, wout_own, wout_other, wq_ref = refs[:6]
    pieces = refs[6 : 6 + n]
    rows_ref, messages = refs[6 + n], refs[7 + n :]
    m = lax.axis_index("mp")
    rows, cols = pieces[0].shape
    feats = rows_ref.shape[1]
    wide = unpack(own_ref[...], rows, feats).astype(F32)
    for i, d in enumerate(places(n)):
        here = pl.ds(pl.multiple_of((m ^ d) * cols, cols), cols)
        wide = wide + mm(pieces[i][...], of_layer(0, wout_own, wout_other, here, slice(None)))
    rounded = wide.astype(BF16)
    rows_ref[...] = rounded
    wide = rounded.astype(F32)
    square = to_row(jnp.sum(wide * wide, axis=-1, keepdims=True))
    high = square.astype(BF16).astype(F32)
    index = lax.broadcasted_iota(jnp.int32, (PAD, rows), 0)
    extra = jnp.where(index == 0, high, jnp.where(index == 1, square - high, 0.0)).astype(BF16)
    gained = (wide * of_layer(1, gain_own, gain_other, m)).astype(BF16)
    for i in range(n):
        messages[i][:rows, :] = mm(gained, wq_ref[i]).astype(BF16)
        messages[i][rows:, :] = extra


def score_grads(tracts, slots, heads, start, att_ref, blocks, probs_ref, grads_ref, scores_ref, soft_ref):
    length = att_ref.shape[0] // tracts
    for c in range(tracts):
        here, span = slice(c * length, (c + 1) * length), slot_slice(c, slots)
        for h in range(heads):
            there = slice(h * HEAD, (h + 1) * HEAD)
            beyond = slice(start + h * HEAD, start + (h + 1) * HEAD)
            grads_ref[c * heads + h] = mm(att_ref[here, there], blocks[span, beyond], NTR)
    for c in range(tracts):
        both = slice(c * heads, (c + 1) * heads)
        probs, grads = probs_ref[both], grads_ref[both]
        inner = jnp.sum(probs * grads, axis=-1, keepdims=True)
        scores_ref[both] = (probs * (grads - inner)).astype(BF16)
        soft_ref[both] = probs.astype(BF16)


def slot_grads(tracts, slots, heads, cols, query_ref, att_ref, scores_ref, soft_ref, dkv_ref):
    length = att_ref.shape[0] // tracts
    for c in range(tracts):
        here, span = slice(c * length, (c + 1) * length), slot_slice(c, slots)
        for h in range(heads):
            there = slice(h * HEAD, (h + 1) * HEAD)
            beyond = slice(cols + h * HEAD, cols + (h + 1) * HEAD)
            dkv_ref[span, there] = mm(
                scores_ref[c * heads + h], query_ref[here, there], TNR
            ).astype(BF16)
            dkv_ref[span, beyond] = mm(
                soft_ref[c * heads + h], att_ref[here, there], TNR
            ).astype(BF16)


def last_layer_body(n, width, tracts, slots, *refs):
    ids_ref, counts_ref = refs[:2]
    messages, grads = refs[2 : 2 + n], refs[2 + n : -13]
    own, other, dkv_ref, out_ref, scale_ref = refs[-13:-8]
    raw_ref, query_ref, att_ref, probs_ref, grads_ref, scores_ref, soft_ref, blocks = refs[-8:]
    fill_slots(own, other, ids_ref, tracts, slots, blocks, own.shape[2] - blocks.shape[1])
    s = lax.axis_index("section")
    rows, cols = raw_ref.shape
    raw = jnp.zeros((rows, cols), F32)
    square = jnp.zeros((1, rows), F32)
    grad = jnp.zeros((rows, cols), F32)
    for d in range(n):
        raw = raw + messages[d][:rows, :].astype(F32)
        extra = messages[d][rows:, :].astype(F32)
        square = square + extra[0:1, :] + extra[1:2, :]
    for part in grads:
        start = max(part.shape[0] - 2 * rows, 0)
        grad = grad + part[start : start + rows, :].astype(F32)
    scale = lax.rsqrt(to_column(square) / width + EPSILON)
    scale_ref[...] = jnp.broadcast_to(scale, scale_ref.shape)
    raw = raw * scale
    raw_ref[...] = raw
    query_ref[...] = (raw * SCALE).astype(BF16)
    att_ref[...] = grad.astype(BF16)
    length = rows // tracts
    heads = cols // HEAD
    for c in range(tracts):
        here, span = slice(c * length, (c + 1) * length), slot_slice(c, slots)
        for h in range(heads):
            there = slice(h * HEAD, (h + 1) * HEAD)
            probs_ref[c * heads + h] = mm(query_ref[here, there], blocks[span, there], NTR)
    for c in range(tracts):
        both = slice(c * heads, (c + 1) * heads)
        probs_ref[both] = softmax_used(probs_ref[both], counts_ref[s, c])
    score_grads(
        tracts, slots, heads, cols, att_ref, blocks, probs_ref, grads_ref, scores_ref, soft_ref
    )
    for c in range(tracts):
        here, span = slice(c * length, (c + 1) * length), slot_slice(c, slots)
        for h in range(heads):
            there = slice(h * HEAD, (h + 1) * HEAD)
            grad_query = mm(scores_ref[c * heads + h], blocks[span, there]) * SCALE
            out_ref[here, there] = grad_query.astype(BF16)
    part = jnp.sum(out_ref[:rows, :].astype(F32) * raw_ref[...], axis=-1, keepdims=True)
    index = lax.broadcasted_iota(jnp.int32, (PAD, rows), 0)
    out_ref[rows:, :] = jnp.where(index == 0, to_row(part), 0.0).astype(BF16)
    slot_grads(tracts, slots, heads, cols, query_ref, att_ref, scores_ref, soft_ref, dkv_ref)


def weight_grads(enc_ref, dkv_ref, kept_ref, sent_ref):
    cols = kept_ref.shape[1]
    first = lax.axis_index("section") == 0
    chunk = enc_ref.shape[0] // 2
    for r in range(0, enc_ref.shape[0], chunk):
        total = mm(enc_ref[r : r + chunk, :], dkv_ref[...])
        keys, values = total[:, :cols], total[:, cols:]
        kept_ref[r : r + chunk, :] = jnp.where(first, keys, values).astype(BF16)
        sent_ref[r : r + chunk, :] = jnp.where(first, values, keys).astype(BF16)


def part_grads_body(keep, enc_ref, dkv_ref, out_ref):
    cols = out_ref.shape[1]
    kind = lax.axis_index("section") if keep else 1 - lax.axis_index("section")
    here = pl.ds(pl.multiple_of(kind * cols, cols), cols)
    out_ref[...] = mm(enc_ref[...], dkv_ref[:, here]).astype(BF16)


def last_grads_body(
    tracts, slots, ids_ref, dkv_ref, own, other, enc_ref, kept_ref, sent_ref
):
    for c in range(tracts):
        for k in range(slots):
            here = slice((c * slots + k) * NT, (c * slots + k + 1) * NT)
            enc_ref[:, here] = slot_value(own, other, ids_ref, c, k, 0, enc_ref.shape[0]).T
    weight_grads(enc_ref, dkv_ref, kept_ref, sent_ref)


def back_between_body(n, width, *refs):
    gain_own, gain_other, rows_ref, og_ref, scale_ref, wq_ref = refs[:6]
    wout_own, wout_other = refs[6:8]
    pieces, messages = refs[8 : 8 + n], refs[8 + n :]
    s, m = lax.axis_index("section"), lax.axis_index("mp")
    rows, feats = rows_ref.shape
    cols = pieces[0].shape[1]
    normed = jnp.zeros((rows, feats), F32)
    total = jnp.zeros((1, rows), F32)
    for d in range(n):
        normed = normed + mm(pieces[d][:rows, :], wq_ref[d], NTR)
        total = total + pieces[d][rows:, :].astype(F32)[0:1, :]
    scale = scale_ref[:, 0:1]
    wide = rows_ref[...].astype(F32)
    gain = of_layer(1, gain_own, gain_other, m)
    grad = og_ref[s].astype(F32) + scale * gain * normed
    grad = grad - wide * (scale * scale * (to_column(total) / width))
    grad = grad.astype(BF16)
    for i, d in enumerate(places(n)):
        here = pl.ds(pl.multiple_of((m ^ d) * cols, cols), cols)
        weight = of_layer(0, wout_own, wout_other, here, slice(None))
        messages[i][...] = mm(grad, weight, NTR).astype(BF16)


def first_back_body(n, tracts, slots, *refs):
    ids_ref, query_ref, probs_ref = refs[:3]
    grads = refs[3 : 3 + n]
    own, other, dkv_ref = refs[3 + n : 6 + n]
    att_ref, grads_ref, scores_ref, soft_ref, blocks = refs[6 + n :]
    fill_slots(own, other, ids_ref, tracts, slots, blocks, query_ref.shape[1])
    rows, cols = query_ref.shape
    grad = jnp.zeros((rows, cols), F32)
    for d in range(n):
        grad = grad + grads[d][...].astype(F32)
    att_ref[...] = grad.astype(BF16)
    heads = cols // HEAD
    score_grads(
        tracts, slots, heads, 0, att_ref, blocks, probs_ref, grads_ref, scores_ref, soft_ref
    )
    slot_grads(tracts, slots, heads, cols, query_ref, att_ref, scores_ref, soft_ref, dkv_ref)


def along_mp(value, n):
    return [value] + [xor_move(value, "mp", d) for d in places(n)[1:]]


def scattered(messages):
    order = places(len(messages))
    return [messages[0]] + [xor_move(messages[i], "mp", order[i]) for i in range(1, len(messages))]


def on_device(
    segment_input,
    out_grad,
    pool_tokens,
    neighbour_ids,
    neighbour_counts,
    enc_gain,
    enc_up,
    enc_down,
    norm_gain,
    w_query,
    w_key,
    w_value,
    w_out,
):
    n, dp = lax.axis_size("mp"), lax.axis_size("dp")
    s = lax.axis_index("section")
    _, _, rows, feats = segment_input.shape
    width = n * feats
    cols = w_query.shape[2]
    half, _, length, enc_width = pool_tokens.shape
    tracts, slots = neighbour_ids.shape[2:]
    ids, counts = neighbour_ids[:, 0], neighbour_counts[:, 0]
    ff = enc_down.shape[0]
    first = s == 0
    gain = norm_gain.reshape(n, 1, feats)
    wq, wk, wv, wout = w_query[0], w_key[0], w_value[0], w_out[0]
    gains, wqs, wouts = ((w, swap(w)) for w in (gain, wq, wout))

    down_t = enc_down.T
    parts = 2 * dp
    up_rows, down_cols = enc_width // parts, ff // parts
    shares = up_rows % 16 == 0 and enc_width // n == 2 * up_rows and down_cols == HEAD
    shares = shares and enc_up.shape[1] == 2 * down_cols and dp == 4 and n == 4
    shares = shares and feats % (32 * parts) == 0 and cols == enc_up.shape[1]
    if shares:
        own_shape = shape((rows * feats // cols, cols))
        messages = [shape((2 * up_rows + feats // parts, 2 * down_cols))] * (n - 1)
        rest = own_shape.shape[0] // 2
        longer = shape((messages[0].shape[0] + rest, cols))
        *messages, own = call(
            functools.partial(share_body, n),
            messages + [longer, own_shape],
            [hbm()] * 5,
            [pltpu.SemaphoreType.DMA((3 + n + feats // cols,))],
            limit=FIRST_LIMIT,
        )(enc_up, down_t, *wqs, segment_input[:, 0])
        line = scattered(messages)
        *grads, far_grads = call(
            functools.partial(out_grads_body, n),
            [shape((rows, cols))] * n + [shape((2 * rows, cols))],
            [vm()] * 3,
            flops=2 * rows * width * cols,
        )(out_grad[:, 0], *wouts)
        piece = (n - 1, up_rows + feats // (2 * parts), 2 * down_cols)
        up, down, near, message, own = call(
            functools.partial(line_body, n, up_rows),
            [shape(piece)] * 2
            + [shape((rest, cols)), shape((rest + 2 * rows, cols)), own_shape],
            [vm()] * (n + 2),
        )(*line, own, far_grads)
        inner, outer = [(1, 2), (2, 1)], [(1, 0), (2, 3)]
        up1, down2 = xor_move(up, "dp", 1), xor_move(down, "dp", 2)
        far_inner = lax.ppermute(own, "mp", inner)
        message = xor_move(message, "mp", 1)
        ups, downs, message, near = call(
            pair_body,
            [shape((2,) + piece)] * 2 + [shape((own_shape.shape[0] + 2 * rows, cols)), own_shape],
            [vm()] * 8,
            deps=[far_inner],
        )(up, up1, down, down2, near, message, grads[1], grads[2])
        up2, down1 = xor_move(ups, "dp", 2), xor_move(downs, "dp", 1)
        next_outer = lax.ppermute(far_inner, "mp", outer)
        message = lax.ppermute(message, "mp", inner)
        gathered, next_inner, close, wk, wv = call(
            gather_body,
            [shape((parts,) + piece), own_shape, shape((rows, cols))]
            + [shape((enc_width, cols))] * 2,
            [vm()] * 10,
            deps=[next_outer],
        )(up, up1, up2, down, down2, down1, message, grads[3], wk, wv)
        pieces = [gathered, swap(gathered), enc_up, down_t, *wqs]
        far_outer = lax.ppermute(next_inner, "mp", outer)
        close = xor_move(close, "mp", 1)
        grad_parts = [grads[0], message, close]
        row_pieces = [own, near, next_inner, next_outer, far_inner, far_outer]
        before_projected = [far_outer, close]
        scratch = [
            pltpu.VMEM((n, parts, up_rows, enc_up.shape[1]), BF16),
            pltpu.VMEM((n, enc_width // n, ff), BF16),
        ]
    else:
        own = call(
            functools.partial(rows_body, cols), [shape((rows * feats // cols, cols))], [vm()]
        )(segment_input[:, 0])[0]
        grad_parts = call(
            functools.partial(out_grads_body, n),
            [shape((rows, cols))] * n,
            [vm()] * 3,
            flops=2 * rows * width * cols,
        )(out_grad[:, 0], *wouts)
        row_pieces, grad_parts = along_mp(own, n), scattered(grad_parts)
        query_shares = call(
            functools.partial(query_shares_body, n), [shape((feats, cols))] * n, [vm()] * 2
        )(*wqs)
        projection = jnp.stack(scattered(query_shares))
        before_projected = []
        pieces = [
            lax.all_gather(enc_up, "mp", axis=0),
            lax.all_gather(down_t, "mp", axis=0, tiled=True),
        ]
        scratch = [
            pltpu.VMEM((n, enc_width, enc_up.shape[1]), BF16),
            pltpu.VMEM((enc_width, ff), BF16),
            pltpu.SemaphoreType.DMA((2,)),
        ]

    wks, wvs = (wk, swap(wk)), (wv, swap(wv))

    pool_rows = pool_tokens[:, 0].reshape(half * length, enc_width)
    normed = call(
        norm_body, [shape((half * length, enc_width))], [vm(), vm()], flops=half * length * enc_width
    )(pool_rows, enc_gain[None, :])[0]
    encoded = call(
        functools.partial(encoder_body, n, parts, not shares),
        [shape((half * length, enc_width))] + [shape((n, feats, cols))] * shares,
        [vm()] * 8 if shares else [vm()] * 2 + [hbm()] * 2,
        [pltpu.VMEM((half * length, ff), BF16)] + scratch,
        flops=4 * half * length * enc_width * ff,
        limit=ENCODER_LIMIT if shares else 48 * 1024 * 1024,
    )(pool_rows, normed, *pieces)
    enc = encoded[0]
    if shares:
        projection = encoded[1]
    enc_own, pool0_own = call(
        projected_body,
        [shape((half, length, enc_width + 2 * cols)), shape((half, length, 2 * cols))],
        [vm()] * 5,
        flops=8 * half * length * enc_width * cols,
        deps=before_projected,
    )(enc, *wks, *wvs)
    pool0_other = swap(pool0_own)
    heads = cols // HEAD
    chunk = rows // tracts
    slot_rows = tracts * slots * NT
    blocks_scratch = pltpu.VMEM((slot_rows, 2 * cols), BF16)
    part_scratch = pltpu.VMEM((slot_rows, cols), BF16)
    wide_scores = pltpu.VMEM((tracts * heads, chunk, slots * NT), F32)
    bf_scores = pltpu.VMEM((tracts * heads, chunk, slots * NT), BF16)
    attention_flops = 2 * rows * slots * NT * cols

    att, query0, probs0, enc_own = call(
        functools.partial(first_layer_body, n, tracts, slots),
        [
            shape((rows, cols)),
            shape((rows, cols)),
            shape((tracts * heads, chunk, slots * NT), F32),
        ],
        [smem(), smem()] + [vm()] * (6 + len(row_pieces)),
        [blocks_scratch],
        flops=2 * rows * width * cols + 2 * attention_flops,
        passing=[enc_own],
    )(ids, counts, *gains, *wqs, *row_pieces, pool0_own, pool0_other)
    enc_other = swap(enc_own)
    att_pieces = along_mp(att, n)
    rows1, *messages = call(
        functools.partial(between_body, n),
        [shape((rows, feats))] + [shape((rows + PAD, cols))] * n,
        [vm()] * (6 + n),
        flops=4 * rows * feats * n * cols,
        deps=[enc_other],
    )(*gains, own, *wouts, projection, *att_pieces)
    query_pieces = scattered(messages)
    dkv1, grad_query, scale1 = call(
        functools.partial(last_layer_body, n, width, tracts, slots),
        [shape((slot_rows, 2 * cols)), shape((rows + PAD, cols)), shape((rows, HEAD), F32)],
        [smem(), smem()] + [vm()] * (n + len(grad_parts) + 2),
        [
            pltpu.VMEM((rows, cols), F32),
            pltpu.VMEM((rows, cols), BF16),
            pltpu.VMEM((rows, cols), BF16),
            wide_scores,
            wide_scores,
            bf_scores,
            bf_scores,
            blocks_scratch,
        ],
        flops=5 * attention_flops,
    )(ids, counts, *query_pieces, *grad_parts, enc_own, enc_other)
    query_grads = along_mp(grad_query, n)
    enc_slots, kept1, sent1 = call(
        functools.partial(last_grads_body, tracts, slots),
        [shape((enc_width, slot_rows)), shape((enc_width, cols)), shape((enc_width, cols))],
        [smem(), vm(), vm(), vm()],
        flops=4 * enc_width * slot_rows * cols,
    )(ids, dkv1, enc_own, enc_other)
    half_shape = shape((enc_width // 2, cols))
    *messages, kept1, sent1 = call(
        functools.partial(back_between_body, n, width),
        [shape((rows, cols))] * n,
        [vm()] * (8 + n),
        flops=4 * rows * feats * n * cols,
        passing=[kept1, sent1],
    )(*gains, rows1, out_grad[:, 0], scale1, projection, *wouts, *query_grads)
    grad_pieces0 = scattered(messages)

    def over_dp(parts, order, deps=()):
        moved = [xor_move(part, "dp", by) for part, by in zip(parts, order)]
        return call(functools.partial(add_body, 2), [half_shape] * 2, [vm()] * 4, first=deps)(
            *parts, *moved
        )

    def summed(kept, sent, deps=()):
        parts = call(halves_body, [half_shape] * 2, [vm()] * 2)(kept, swap(sent))
        if dp == 4:
            parts = over_dp(over_dp(parts, (1, 2), deps), (2, 1))
        else:
            parts = [lax.psum(part, "dp") for part in parts]
        return jnp.concatenate(parts, axis=0)

    sum1 = summed(kept1, sent1, grad_pieces0[1:])
    dkv0 = call(
        functools.partial(first_back_body, n, tracts, slots),
        [shape((slot_rows, 2 * cols))],
        [smem()] + [vm()] * (n + 4),
        [
            pltpu.VMEM((rows, cols), BF16),
            wide_scores,
            bf_scores,
            bf_scores,
            part_scratch,
        ],
        flops=3 * attention_flops,
    )(ids, query0, probs0, *grad_pieces0, pool0_own, pool0_other)[0]
    sent0, kept0 = (
        call(
            functools.partial(part_grads_body, keep),
            [shape((enc_width, cols))],
            [vm()] * 2,
            flops=2 * enc_width * slot_rows * cols,
            deps=[] if keep else [sum1],
        )(enc_slots, dkv0)[0]
        for keep in (False, True)
    )
    sum0 = summed(kept0, sent0)
    received = swap(jnp.where(first, sum1, sum0))
    key_total = jnp.where(first, sum0, received)
    value_total = jnp.where(first, received, sum1)
    return (key_total[None], value_total[None])


def solution(mesh):
    placed = (
        P(None, "dp", None, "mp"),
        P(None, "dp", None, "mp"),
        P("section", "dp", None, None),
        P(None, "dp", None, None),
        P(None, "dp", None),
        P(),
        P(None, "mp"),
        P(None, "mp"),
        P("section", None),
        P("section", None, "mp"),
        P("section", None, "mp"),
        P("section", None, "mp"),
        P("section", None, "mp"),
    )
    return jax.shard_map(
        on_device,
        mesh=mesh,
        in_specs=placed,
        out_specs=(P("section", None, "mp"), P("section", None, "mp")),
        check_vma=False,
    )
```

```python
import functools

import jax
import jax.numpy as jnp
from jax import lax
from jax.experimental import pallas as pl
from jax.experimental.pallas import tpu as pltpu
from jax.sharding import PartitionSpec as P

HEAD = 128
NT = 128
EPSILON = 1e-05
SCALE = HEAD ** (-0.5)
PAD = 16
VMEM_LIMIT = 20 * 1024 * 1024
ENCODER_LIMIT = 32 * 1024 * 1024
FIRST_LIMIT = 60 * 1024 * 1024

BF16 = jnp.bfloat16
F32 = jnp.float32
NN = (((1,), (0,)), ((), ()))
NTR = (((1,), (1,)), ((), ()))
TNR = (((0,), (0,)), ((), ()))


def mm(a, b, dims=NN):
    return lax.dot_general(a, b, dims, preferred_element_type=F32)


def xor_move(value, axis, by):
    count = lax.axis_size(axis)
    return lax.ppermute(value, axis, [(i, i ^ by) for i in range(count)])


def places(n):
    return (0, 2, 3, 1) if n == 4 else tuple(range(n))


def swap(value):
    return xor_move(value, "section", 1)


def vm():
    return pl.BlockSpec(memory_space=pltpu.VMEM)


def hbm():
    return pl.BlockSpec(memory_space=pl.ANY)


def hbm_only():
    return pl.BlockSpec(memory_space=pltpu.HBM)


def smem():
    return pl.BlockSpec(memory_space=pltpu.SMEM)


def call(body, outs, specs, scratch=(), flops=0, limit=VMEM_LIMIT, first=(), deps=(), passing=()):
    count, more, kept, results = len(specs), len(deps), len(passing), len(outs)
    nbytes = sum(o.size * o.dtype.itemsize for o in outs)
    begin = len(first)
    start = begin + count + more + kept

    def kernel(*refs):
        given = refs[begin : begin + count]
        body(*given, *refs[start : start + results], *refs[start + results + kept :])

    def run(*args):
        return pl.pallas_call(
            kernel,
            out_shape=list(outs) + [shape(x.shape, x.dtype) for x in passing],
            in_specs=[hbm()] * begin + list(specs) + [hbm()] * (more + kept),
            out_specs=[vm() for _ in outs] + [hbm()] * kept,
            scratch_shapes=list(scratch),
            input_output_aliases={begin + count + more + i: results + i for i in range(kept)},
            compiler_params=pltpu.CompilerParams(vmem_limit_bytes=limit),
            cost_estimate=pl.CostEstimate(
                flops=flops // 1000, bytes_accessed=nbytes // 1000, transcendentals=0
            ),
        )(*first, *args, *deps, *passing)

    return run


def shape(dims, dtype=BF16):
    return jax.ShapeDtypeStruct(dims, dtype)


def to_row(column):
    rows = column.shape[0]
    here = lax.broadcasted_iota(jnp.int32, (rows, rows), 0)
    there = lax.broadcasted_iota(jnp.int32, (rows, rows), 1)
    return jnp.sum(jnp.where(here == there, column, 0.0), axis=0, keepdims=True)


def to_column(row):
    rows = row.shape[1]
    here = lax.broadcasted_iota(jnp.int32, (rows, rows), 0)
    there = lax.broadcasted_iota(jnp.int32, (rows, rows), 1)
    return jnp.sum(jnp.where(here == there, row, 0.0), axis=1, keepdims=True)


def slot_value(own, other, ids_ref, tract, slot, start, size):
    half = own.shape[0]
    s = lax.axis_index("section")
    place = ids_ref[s, tract, slot]
    mine, theirs = place - s * half, place - (1 - s) * half
    here = jnp.logical_and(mine >= 0, mine < half)
    cols = slice(start, start + size)
    return jnp.where(
        here,
        own[jnp.clip(mine, 0, half - 1), :, cols],
        other[jnp.clip(theirs, 0, half - 1), :, cols],
    )


def fill_slots(own, other, ids_ref, tracts, slots, blocks, start=0):
    for c in range(tracts):
        for k in range(slots):
            here = slice((c * slots + k) * NT, (c * slots + k + 1) * NT)
            blocks[here, :] = slot_value(own, other, ids_ref, c, k, start, blocks.shape[1])


def of_layer(layer, own_ref, other_ref, *index):
    index = index or (Ellipsis,)
    own = lax.axis_index("section") == layer
    return jnp.where(own, own_ref[index], other_ref[index])


def pack(value, cols):
    rows, feats = value.shape
    if feats >= cols:
        return jnp.concatenate([value[:, i : i + cols] for i in range(0, feats, cols)], axis=0)
    share = rows * feats // cols
    return jnp.concatenate([value[i : i + share] for i in range(0, rows, share)], axis=1)


def unpack(value, rows, feats):
    cols = value.shape[1]
    if feats >= cols:
        return jnp.concatenate(
            [value[i : i + rows] for i in range(0, value.shape[0], rows)], axis=1
        )
    return jnp.concatenate([value[:, i : i + feats] for i in range(0, cols, feats)], axis=0)


def share_body(n, up_ref, down_ref, wq_own, wq_other, rows_ref, *refs):
    outs, own_ref, sems = refs[:n], refs[n], refs[n + 1]
    s, m = lax.axis_index("section"), lax.axis_index("mp")
    place = s * lax.axis_size("dp") + lax.axis_index("dp")
    parts = 2 * lax.axis_size("dp")
    tall = up_ref.shape[0] // parts
    share = wq_own.shape[0] // (n * parts)
    rows = pl.ds(pl.multiple_of(place * tall, 16), tall)
    cols = pl.ds(pl.multiple_of(place * HEAD, HEAD), HEAD)
    copies = [pltpu.make_async_copy(up_ref.at[rows], outs[0].at[pl.ds(0, tall)], sems.at[0])]
    for side in range(2):
        copies.append(
            pltpu.make_async_copy(
                down_ref.at[pl.ds(side * tall, tall), cols],
                outs[0].at[pl.ds(tall, tall), pl.ds(side * HEAD, HEAD)],
                sems.at[1 + side],
            )
        )
    for copy in copies:
        copy.start()
    for i, d in enumerate(places(n)):
        start = ((m ^ d) * parts + place) * share
        here = pl.ds(pl.multiple_of(start, share), share)
        target = outs[i].at[pl.ds(2 * tall, share)]
        copies.append(pltpu.make_async_copy(wq_own.at[here], target, sems.at[3 + i]))

        @pl.when(s == 1)
        def _(here=here, target=target, i=i):
            pltpu.make_async_copy(wq_own.at[here], target, sems.at[3 + i]).start()

        @pl.when(s != 1)
        def _(here=here, target=target, i=i):
            pltpu.make_async_copy(wq_other.at[here], target, sems.at[3 + i]).start()

    total, length = rows_ref.shape[1], own_ref.shape[1]
    for i in range(own_ref.shape[0] // total):
        source = rows_ref.at[s, :, pl.ds(i * length, length)]
        target = own_ref.at[pl.ds(i * total, total)]
        copies.append(pltpu.make_async_copy(source, target, sems.at[3 + n + i]))
        copies[-1].start()
    for copy in copies:
        copy.wait()
    half = own_ref.shape[0] // 2
    outs[n - 1][2 * tall + share :, :] = own_ref[:half, :]
    for i in range(1, n):
        outs[i][: 2 * tall, :] = outs[0][: 2 * tall, :]


def line_body(n, tall, *refs):
    half = (refs[0].shape[0] - 2 * tall) // 2
    own_ref, far_ref = refs[n], refs[n + 1]
    near_ref, message, kept_ref = refs[n + 4 :]
    kept_ref[...] = own_ref[...]
    near_ref[...] = refs[n - 1][2 * (tall + half) :, :]
    rest = own_ref.shape[0] // 2
    message[:rest, :] = own_ref[rest:, :]
    message[rest:, :] = far_ref[...]
    for i in range(1, n):
        for j in range(2):
            start = 2 * tall + j * half
            refs[n + 2 + j][i - 1, :tall] = refs[i][j * tall : (j + 1) * tall, :]
            refs[n + 2 + j][i - 1, tall:] = refs[i][start : start + half, :]


def pair_body(up, up1, down, down2, near1, moved, far2, far3, ups, downs, message, near):
    for here, there, out_ref in ((up, up1, ups), (down, down2, downs)):
        out_ref[0] = here[...]
        out_ref[1] = there[...]
    first, rest, rows = near.shape[0], near1.shape[0], far2.shape[0]
    near[:rest, :] = near1[...]
    near[rest:, :] = moved[:rest, :]
    message[:first, :] = near[...]
    for i, far in enumerate((far3, far2)):
        start = rest + i * rows
        total = moved[start : start + rows, :].astype(F32) + far[...].astype(F32)
        message[first + i * rows : first + (i + 1) * rows, :] = total.astype(BF16)


def gather_body(
    up, up1, up2, down, down2, down1, moved, close, key_ref, value_ref,
    out_ref, next_ref, message, weight_ref,
):
    tall = key_ref.shape[0]
    weight_ref[:tall, :] = key_ref[...]
    weight_ref[tall:, :] = value_ref[...]
    for base, parts in ((0, (up, up1, up2)), (4, (down, down2, down1))):
        near = 1 if base == 0 else 2
        out_ref[base] = parts[0][...]
        out_ref[base + near] = parts[1][...]
        out_ref[base + 3 - near] = parts[2][0]
        out_ref[base + 3] = parts[2][1]
    first, rows = next_ref.shape[0], close.shape[0]
    next_ref[...] = moved[:first, :]
    message[:first, :] = moved[:first, :]
    total = moved[first + rows :, :].astype(F32) + close[...].astype(F32)
    message[first:, :] = total.astype(BF16)


def rows_body(cols, rows_ref, own_ref):
    own_ref[...] = pack(rows_ref[lax.axis_index("section")], cols)


def query_shares_body(n, wq_own, wq_other, *outs):
    m = lax.axis_index("mp")
    tall = outs[0].shape[0]
    for i, d in enumerate(places(n)):
        here = pl.ds(pl.multiple_of((m ^ d) * tall, tall), tall)
        outs[i][...] = of_layer(1, wq_own, wq_other, here, slice(None))


def out_grads_body(n, og_ref, wout_own, wout_other, *outs):
    s, m = lax.axis_index("section"), lax.axis_index("mp")
    cols = outs[0].shape[1]
    rows = og_ref.shape[1]
    for i, d in enumerate(places(n)):
        here = pl.ds(pl.multiple_of((m ^ d) * cols, cols), cols)
        weight = of_layer(1, wout_own, wout_other, here, slice(None))
        outs[i][...] = mm(og_ref[s], weight, NTR).astype(BF16)
    for i, out_ref in enumerate(outs[1:3]):
        if len(outs) > n:
            outs[n][i * rows : (i + 1) * rows, :] = out_ref[...]


def add_body(count, *refs):
    for i in range(count):
        total = refs[i][...].astype(F32) + refs[count + i][...].astype(F32)
        refs[2 * count + i][...] = total.astype(BF16)


def pieces_body(kept_ref, other_ref, *outs):
    start = 0
    for out_ref in outs:
        here = slice(start, start + out_ref.shape[0])
        start += out_ref.shape[0]
        total = kept_ref[here, :].astype(F32) + other_ref[here, :].astype(F32)
        out_ref[...] = total.astype(BF16)


def norm_body(pool_ref, gain_ref, out_ref):
    wide = pool_ref[...].astype(F32)
    scale = lax.rsqrt(jnp.mean(wide * wide, axis=-1, keepdims=True) + EPSILON)
    out_ref[...] = (wide * scale * gain_ref[...]).astype(BF16)


def encoder_body(n, parts, gathered, *refs):
    pool_ref, normed_ref = refs[:2]
    if gathered:
        pieces, (enc_ref, hidden, up, down, *sems) = refs[2:4], refs[4:]
    else:
        pieces, (enc_ref, wq_ref, hidden, up, down) = refs[2:4], refs[8:]
        up_ref, down_ref, wq_own, wq_other = refs[4:8]
    m = lax.axis_index("mp")
    if gathered:
        copies = [[pltpu.make_async_copy(pieces[i], (up, down)[i], sems[0].at[i])] for i in range(2)]
        downs = copies[1]
        ups = copies[:1] + [[]] * (n - 1)
        ups[0][0].start()
        downs[0].start()
    else:
        s, g = lax.axis_index("section"), lax.axis_index("dp")
        dp, tall, wide = parts // 2, up.shape[2], HEAD
        share = pieces[0].shape[2] - tall
        ups, downs = [[] for _ in range(n)], []
        up[m] = up_ref[...].reshape(up.shape[1:])
        down[m] = down_ref[...]
        here = pl.ds(pl.multiple_of(m * wq_ref.shape[1], wq_ref.shape[1]), wq_ref.shape[1])
        wq_ref[0] = of_layer(1, wq_own, wq_other, here, slice(None))
        for j, dz in enumerate(places(n)[1:]):
            for i in range(parts):
                half, dg = divmod(i, dp)
                place = (s ^ half) * dp + (g ^ dg)
                for k in range(2):
                    start = pl.multiple_of((2 * place + k) * share, share)
                    wq_ref[j + 1, pl.ds(start, share)] = pieces[half][k * dp + dg, j, tall:]
                up[m ^ dz, place] = pieces[half][dg, j, :tall]
                where = pl.ds(pl.multiple_of(place * wide, wide), wide)
                for side in range(2):
                    rows_of = slice(side * tall, (side + 1) * tall)
                    down[m ^ dz, rows_of, where] = pieces[half][
                        dp + dg, j, :tall, side * wide : (side + 1) * wide
                    ]
    rows, width = normed_ref.shape
    cols = up.shape[-1]
    chunk = rows // 4
    for dz in range(n):
        for copy in ups[dz]:
            copy.wait()
        k = dz if gathered else m ^ dz
        there = pl.ds(pl.multiple_of(k * cols, cols), cols)
        weight = up[k].reshape(width, cols)
        for r in range(0, rows, chunk):
            product = mm(normed_ref[r : r + chunk, :], weight)
            hidden[r : r + chunk, there] = jax.nn.gelu(product).astype(BF16)
    for copy in downs:
        copy.wait()
    for r in range(0, rows, chunk):
        weight = down[...].reshape(width, hidden.shape[1])
        enc = pool_ref[r : r + chunk, :].astype(F32) + mm(hidden[r : r + chunk, :], weight, NTR)
        enc_ref[r : r + chunk, :] = enc.astype(BF16)


def projected_body(layer, enc_ref, wkv_own, wkv_other, out_ref):
    count, length, total = out_ref.shape
    cols, width = wkv_own.shape[1], wkv_own.shape[0] // 2
    enc = enc_ref[...]
    start = total - 2 * cols
    if start:
        out_ref[:, :, :start] = enc.reshape(count, length, width)
    for kind in range(2):
        weight = of_layer(layer, wkv_own, wkv_other, slice(kind * width, (kind + 1) * width))
        out = mm(enc, weight).astype(BF16).reshape(count, length, cols)
        out_ref[:, :, start + kind * cols : start + (kind + 1) * cols] = out


def slot_slice(c, slots):
    return slice(c * slots * NT, (c + 1) * slots * NT)


def softmax_used(scores, used):
    lane = lax.broadcasted_iota(jnp.int32, scores.shape, scores.ndim - 1)
    scores = jnp.where(lane < used * NT, scores, -1e30)
    powers = jnp.exp(scores - jnp.max(scores, axis=-1, keepdims=True))
    return powers / jnp.sum(powers, axis=-1, keepdims=True)


def query_body(n, gain_own, gain_other, wq_own, wq_other, *refs):
    pieces, query_ref = refs[:-1], refs[-1]
    m = lax.axis_index("mp")
    rows, cols = query_ref.shape
    feats = gain_own.shape[-1]

    def piece(k):
        if len(pieces) == n or k < 2:
            return unpack(pieces[k][...], rows, feats).astype(F32)
        inner = jnp.logical_or(m == 1, m == 2)
        inside, outside = pieces[2 * k - 2 : 2 * k]
        here = slice(0, rows * feats // cols)
        value = jnp.where(inner, inside[here, :], outside[here, :])
        return unpack(value, rows, feats).astype(F32)

    total = jnp.zeros((rows, 1), F32)
    for k in range(n):
        wide = piece(k)
        total = total + jnp.sum(wide * wide, axis=-1, keepdims=True)
    scale = lax.rsqrt(total / (n * feats) + EPSILON)
    raw = jnp.zeros((rows, cols), F32)
    for k in range(n):
        gain = of_layer(0, gain_own, gain_other, m ^ k)
        normed = (piece(k) * scale * gain).astype(BF16)
        here = pl.ds(pl.multiple_of((m ^ k) * feats, feats), feats)
        raw = raw + mm(normed, of_layer(0, wq_own, wq_other, here, slice(None)))
    query_ref[...] = (raw * SCALE).astype(BF16)


def scores_of(tracts, slots, heads, query_ref, counts_ref, blocks, probs_ref):
    s = lax.axis_index("section")
    length = query_ref.shape[0] // tracts
    for c in range(tracts):
        here, span = slice(c * length, (c + 1) * length), slot_slice(c, slots)
        for h in range(heads):
            there = slice(h * HEAD, (h + 1) * HEAD)
            probs_ref[c * heads + h] = mm(query_ref[here, there], blocks[span, there], NTR)
    for c in range(tracts):
        both = slice(c * heads, (c + 1) * heads)
        probs_ref[both] = softmax_used(probs_ref[both], counts_ref[s, c])


def first_layer_body(
    tracts, slots, ids_ref, counts_ref, query_ref, own, other, att_ref, probs_ref, blocks
):
    fill_slots(own, other, ids_ref, tracts, slots, blocks)
    rows, cols = query_ref.shape
    heads, length = cols // HEAD, rows // tracts
    scores_of(tracts, slots, heads, query_ref, counts_ref, blocks, probs_ref)
    for c in range(tracts):
        here, span = slice(c * length, (c + 1) * length), slot_slice(c, slots)
        for h in range(heads):
            there = slice(h * HEAD, (h + 1) * HEAD)
            beyond = slice(cols + h * HEAD, cols + (h + 1) * HEAD)
            probs = probs_ref[c * heads + h].astype(BF16)
            att_ref[here, there] = mm(probs, blocks[span, beyond]).astype(BF16)


def between_body(n, *refs):
    gain_own, gain_other, own_ref, wout_own, wout_other, wq_ref = refs[:6]
    pieces = refs[6 : 6 + n]
    rows_ref, messages = refs[6 + n], refs[7 + n :]
    m = lax.axis_index("mp")
    rows, cols = pieces[0].shape
    feats = rows_ref.shape[1]
    wide = unpack(own_ref[...], rows, feats).astype(F32)
    for i, d in enumerate(places(n)):
        here = pl.ds(pl.multiple_of((m ^ d) * cols, cols), cols)
        wide = wide + mm(pieces[i][...], of_layer(0, wout_own, wout_other, here, slice(None)))
    rounded = wide.astype(BF16)
    rows_ref[...] = rounded
    wide = rounded.astype(F32)
    square = to_row(jnp.sum(wide * wide, axis=-1, keepdims=True))
    high = square.astype(BF16).astype(F32)
    index = lax.broadcasted_iota(jnp.int32, (PAD, rows), 0)
    extra = jnp.where(index == 0, high, jnp.where(index == 1, square - high, 0.0)).astype(BF16)
    gained = (wide * of_layer(1, gain_own, gain_other, m)).astype(BF16)
    for i in range(n):
        messages[i][:rows, :] = mm(gained, wq_ref[i]).astype(BF16)
        messages[i][rows:, :] = extra


def prob_grads(tracts, slots, heads, att_ref, blocks, grads_ref):
    rows, cols = att_ref.shape
    length = rows // tracts
    for c in range(tracts):
        here, span = slice(c * length, (c + 1) * length), slot_slice(c, slots)
        for h in range(heads):
            there = slice(h * HEAD, (h + 1) * HEAD)
            beyond = slice(cols + h * HEAD, cols + (h + 1) * HEAD)
            grads_ref[c * heads + h] = mm(att_ref[here, there], blocks[span, beyond], NTR)


def score_grads(tracts, heads, probs_ref, grads_ref, scores_ref, soft_ref):
    for c in range(tracts):
        both = slice(c * heads, (c + 1) * heads)
        probs, grads = probs_ref[both], grads_ref[both]
        inner = jnp.sum(probs * grads, axis=-1, keepdims=True)
        scores_ref[both] = (probs * (grads - inner)).astype(BF16)
        soft_ref[both] = probs.astype(BF16)


def slot_grads(tracts, slots, heads, cols, query_ref, att_ref, scores_ref, soft_ref, dkv_ref):
    length = att_ref.shape[0] // tracts
    for c in range(tracts):
        here, span = slice(c * length, (c + 1) * length), slot_slice(c, slots)
        for h in range(heads):
            there = slice(h * HEAD, (h + 1) * HEAD)
            beyond = slice(cols + h * HEAD, cols + (h + 1) * HEAD)
            dkv_ref[span, there] = mm(
                scores_ref[c * heads + h], query_ref[here, there], TNR
            ).astype(BF16)
            dkv_ref[span, beyond] = mm(
                soft_ref[c * heads + h], att_ref[here, there], TNR
            ).astype(BF16)


def last_values_body(tracts, slots, ids_ref, *refs):
    grads, (own, other, blocks, att_ref, grads_ref) = refs[:-5], refs[-5:]
    fill_slots(own, other, ids_ref, tracts, slots, blocks, own.shape[2] - blocks.shape[1])
    rows, cols = att_ref.shape
    grad = jnp.zeros((rows, cols), F32)
    for part in grads:
        start = grads[1].shape[0] - 2 * rows if part.shape[0] > rows else 0
        grad = grad + part[start : start + rows, :].astype(F32)
    att_ref[...] = grad.astype(BF16)
    prob_grads(tracts, slots, cols // HEAD, att_ref, blocks, grads_ref)


def last_layer_body(n, width, tracts, slots, counts_ref, *refs):
    messages, (blocks, grads_ref) = refs[:n], refs[n : n + 2]
    out_ref, scale_ref, query_ref, scores_ref, soft_ref, raw_ref, probs_ref = refs[n + 2 :]
    rows, cols = raw_ref.shape
    raw = jnp.zeros((rows, cols), F32)
    square = jnp.zeros((1, rows), F32)
    for d in range(n):
        raw = raw + messages[d][:rows, :].astype(F32)
        extra = messages[d][rows:, :].astype(F32)
        square = square + extra[0:1, :] + extra[1:2, :]
    scale = lax.rsqrt(to_column(square) / width + EPSILON)
    scale_ref[...] = jnp.broadcast_to(scale, scale_ref.shape)
    raw = raw * scale
    raw_ref[...] = raw
    query_ref[...] = (raw * SCALE).astype(BF16)
    length = rows // tracts
    heads = cols // HEAD
    scores_of(tracts, slots, heads, query_ref, counts_ref, blocks, probs_ref)
    score_grads(tracts, heads, probs_ref, grads_ref, scores_ref, soft_ref)
    for c in range(tracts):
        here, span = slice(c * length, (c + 1) * length), slot_slice(c, slots)
        for h in range(heads):
            there = slice(h * HEAD, (h + 1) * HEAD)
            grad_query = mm(scores_ref[c * heads + h], blocks[span, there]) * SCALE
            out_ref[here, there] = grad_query.astype(BF16)
    part = jnp.sum(out_ref[:rows, :].astype(F32) * raw_ref[...], axis=-1, keepdims=True)
    index = lax.broadcasted_iota(jnp.int32, (PAD, rows), 0)
    out_ref[rows:, :] = jnp.where(index == 0, to_row(part), 0.0).astype(BF16)


def last_slots_body(tracts, slots, query_ref, att_ref, scores_ref, soft_ref, dkv_ref):
    cols = query_ref.shape[1]
    slot_grads(
        tracts, slots, cols // HEAD, cols, query_ref, att_ref, scores_ref, soft_ref, dkv_ref
    )


def weight_grads(enc_ref, dkv_ref, kept_ref, sent_ref):
    cols = kept_ref.shape[1]
    first = lax.axis_index("section") == 0
    chunk = enc_ref.shape[0] // 2
    for r in range(0, enc_ref.shape[0], chunk):
        total = mm(enc_ref[r : r + chunk, :], dkv_ref[...])
        keys, values = total[:, :cols], total[:, cols:]
        kept_ref[r : r + chunk, :] = jnp.where(first, keys, values).astype(BF16)
        sent_ref[r : r + chunk, :] = jnp.where(first, values, keys).astype(BF16)


def part_grads_body(keep, enc_ref, dkv_ref, out_ref):
    cols = out_ref.shape[1]
    kind = lax.axis_index("section") if keep else 1 - lax.axis_index("section")
    here = pl.ds(pl.multiple_of(kind * cols, cols), cols)
    out_ref[...] = mm(enc_ref[...], dkv_ref[:, here]).astype(BF16)


def last_grads_body(
    tracts, slots, ids_ref, dkv_ref, own, other, enc_ref, kept_ref, sent_ref
):
    for c in range(tracts):
        for k in range(slots):
            here = slice((c * slots + k) * NT, (c * slots + k + 1) * NT)
            enc_ref[:, here] = slot_value(own, other, ids_ref, c, k, 0, enc_ref.shape[0]).T
    weight_grads(enc_ref, dkv_ref, kept_ref, sent_ref)


def back_between_body(n, width, *refs):
    gain_own, gain_other, rows_ref, og_ref, scale_ref, wq_ref = refs[:6]
    wout_own, wout_other = refs[6:8]
    pieces, messages = refs[8 : 8 + n], refs[8 + n :]
    s, m = lax.axis_index("section"), lax.axis_index("mp")
    rows, feats = rows_ref.shape
    cols = pieces[0].shape[1]
    normed = jnp.zeros((rows, feats), F32)
    total = jnp.zeros((1, rows), F32)
    for d in range(n):
        normed = normed + mm(pieces[d][:rows, :], wq_ref[d], NTR)
        total = total + pieces[d][rows:, :].astype(F32)[0:1, :]
    scale = scale_ref[:, 0:1]
    wide = rows_ref[...].astype(F32)
    gain = of_layer(1, gain_own, gain_other, m)
    grad = og_ref[s].astype(F32) + scale * gain * normed
    grad = grad - wide * (scale * scale * (to_column(total) / width))
    grad = grad.astype(BF16)
    for i, d in enumerate(places(n)):
        here = pl.ds(pl.multiple_of((m ^ d) * cols, cols), cols)
        weight = of_layer(0, wout_own, wout_other, here, slice(None))
        messages[i][...] = mm(grad, weight, NTR).astype(BF16)


def first_back_body(n, tracts, slots, query_ref, probs_ref, blocks, *refs):
    grads, (dkv_ref, att_ref, grads_ref, scores_ref, soft_ref) = refs[:n], refs[n:]
    rows, cols = query_ref.shape
    grad = jnp.zeros((rows, cols), F32)
    for d in range(n):
        grad = grad + grads[d][...].astype(F32)
    att_ref[...] = grad.astype(BF16)
    heads = cols // HEAD
    prob_grads(tracts, slots, heads, att_ref, blocks, grads_ref)
    score_grads(tracts, heads, probs_ref, grads_ref, scores_ref, soft_ref)
    slot_grads(tracts, slots, heads, cols, query_ref, att_ref, scores_ref, soft_ref, dkv_ref)


def along_mp(value, n):
    return [value] + [xor_move(value, "mp", d) for d in places(n)[1:]]


def scattered(messages):
    order = places(len(messages))
    return [messages[0]] + [xor_move(messages[i], "mp", order[i]) for i in range(1, len(messages))]


def on_device(
    segment_input,
    out_grad,
    pool_tokens,
    neighbour_ids,
    neighbour_counts,
    enc_gain,
    enc_up,
    enc_down,
    norm_gain,
    w_query,
    w_key,
    w_value,
    w_out,
):
    n, dp = lax.axis_size("mp"), lax.axis_size("dp")
    s = lax.axis_index("section")
    _, _, rows, feats = segment_input.shape
    width = n * feats
    cols = w_query.shape[2]
    half, _, length, enc_width = pool_tokens.shape
    tracts, slots = neighbour_ids.shape[2:]
    ids, counts = neighbour_ids[:, 0], neighbour_counts[:, 0]
    ff = enc_down.shape[0]
    first = s == 0
    gain = norm_gain.reshape(n, 1, feats)
    wq, wk, wv, wout = w_query[0], w_key[0], w_value[0], w_out[0]
    gains, wqs, wouts = ((w, swap(w)) for w in (gain, wq, wout))

    pool_rows = pool_tokens[:, 0].reshape(half * length, enc_width)
    normed = call(
        norm_body, [shape((half * length, enc_width))], [vm(), vm()], flops=half * length * enc_width
    )(pool_rows, enc_gain[None, :])[0]
    down_t = enc_down.T
    parts = 2 * dp
    up_rows, down_cols = enc_width // parts, ff // parts
    shares = up_rows % 16 == 0 and enc_width // n == 2 * up_rows and down_cols == HEAD
    shares = shares and enc_up.shape[1] == 2 * down_cols and dp == 4 and n == 4
    shares = shares and feats % (32 * parts) == 0 and cols == enc_up.shape[1]
    if shares:
        own_shape = shape((rows * feats // cols, cols))
        messages = [shape((2 * up_rows + feats // parts, 2 * down_cols))] * (n - 1)
        rest = own_shape.shape[0] // 2
        longer = shape((messages[0].shape[0] + rest, cols))
        *messages, own = call(
            functools.partial(share_body, n),
            messages + [longer, own_shape],
            [hbm()] * 5,
            [pltpu.SemaphoreType.DMA((3 + n + feats // cols,))],
            limit=FIRST_LIMIT,
        )(enc_up, down_t, *wqs, segment_input[:, 0])
        line = scattered(messages)
        *grads, far_grads = call(
            functools.partial(out_grads_body, n),
            [shape((rows, cols))] * n + [shape((2 * rows, cols))],
            [vm()] * 3,
            flops=2 * rows * width * cols,
        )(out_grad[:, 0], *wouts)
        piece = (n - 1, up_rows + feats // (2 * parts), 2 * down_cols)
        up, down, near, message, own = call(
            functools.partial(line_body, n, up_rows),
            [shape(piece)] * 2
            + [shape((rest, cols)), shape((rest + 2 * rows, cols)), own_shape],
            [vm()] * (n + 2),
            deps=[gains[1]],
        )(*line, own, far_grads)
        inner, outer = [(1, 2), (2, 1)], [(1, 0), (2, 3)]
        up1, down2 = xor_move(up, "dp", 1), xor_move(down, "dp", 2)
        far_inner = lax.ppermute(own, "mp", inner)
        message = xor_move(message, "mp", 1)
        ups, downs, message, near = call(
            pair_body,
            [shape((2,) + piece)] * 2 + [shape((own_shape.shape[0] + 2 * rows, cols)), own_shape],
            [vm()] * 8,
            deps=[far_inner],
        )(up, up1, down, down2, near, message, grads[1], grads[2])
        up2, down1 = xor_move(ups, "dp", 2), xor_move(downs, "dp", 1)
        next_outer = lax.ppermute(far_inner, "mp", outer)
        message = lax.ppermute(message, "mp", inner)
        last = shape((own_shape.shape[0] + rows, cols))
        gathered, next_inner, close, wkv = call(
            gather_body,
            [shape((parts,) + piece), own_shape, last, shape((2 * enc_width, cols))],
            [vm()] * 10,
            deps=[next_outer, normed],
        )(up, up1, up2, down, down2, down1, message, grads[3], wk, wv)
        pieces = [gathered, swap(gathered), enc_up, down_t, *wqs]
        close = xor_move(close, "mp", 1)
        grad_parts = [grads[0], message, close]
        row_pieces = [own, near, next_inner, next_outer, far_inner, close]
        before_projected = [close]
        scratch = [
            pltpu.VMEM((n, parts, up_rows, enc_up.shape[1]), BF16),
            pltpu.VMEM((n, enc_width // n, ff), BF16),
        ]
    else:
        own = call(
            functools.partial(rows_body, cols), [shape((rows * feats // cols, cols))], [vm()]
        )(segment_input[:, 0])[0]
        grad_parts = call(
            functools.partial(out_grads_body, n),
            [shape((rows, cols))] * n,
            [vm()] * 3,
            flops=2 * rows * width * cols,
        )(out_grad[:, 0], *wouts)
        row_pieces, grad_parts = along_mp(own, n), scattered(list(grad_parts))
        query_shares = call(
            functools.partial(query_shares_body, n), [shape((feats, cols))] * n, [vm()] * 2
        )(*wqs)
        projection = jnp.stack(scattered(query_shares))
        wkv = jnp.concatenate([wk, wv], axis=0)
        before_projected = []
        pieces = [
            lax.all_gather(enc_up, "mp", axis=0),
            lax.all_gather(down_t, "mp", axis=0, tiled=True),
        ]
        scratch = [
            pltpu.VMEM((n, enc_width, enc_up.shape[1]), BF16),
            pltpu.VMEM((enc_width, ff), BF16),
            pltpu.SemaphoreType.DMA((2,)),
        ]

    wkvs = (wkv, swap(wkv))

    encoded = call(
        functools.partial(encoder_body, n, parts, not shares),
        [shape((half * length, enc_width))] + [shape((n, feats, cols))] * shares,
        [vm()] * 8 if shares else [vm()] * 2 + [hbm()] * 2,
        [pltpu.VMEM((half * length, ff), BF16)] + scratch,
        flops=4 * half * length * enc_width * ff,
        limit=ENCODER_LIMIT if shares else 48 * 1024 * 1024,
    )(pool_rows, normed, *pieces)
    enc = encoded[0]
    if shares:
        projection = encoded[1]
    pool0_own, enc_own = (
        call(
            functools.partial(projected_body, layer),
            [shape((half, length, layer * enc_width + 2 * cols))],
            [vm()] * 3,
            flops=4 * half * length * enc_width * cols,
            deps=before_projected,
        )(enc, *wkvs)[0]
        for layer in (0, 1)
    )
    pool0_other = swap(pool0_own)
    heads = cols // HEAD
    chunk = rows // tracts
    slot_rows = tracts * slots * NT
    wide_scores = pltpu.VMEM((tracts * heads, chunk, slots * NT), F32)
    bf_scores = pltpu.VMEM((tracts * heads, chunk, slots * NT), BF16)
    attention_flops = 2 * rows * slots * NT * cols

    wide_shape = shape((tracts * heads, chunk, slots * NT), F32)
    block_shape = shape((slot_rows, 2 * cols))
    query0 = call(
        functools.partial(query_body, n),
        [shape((rows, cols))],
        [vm()] * (4 + len(row_pieces)),
        flops=2 * rows * width * cols,
        deps=[pool0_own],
    )(*gains, *wqs, *row_pieces)[0]
    att, probs0, blocks0, enc_own = call(
        functools.partial(first_layer_body, tracts, slots),
        [shape((rows, cols)), wide_shape, block_shape],
        [smem(), smem()] + [vm()] * 3,
        flops=2 * attention_flops,
        passing=[enc_own],
    )(ids, counts, query0, pool0_own, pool0_other)
    enc_other = swap(enc_own)
    att_pieces = along_mp(att, n)
    rows1, *messages = call(
        functools.partial(between_body, n),
        [shape((rows, feats))] + [shape((rows + PAD, cols))] * n,
        [vm()] * (6 + n),
        flops=4 * rows * feats * n * cols,
        deps=[enc_other],
    )(*gains, own, *wouts, projection, *att_pieces)
    query_pieces = scattered(messages)
    bf_shape = shape((tracts * heads, chunk, slots * NT))
    blocks1, att1, prob_grads1 = call(
        functools.partial(last_values_body, tracts, slots),
        [block_shape, shape((rows, cols)), wide_shape],
        [smem()] + [vm()] * (len(grad_parts) + 2),
        flops=attention_flops,
    )(ids, *grad_parts, enc_own, enc_other)
    grad_query, scale1, query1, *soft1 = call(
        functools.partial(last_layer_body, n, width, tracts, slots),
        [shape((rows + PAD, cols)), shape((rows, HEAD), F32), shape((rows, cols))] + [bf_shape] * 2,
        [smem()] + [vm()] * (n + 2),
        [pltpu.VMEM((rows, cols), F32), wide_scores],
        flops=3 * attention_flops,
    )(counts, *query_pieces, blocks1, prob_grads1)
    dkv1 = call(
        functools.partial(last_slots_body, tracts, slots),
        [shape((slot_rows, 2 * cols))],
        [vm()] * 4,
        flops=2 * attention_flops,
    )(query1, att1, *soft1)[0]
    query_grads = along_mp(grad_query, n)
    enc_slots, kept1, sent1 = call(
        functools.partial(last_grads_body, tracts, slots),
        [shape((enc_width, slot_rows)), shape((enc_width, cols)), shape((enc_width, cols))],
        [smem(), vm(), vm(), vm()],
        flops=4 * enc_width * slot_rows * cols,
    )(ids, dkv1, enc_own, enc_other)
    *messages, kept1, sent1 = call(
        functools.partial(back_between_body, n, width),
        [shape((rows, cols))] * n,
        [vm()] * (8 + n),
        flops=4 * rows * feats * n * cols,
        passing=[kept1, sent1],
    )(*gains, rows1, out_grad[:, 0], scale1, projection, *wouts, *query_grads)
    grad_pieces0 = scattered(messages)

    def over_dp(parts, order):
        size = len(parts)
        moved = [None] * size
        for by in sorted(set(order)):
            members = [i for i in range(size) if order[i] == by]
            if len(members) == 1:
                moved[members[0]] = xor_move(parts[members[0]], "dp", by)
                continue
            message = xor_move(jnp.concatenate([parts[i] for i in members], axis=0), "dp", by)
            start = 0
            for i in members:
                moved[i] = lax.slice_in_dim(message, start, start + parts[i].shape[0])
                start += parts[i].shape[0]
        shapes = [shape(part.shape) for part in parts]
        return call(functools.partial(add_body, size), shapes, [vm()] * (2 * size))(*parts, *moved)

    def pieces_of(kept, sent, sizes):
        parts = [shape((size, cols)) for size in sizes]
        return call(pieces_body, parts, [vm()] * 2)(kept, swap(sent))

    size = enc_width // 2
    early = size // 2 + 16 if size % 32 == 0 else size // 2
    ax, bx, ay, by = pieces_of(kept1, sent1, [early, size - early] * 2)
    if dp == 4:
        ax, ay = over_dp([ax, ay], (1, 2))
    dkv0 = call(
        functools.partial(first_back_body, n, tracts, slots),
        [shape((slot_rows, 2 * cols))],
        [vm()] * (n + 3),
        [pltpu.VMEM((rows, cols), BF16), wide_scores, bf_scores, bf_scores],
        flops=3 * attention_flops,
    )(query0, probs0, blocks0, *grad_pieces0)[0]
    sent0, kept0 = (
        call(
            functools.partial(part_grads_body, keep),
            [shape((enc_width, cols))],
            [vm()] * 2,
            flops=2 * enc_width * slot_rows * cols,
            deps=[] if keep else [ax, ay],
        )(enc_slots, dkv0)[0]
        for keep in (False, True)
    )
    top, bottom = pieces_of(kept0, sent0, [size] * 2)
    if dp == 4:
        top, bottom, ax, ay, bx, by = over_dp([top, bottom, ax, ay, bx, by], (1, 2, 2, 1, 1, 2))
        top, bottom, bx, by = over_dp([top, bottom, bx, by], (2, 1, 2, 1))
    else:
        top, bottom, ax, ay, bx, by = lax.psum((top, bottom, ax, ay, bx, by), "dp")
    sum0 = jnp.concatenate([top, bottom], axis=0)
    sum1 = jnp.concatenate([ax, bx, ay, by], axis=0)
    received = swap(jnp.where(first, sum1, sum0))
    key_total = jnp.where(first, sum0, received)
    value_total = jnp.where(first, received, sum1)
    return (key_total[None], value_total[None])


def solution(mesh):
    placed = (
        P(None, "dp", None, "mp"),
        P(None, "dp", None, "mp"),
        P("section", "dp", None, None),
        P(None, "dp", None, None),
        P(None, "dp", None),
        P(),
        P(None, "mp"),
        P(None, "mp"),
        P("section", None),
        P("section", None, "mp"),
        P("section", None, "mp"),
        P("section", None, "mp"),
        P("section", None, "mp"),
    )
    return jax.shard_map(
        on_device,
        mesh=mesh,
        in_specs=placed,
        out_specs=(P("section", None, "mp"), P("section", None, "mp")),
        check_vma=False,
    )
```

```python
import functools

import jax
import jax.numpy as jnp
from jax import lax
from jax.experimental import pallas as pl
from jax.experimental.pallas import tpu as pltpu
from jax.sharding import PartitionSpec as P

HEAD = 128
NT = 128
EPSILON = 1e-05
SCALE = HEAD ** (-0.5)
PAD = 16
VMEM_LIMIT = 20 * 1024 * 1024
ENCODER_LIMIT = 32 * 1024 * 1024
FIRST_LIMIT = 60 * 1024 * 1024

BF16 = jnp.bfloat16
F32 = jnp.float32
NN = (((1,), (0,)), ((), ()))
NTR = (((1,), (1,)), ((), ()))
TNR = (((0,), (0,)), ((), ()))


def mm(a, b, dims=NN):
    return lax.dot_general(a, b, dims, preferred_element_type=F32)


def xor_move(value, axis, by):
    count = lax.axis_size(axis)
    return lax.ppermute(value, axis, [(i, i ^ by) for i in range(count)])


def places(n):
    return (0, 2, 3, 1) if n == 4 else tuple(range(n))


def swap(value):
    return xor_move(value, "section", 1)


def vm():
    return pl.BlockSpec(memory_space=pltpu.VMEM)


def hbm():
    return pl.BlockSpec(memory_space=pl.ANY)


def hbm_only():
    return pl.BlockSpec(memory_space=pltpu.HBM)


def smem():
    return pl.BlockSpec(memory_space=pltpu.SMEM)


def call(body, outs, specs, scratch=(), flops=0, limit=VMEM_LIMIT, first=(), deps=(), passing=()):
    count, more, kept, results = len(specs), len(deps), len(passing), len(outs)
    nbytes = sum(o.size * o.dtype.itemsize for o in outs)
    begin = len(first)
    start = begin + count + more + kept

    def kernel(*refs):
        given = refs[begin : begin + count]
        body(*given, *refs[start : start + results], *refs[start + results + kept :])

    def run(*args):
        return pl.pallas_call(
            kernel,
            out_shape=list(outs) + [shape(x.shape, x.dtype) for x in passing],
            in_specs=[hbm()] * begin + list(specs) + [hbm()] * (more + kept),
            out_specs=[vm() for _ in outs] + [hbm()] * kept,
            scratch_shapes=list(scratch),
            input_output_aliases={begin + count + more + i: results + i for i in range(kept)},
            compiler_params=pltpu.CompilerParams(vmem_limit_bytes=limit),
            cost_estimate=pl.CostEstimate(
                flops=flops // 1000, bytes_accessed=nbytes // 1000, transcendentals=0
            ),
        )(*first, *args, *deps, *passing)

    return run


def shape(dims, dtype=BF16):
    return jax.ShapeDtypeStruct(dims, dtype)


def to_row(column):
    rows = column.shape[0]
    here = lax.broadcasted_iota(jnp.int32, (rows, rows), 0)
    there = lax.broadcasted_iota(jnp.int32, (rows, rows), 1)
    return jnp.sum(jnp.where(here == there, column, 0.0), axis=0, keepdims=True)


def to_column(row):
    rows = row.shape[1]
    here = lax.broadcasted_iota(jnp.int32, (rows, rows), 0)
    there = lax.broadcasted_iota(jnp.int32, (rows, rows), 1)
    return jnp.sum(jnp.where(here == there, row, 0.0), axis=1, keepdims=True)


def slot_value(own, other, ids_ref, tract, slot, start, size):
    half = own.shape[0]
    s = lax.axis_index("section")
    place = ids_ref[s, tract, slot]
    mine, theirs = place - s * half, place - (1 - s) * half
    here = jnp.logical_and(mine >= 0, mine < half)
    cols = slice(start, start + size)
    return jnp.where(
        here,
        own[jnp.clip(mine, 0, half - 1), :, cols],
        other[jnp.clip(theirs, 0, half - 1), :, cols],
    )


def fill_slots(own, other, ids_ref, tracts, slots, blocks, start=0):
    for c in range(tracts):
        for k in range(slots):
            here = slice((c * slots + k) * NT, (c * slots + k + 1) * NT)
            blocks[here, :] = slot_value(own, other, ids_ref, c, k, start, blocks.shape[1])


def of_layer(layer, own_ref, other_ref, *index):
    index = index or (Ellipsis,)
    own = lax.axis_index("section") == layer
    return jnp.where(own, own_ref[index], other_ref[index])


def pack(value, cols):
    rows, feats = value.shape
    if feats >= cols:
        return jnp.concatenate([value[:, i : i + cols] for i in range(0, feats, cols)], axis=0)
    share = rows * feats // cols
    return jnp.concatenate([value[i : i + share] for i in range(0, rows, share)], axis=1)


def unpack(value, rows, feats):
    cols = value.shape[1]
    if feats >= cols:
        return jnp.concatenate(
            [value[i : i + rows] for i in range(0, value.shape[0], rows)], axis=1
        )
    return jnp.concatenate([value[:, i : i + feats] for i in range(0, cols, feats)], axis=0)


def share_body(n, up_ref, down_ref, wq_own, wq_other, rows_ref, *refs):
    outs, own_ref, sems = refs[:n], refs[n], refs[n + 1]
    s, m = lax.axis_index("section"), lax.axis_index("mp")
    place = s * lax.axis_size("dp") + lax.axis_index("dp")
    parts = 2 * lax.axis_size("dp")
    tall = up_ref.shape[0] // parts
    share = wq_own.shape[0] // (n * parts)
    rows = pl.ds(pl.multiple_of(place * tall, 16), tall)
    cols = pl.ds(pl.multiple_of(place * HEAD, HEAD), HEAD)
    copies = [pltpu.make_async_copy(up_ref.at[rows], outs[0].at[pl.ds(0, tall)], sems.at[0])]
    for side in range(2):
        copies.append(
            pltpu.make_async_copy(
                down_ref.at[pl.ds(side * tall, tall), cols],
                outs[0].at[pl.ds(tall, tall), pl.ds(side * HEAD, HEAD)],
                sems.at[1 + side],
            )
        )
    for copy in copies:
        copy.start()
    for i, d in enumerate(places(n)):
        start = ((m ^ d) * parts + place) * share
        here = pl.ds(pl.multiple_of(start, share), share)
        target = outs[i].at[pl.ds(2 * tall, share)]
        copies.append(pltpu.make_async_copy(wq_own.at[here], target, sems.at[3 + i]))

        @pl.when(s == 1)
        def _(here=here, target=target, i=i):
            pltpu.make_async_copy(wq_own.at[here], target, sems.at[3 + i]).start()

        @pl.when(s != 1)
        def _(here=here, target=target, i=i):
            pltpu.make_async_copy(wq_other.at[here], target, sems.at[3 + i]).start()

    total, length = rows_ref.shape[1], own_ref.shape[1]
    for i in range(own_ref.shape[0] // total):
        source = rows_ref.at[s, :, pl.ds(i * length, length)]
        target = own_ref.at[pl.ds(i * total, total)]
        copies.append(pltpu.make_async_copy(source, target, sems.at[3 + n + i]))
        copies[-1].start()
    for copy in copies:
        copy.wait()
    half = own_ref.shape[0] // 2
    outs[n - 1][2 * tall + share :, :] = own_ref[:half, :]
    for i in range(1, n):
        outs[i][: 2 * tall, :] = outs[0][: 2 * tall, :]


def line_body(n, tall, *refs):
    half = (refs[0].shape[0] - 2 * tall) // 2
    own_ref, far_ref = refs[n], refs[n + 1]
    near_ref, message, inner_ref = refs[n + 4 :]
    size = own_ref.shape[0]
    inner_ref[:size, :] = own_ref[...]
    inner_ref[size:, :] = refs[n - 1][2 * (tall + half) :, :]
    near_ref[...] = refs[n - 1][2 * (tall + half) :, :]
    rest = own_ref.shape[0] // 2
    message[:rest, :] = own_ref[rest:, :]
    message[rest:-PAD, :] = far_ref[...]
    message[-PAD:, :] = jnp.zeros((PAD, message.shape[1]), BF16)
    for i in range(1, n):
        for j in range(2):
            start = 2 * tall + j * half
            refs[n + 2 + j][i - 1, :tall] = refs[i][j * tall : (j + 1) * tall, :]
            refs[n + 2 + j][i - 1, tall:] = refs[i][start : start + half, :]


def pair_body(up, up1, down, down2, near1, moved, far2, far3, ups, downs, message, near):
    for here, there, out_ref in ((up, up1, ups), (down, down2, downs)):
        out_ref[0] = here[...]
        out_ref[1] = there[...]
    rest, rows = near1.shape[0], far2.shape[0]
    near[:rest, :] = near1[...]
    near[rest:, :] = moved[:rest, :]
    message[:rest, :] = moved[:rest, :]
    for i, far in enumerate((far3, far2)):
        start = rest + i * rows
        total = moved[start : start + rows, :].astype(F32) + far[...].astype(F32)
        message[start : start + rows, :] = total.astype(BF16)


def gather_body(
    up, up1, up2, down, down2, down1, moved, close, key_ref, value_ref,
    out_ref, message, weight_ref,
):
    tall = key_ref.shape[0]
    weight_ref[:tall, :] = key_ref[...]
    weight_ref[tall:, :] = value_ref[...]
    for base, parts in ((0, (up, up1, up2)), (4, (down, down2, down1))):
        near = 1 if base == 0 else 2
        out_ref[base] = parts[0][...]
        out_ref[base + near] = parts[1][...]
        out_ref[base + 3 - near] = parts[2][0]
        out_ref[base + 3] = parts[2][1]
    rows = close.shape[0]
    rest = message.shape[0] - rows
    message[:rest, :] = moved[:rest, :]
    total = moved[rest + rows :, :].astype(F32) + close[...].astype(F32)
    message[rest:, :] = total.astype(BF16)


def rows_body(cols, rows_ref, own_ref):
    own_ref[...] = pack(rows_ref[lax.axis_index("section")], cols)


def query_shares_body(n, wq_own, wq_other, *outs):
    m = lax.axis_index("mp")
    tall = outs[0].shape[0]
    for i, d in enumerate(places(n)):
        here = pl.ds(pl.multiple_of((m ^ d) * tall, tall), tall)
        outs[i][...] = of_layer(1, wq_own, wq_other, here, slice(None))


def out_grads_body(n, og_ref, wout_own, wout_other, *outs):
    s, m = lax.axis_index("section"), lax.axis_index("mp")
    cols = outs[0].shape[1]
    rows = og_ref.shape[1]
    for i, d in enumerate(places(n)):
        here = pl.ds(pl.multiple_of((m ^ d) * cols, cols), cols)
        weight = of_layer(1, wout_own, wout_other, here, slice(None))
        outs[i][...] = mm(og_ref[s], weight, NTR).astype(BF16)
    for i, out_ref in enumerate(outs[1:3]):
        if len(outs) > n:
            outs[n][i * rows : (i + 1) * rows, :] = out_ref[...]


def add_body(count, *refs):
    for i in range(count):
        total = refs[i][...].astype(F32) + refs[count + i][...].astype(F32)
        refs[2 * count + i][...] = total.astype(BF16)


def pieces_body(kept_ref, other_ref, *outs):
    start = 0
    for out_ref in outs:
        here = slice(start, start + out_ref.shape[0])
        start += out_ref.shape[0]
        total = kept_ref[here, :].astype(F32) + other_ref[here, :].astype(F32)
        out_ref[...] = total.astype(BF16)


def norm_body(pool_ref, gain_ref, out_ref):
    wide = pool_ref[...].astype(F32)
    scale = lax.rsqrt(jnp.mean(wide * wide, axis=-1, keepdims=True) + EPSILON)
    out_ref[...] = (wide * scale * gain_ref[...]).astype(BF16)


def encoder_body(n, parts, gathered, *refs):
    pool_ref, normed_ref = refs[:2]
    if gathered:
        pieces, (enc_ref, hidden, up, down, *sems) = refs[2:4], refs[4:]
    else:
        pieces, (enc_ref, wq_ref, hidden, up, down) = refs[2:4], refs[8:]
        up_ref, down_ref, wq_own, wq_other = refs[4:8]
    m = lax.axis_index("mp")
    if gathered:
        copies = [[pltpu.make_async_copy(pieces[i], (up, down)[i], sems[0].at[i])] for i in range(2)]
        downs = copies[1]
        ups = copies[:1] + [[]] * (n - 1)
        ups[0][0].start()
        downs[0].start()
    else:
        s, g = lax.axis_index("section"), lax.axis_index("dp")
        dp, tall, wide = parts // 2, up.shape[2], HEAD
        share = pieces[0].shape[2] - tall
        ups, downs = [[] for _ in range(n)], []
        up[m] = up_ref[...].reshape(up.shape[1:])
        down[m] = down_ref[...]
        here = pl.ds(pl.multiple_of(m * wq_ref.shape[1], wq_ref.shape[1]), wq_ref.shape[1])
        wq_ref[0] = of_layer(1, wq_own, wq_other, here, slice(None))
        for j, dz in enumerate(places(n)[1:]):
            for i in range(parts):
                half, dg = divmod(i, dp)
                place = (s ^ half) * dp + (g ^ dg)
                for k in range(2):
                    start = pl.multiple_of((2 * place + k) * share, share)
                    wq_ref[j + 1, pl.ds(start, share)] = pieces[half][k * dp + dg, j, tall:]
                up[m ^ dz, place] = pieces[half][dg, j, :tall]
                where = pl.ds(pl.multiple_of(place * wide, wide), wide)
                for side in range(2):
                    rows_of = slice(side * tall, (side + 1) * tall)
                    down[m ^ dz, rows_of, where] = pieces[half][
                        dp + dg, j, :tall, side * wide : (side + 1) * wide
                    ]
    rows, width = normed_ref.shape
    cols = up.shape[-1]
    chunk = rows // 4
    for dz in range(n):
        for copy in ups[dz]:
            copy.wait()
        k = dz if gathered else m ^ dz
        there = pl.ds(pl.multiple_of(k * cols, cols), cols)
        weight = up[k].reshape(width, cols)
        for r in range(0, rows, chunk):
            product = mm(normed_ref[r : r + chunk, :], weight)
            hidden[r : r + chunk, there] = jax.nn.gelu(product).astype(BF16)
    for copy in downs:
        copy.wait()
    for r in range(0, rows, chunk):
        weight = down[...].reshape(width, hidden.shape[1])
        enc = pool_ref[r : r + chunk, :].astype(F32) + mm(hidden[r : r + chunk, :], weight, NTR)
        enc_ref[r : r + chunk, :] = enc.astype(BF16)


def projected_body(layer, enc_ref, wkv_own, wkv_other, out_ref):
    count, length, total = out_ref.shape
    cols, width = wkv_own.shape[1], wkv_own.shape[0] // 2
    enc = enc_ref[...]
    start = total - 2 * cols
    if start:
        out_ref[:, :, :start] = enc.reshape(count, length, width)
    for kind in range(2):
        weight = of_layer(layer, wkv_own, wkv_other, slice(kind * width, (kind + 1) * width))
        out = mm(enc, weight).astype(BF16).reshape(count, length, cols)
        out_ref[:, :, start + kind * cols : start + (kind + 1) * cols] = out


def slot_slice(c, slots):
    return slice(c * slots * NT, (c + 1) * slots * NT)


def softmax_used(scores, used):
    lane = lax.broadcasted_iota(jnp.int32, scores.shape, scores.ndim - 1)
    scores = jnp.where(lane < used * NT, scores, -1e30)
    powers = jnp.exp(scores - jnp.max(scores, axis=-1, keepdims=True))
    return powers / jnp.sum(powers, axis=-1, keepdims=True)


def query_body(n, gain_own, gain_other, wq_own, wq_other, *refs):
    pieces, query_ref = refs[:-1], refs[-1]
    m = lax.axis_index("mp")
    rows, cols = query_ref.shape
    feats = gain_own.shape[-1]

    def piece(k):
        if len(pieces) == n or k < 2:
            return unpack(pieces[k][...], rows, feats).astype(F32)
        far_inner, next_outer, late_inner, late_outer = (ref[...] for ref in pieces[2:])
        size = rows * feats // cols
        rest = size // 2
        inner = jnp.logical_or(m == 1, m == 2)
        if k == 2:
            inside = jnp.concatenate([far_inner[size:], late_inner[:rest]], axis=0)
            value = jnp.where(inner, inside, next_outer[:size])
        else:
            outside = jnp.concatenate([next_outer[size:], late_outer[:rest]], axis=0)
            value = jnp.where(inner, far_inner[:size], outside)
        return unpack(value, rows, feats).astype(F32)

    total = jnp.zeros((rows, 1), F32)
    for k in range(n):
        wide = piece(k)
        total = total + jnp.sum(wide * wide, axis=-1, keepdims=True)
    scale = lax.rsqrt(total / (n * feats) + EPSILON)
    raw = jnp.zeros((rows, cols), F32)
    for k in range(n):
        gain = of_layer(0, gain_own, gain_other, m ^ k)
        normed = (piece(k) * scale * gain).astype(BF16)
        here = pl.ds(pl.multiple_of((m ^ k) * feats, feats), feats)
        raw = raw + mm(normed, of_layer(0, wq_own, wq_other, here, slice(None)))
    query_ref[...] = (raw * SCALE).astype(BF16)


def scores_of(tracts, slots, heads, query_ref, counts_ref, blocks, probs_ref):
    s = lax.axis_index("section")
    length = query_ref.shape[0] // tracts
    for c in range(tracts):
        here, span = slice(c * length, (c + 1) * length), slot_slice(c, slots)
        for h in range(heads):
            there = slice(h * HEAD, (h + 1) * HEAD)
            probs_ref[c * heads + h] = mm(query_ref[here, there], blocks[span, there], NTR)
    for c in range(tracts):
        both = slice(c * heads, (c + 1) * heads)
        probs_ref[both] = softmax_used(probs_ref[both], counts_ref[s, c])


def first_layer_body(
    tracts, slots, ids_ref, counts_ref, query_ref, own, other, att_ref, probs_ref, blocks
):
    fill_slots(own, other, ids_ref, tracts, slots, blocks)
    rows, cols = query_ref.shape
    heads, length = cols // HEAD, rows // tracts
    scores_of(tracts, slots, heads, query_ref, counts_ref, blocks, probs_ref)
    for c in range(tracts):
        here, span = slice(c * length, (c + 1) * length), slot_slice(c, slots)
        for h in range(heads):
            there = slice(h * HEAD, (h + 1) * HEAD)
            beyond = slice(cols + h * HEAD, cols + (h + 1) * HEAD)
            probs = probs_ref[c * heads + h].astype(BF16)
            att_ref[here, there] = mm(probs, blocks[span, beyond]).astype(BF16)


def between_body(n, *refs):
    gain_own, gain_other, own_ref, wout_own, wout_other, wq_ref = refs[:6]
    pieces = refs[6 : 6 + n]
    rows_ref, messages = refs[6 + n], refs[7 + n :]
    m = lax.axis_index("mp")
    rows, cols = pieces[0].shape
    feats = rows_ref.shape[1]
    wide = unpack(own_ref[...], rows, feats).astype(F32)
    for i, d in enumerate(places(n)):
        here = pl.ds(pl.multiple_of((m ^ d) * cols, cols), cols)
        wide = wide + mm(pieces[i][...], of_layer(0, wout_own, wout_other, here, slice(None)))
    rounded = wide.astype(BF16)
    rows_ref[...] = rounded
    wide = rounded.astype(F32)
    square = to_row(jnp.sum(wide * wide, axis=-1, keepdims=True))
    high = square.astype(BF16).astype(F32)
    index = lax.broadcasted_iota(jnp.int32, (PAD, rows), 0)
    extra = jnp.where(index == 0, high, jnp.where(index == 1, square - high, 0.0)).astype(BF16)
    gained = (wide * of_layer(1, gain_own, gain_other, m)).astype(BF16)
    for i in range(n):
        messages[i][:rows, :] = mm(gained, wq_ref[i]).astype(BF16)
        messages[i][rows:, :] = extra


def prob_grads(tracts, slots, heads, att_ref, blocks, grads_ref):
    rows, cols = att_ref.shape
    length = rows // tracts
    for c in range(tracts):
        here, span = slice(c * length, (c + 1) * length), slot_slice(c, slots)
        for h in range(heads):
            there = slice(h * HEAD, (h + 1) * HEAD)
            beyond = slice(cols + h * HEAD, cols + (h + 1) * HEAD)
            grads_ref[c * heads + h] = mm(att_ref[here, there], blocks[span, beyond], NTR)


def score_grads(tracts, heads, probs_ref, grads_ref, scores_ref, soft_ref):
    for c in range(tracts):
        both = slice(c * heads, (c + 1) * heads)
        probs, grads = probs_ref[both], grads_ref[both]
        inner = jnp.sum(probs * grads, axis=-1, keepdims=True)
        scores_ref[both] = (probs * (grads - inner)).astype(BF16)
        soft_ref[both] = probs.astype(BF16)


def slot_grads(tracts, slots, heads, cols, query_ref, att_ref, scores_ref, soft_ref, dkv_ref):
    length = att_ref.shape[0] // tracts
    for c in range(tracts):
        here, span = slice(c * length, (c + 1) * length), slot_slice(c, slots)
        for h in range(heads):
            there = slice(h * HEAD, (h + 1) * HEAD)
            beyond = slice(cols + h * HEAD, cols + (h + 1) * HEAD)
            dkv_ref[span, there] = mm(
                scores_ref[c * heads + h], query_ref[here, there], TNR
            ).astype(BF16)
            dkv_ref[span, beyond] = mm(
                soft_ref[c * heads + h], att_ref[here, there], TNR
            ).astype(BF16)


def last_values_body(tracts, slots, ids_ref, *refs):
    grads, (own, other, blocks, att_ref, grads_ref) = refs[:-5], refs[-5:]
    fill_slots(own, other, ids_ref, tracts, slots, blocks, own.shape[2] - blocks.shape[1])
    rows, cols = att_ref.shape
    grad = jnp.zeros((rows, cols), F32)
    for part in grads:
        start = grads[1].shape[0] - 2 * rows if part.shape[0] > rows else 0
        grad = grad + part[start : start + rows, :].astype(F32)
    att_ref[...] = grad.astype(BF16)
    prob_grads(tracts, slots, cols // HEAD, att_ref, blocks, grads_ref)


def last_layer_body(n, width, tracts, slots, counts_ref, *refs):
    messages, (blocks, grads_ref) = refs[:n], refs[n : n + 2]
    out_ref, scale_ref, query_ref, scores_ref, soft_ref, raw_ref, probs_ref = refs[n + 2 :]
    rows, cols = raw_ref.shape
    raw = jnp.zeros((rows, cols), F32)
    square = jnp.zeros((1, rows), F32)
    for d in range(n):
        raw = raw + messages[d][:rows, :].astype(F32)
        extra = messages[d][rows:, :].astype(F32)
        square = square + extra[0:1, :] + extra[1:2, :]
    scale = lax.rsqrt(to_column(square) / width + EPSILON)
    scale_ref[...] = jnp.broadcast_to(scale, scale_ref.shape)
    raw = raw * scale
    raw_ref[...] = raw
    query_ref[...] = (raw * SCALE).astype(BF16)
    length = rows // tracts
    heads = cols // HEAD
    scores_of(tracts, slots, heads, query_ref, counts_ref, blocks, probs_ref)
    score_grads(tracts, heads, probs_ref, grads_ref, scores_ref, soft_ref)
    for c in range(tracts):
        here, span = slice(c * length, (c + 1) * length), slot_slice(c, slots)
        for h in range(heads):
            there = slice(h * HEAD, (h + 1) * HEAD)
            grad_query = mm(scores_ref[c * heads + h], blocks[span, there]) * SCALE
            out_ref[here, there] = grad_query.astype(BF16)
    part = jnp.sum(out_ref[:rows, :].astype(F32) * raw_ref[...], axis=-1, keepdims=True)
    index = lax.broadcasted_iota(jnp.int32, (PAD, rows), 0)
    out_ref[rows:, :] = jnp.where(index == 0, to_row(part), 0.0).astype(BF16)


def last_slots_body(tracts, slots, query_ref, att_ref, scores_ref, soft_ref, dkv_ref):
    cols = query_ref.shape[1]
    slot_grads(
        tracts, slots, cols // HEAD, cols, query_ref, att_ref, scores_ref, soft_ref, dkv_ref
    )


def weight_grads(enc_ref, dkv_ref, kept_ref, sent_ref):
    cols = kept_ref.shape[1]
    first = lax.axis_index("section") == 0
    chunk = enc_ref.shape[0] // 2
    for r in range(0, enc_ref.shape[0], chunk):
        total = mm(enc_ref[r : r + chunk, :], dkv_ref[...])
        keys, values = total[:, :cols], total[:, cols:]
        kept_ref[r : r + chunk, :] = jnp.where(first, keys, values).astype(BF16)
        sent_ref[r : r + chunk, :] = jnp.where(first, values, keys).astype(BF16)


def part_grads_body(keep, enc_ref, dkv_ref, out_ref):
    cols = out_ref.shape[1]
    kind = lax.axis_index("section") if keep else 1 - lax.axis_index("section")
    here = pl.ds(pl.multiple_of(kind * cols, cols), cols)
    out_ref[...] = mm(enc_ref[...], dkv_ref[:, here]).astype(BF16)


def last_grads_body(
    tracts, slots, ids_ref, dkv_ref, own, other, enc_ref, kept_ref, sent_ref
):
    for c in range(tracts):
        for k in range(slots):
            here = slice((c * slots + k) * NT, (c * slots + k + 1) * NT)
            enc_ref[:, here] = slot_value(own, other, ids_ref, c, k, 0, enc_ref.shape[0]).T
    weight_grads(enc_ref, dkv_ref, kept_ref, sent_ref)


def back_between_body(n, width, *refs):
    gain_own, gain_other, rows_ref, og_ref, scale_ref, wq_ref = refs[:6]
    wout_own, wout_other = refs[6:8]
    pieces, messages = refs[8 : 8 + n], refs[8 + n :]
    s, m = lax.axis_index("section"), lax.axis_index("mp")
    rows, feats = rows_ref.shape
    cols = pieces[0].shape[1]
    normed = jnp.zeros((rows, feats), F32)
    total = jnp.zeros((1, rows), F32)
    for d in range(n):
        normed = normed + mm(pieces[d][:rows, :], wq_ref[d], NTR)
        total = total + pieces[d][rows:, :].astype(F32)[0:1, :]
    scale = scale_ref[:, 0:1]
    wide = rows_ref[...].astype(F32)
    gain = of_layer(1, gain_own, gain_other, m)
    grad = og_ref[s].astype(F32) + scale * gain * normed
    grad = grad - wide * (scale * scale * (to_column(total) / width))
    grad = grad.astype(BF16)
    for i, d in enumerate(places(n)):
        here = pl.ds(pl.multiple_of((m ^ d) * cols, cols), cols)
        weight = of_layer(0, wout_own, wout_other, here, slice(None))
        messages[i][...] = mm(grad, weight, NTR).astype(BF16)


def first_back_body(n, tracts, slots, query_ref, probs_ref, blocks, *refs):
    grads, (dkv_ref, att_ref, grads_ref, scores_ref, soft_ref) = refs[:n], refs[n:]
    rows, cols = query_ref.shape
    grad = jnp.zeros((rows, cols), F32)
    for d in range(n):
        grad = grad + grads[d][...].astype(F32)
    att_ref[...] = grad.astype(BF16)
    heads = cols // HEAD
    prob_grads(tracts, slots, heads, att_ref, blocks, grads_ref)
    score_grads(tracts, heads, probs_ref, grads_ref, scores_ref, soft_ref)
    slot_grads(tracts, slots, heads, cols, query_ref, att_ref, scores_ref, soft_ref, dkv_ref)


def along_mp(value, n):
    return [value] + [xor_move(value, "mp", d) for d in places(n)[1:]]


def scattered(messages):
    order = places(len(messages))
    return [messages[0]] + [xor_move(messages[i], "mp", order[i]) for i in range(1, len(messages))]


def on_device(
    segment_input,
    out_grad,
    pool_tokens,
    neighbour_ids,
    neighbour_counts,
    enc_gain,
    enc_up,
    enc_down,
    norm_gain,
    w_query,
    w_key,
    w_value,
    w_out,
):
    n, dp = lax.axis_size("mp"), lax.axis_size("dp")
    s = lax.axis_index("section")
    _, _, rows, feats = segment_input.shape
    width = n * feats
    cols = w_query.shape[2]
    half, _, length, enc_width = pool_tokens.shape
    tracts, slots = neighbour_ids.shape[2:]
    ids, counts = neighbour_ids[:, 0], neighbour_counts[:, 0]
    ff = enc_down.shape[0]
    first = s == 0
    gain = norm_gain.reshape(n, 1, feats)
    wq, wk, wv, wout = w_query[0], w_key[0], w_value[0], w_out[0]
    gains, wqs, wouts = ((w, swap(w)) for w in (gain, wq, wout))

    pool_rows = pool_tokens[:, 0].reshape(half * length, enc_width)
    normed = call(
        norm_body, [shape((half * length, enc_width))], [vm(), vm()], flops=half * length * enc_width
    )(pool_rows, enc_gain[None, :])[0]
    down_t = enc_down.T
    parts = 2 * dp
    up_rows, down_cols = enc_width // parts, ff // parts
    shares = up_rows % 16 == 0 and enc_width // n == 2 * up_rows and down_cols == HEAD
    shares = shares and enc_up.shape[1] == 2 * down_cols and dp == 4 and n == 4
    shares = shares and feats % (32 * parts) == 0 and cols == enc_up.shape[1]
    if shares:
        own_shape = shape((rows * feats // cols, cols))
        messages = [shape((2 * up_rows + feats // parts, 2 * down_cols))] * (n - 1)
        rest = own_shape.shape[0] // 2
        longer = shape((messages[0].shape[0] + rest, cols))
        *messages, own = call(
            functools.partial(share_body, n),
            messages + [longer, own_shape],
            [hbm()] * 5,
            [pltpu.SemaphoreType.DMA((3 + n + feats // cols,))],
            limit=FIRST_LIMIT,
        )(enc_up, down_t, *wqs, segment_input[:, 0])
        line = scattered(messages)
        *grads, far_grads = call(
            functools.partial(out_grads_body, n),
            [shape((rows, cols))] * n + [shape((2 * rows, cols))],
            [vm()] * 3,
            flops=2 * rows * width * cols,
        )(out_grad[:, 0], *wouts)
        piece = (n - 1, up_rows + feats // (2 * parts), 2 * down_cols)
        up, down, near, message, inner_rows = call(
            functools.partial(line_body, n, up_rows),
            [shape(piece)] * 2
            + [shape((rest + size, cols)) for size in (0, 2 * rows + PAD, own_shape.shape[0])],
            [vm()] * (n + 2),
            deps=[gains[1]],
        )(*line, own, far_grads)
        inner, outer = [(1, 2), (2, 1)], [(1, 0), (2, 3)]
        up1, down2 = xor_move(up, "dp", 1), xor_move(down, "dp", 2)
        far_inner = lax.ppermute(inner_rows, "mp", inner)
        message = xor_move(message, "mp", 1)
        ups, downs, message, near = call(
            pair_body,
            [shape((2,) + piece)] * 2 + [shape((rest + 2 * rows, cols)), own_shape],
            [vm()] * 8,
            deps=[far_inner],
        )(up, up1, down, down2, near, message, grads[1], grads[2])
        up2, down1 = xor_move(ups, "dp", 2), xor_move(downs, "dp", 1)
        next_outer = lax.ppermute(far_inner, "mp", outer)
        message = lax.ppermute(message, "mp", inner)
        gathered, close, wkv = call(
            gather_body,
            [shape((parts,) + piece), shape((rest + rows, cols)), shape((2 * enc_width, cols))],
            [vm()] * 10,
            deps=[next_outer, normed],
        )(up, up1, up2, down, down2, down1, message, grads[3], wk, wv)
        pieces = [gathered, swap(gathered), enc_up, down_t, *wqs]
        close = xor_move(close, "mp", 1)
        grad_parts = [grads[0], message, close]
        row_pieces = [own, near, far_inner, next_outer, message, close]
        before_projected = [close]
        scratch = [
            pltpu.VMEM((n, parts, up_rows, enc_up.shape[1]), BF16),
            pltpu.VMEM((n, enc_width // n, ff), BF16),
        ]
    else:
        own = call(
            functools.partial(rows_body, cols), [shape((rows * feats // cols, cols))], [vm()]
        )(segment_input[:, 0])[0]
        grad_parts = call(
            functools.partial(out_grads_body, n),
            [shape((rows, cols))] * n,
            [vm()] * 3,
            flops=2 * rows * width * cols,
        )(out_grad[:, 0], *wouts)
        row_pieces, grad_parts = along_mp(own, n), scattered(list(grad_parts))
        query_shares = call(
            functools.partial(query_shares_body, n), [shape((feats, cols))] * n, [vm()] * 2
        )(*wqs)
        projection = jnp.stack(scattered(query_shares))
        wkv = jnp.concatenate([wk, wv], axis=0)
        before_projected = []
        pieces = [
            lax.all_gather(enc_up, "mp", axis=0),
            lax.all_gather(down_t, "mp", axis=0, tiled=True),
        ]
        scratch = [
            pltpu.VMEM((n, enc_width, enc_up.shape[1]), BF16),
            pltpu.VMEM((enc_width, ff), BF16),
            pltpu.SemaphoreType.DMA((2,)),
        ]

    wkvs = (wkv, swap(wkv))

    encoded = call(
        functools.partial(encoder_body, n, parts, not shares),
        [shape((half * length, enc_width))] + [shape((n, feats, cols))] * shares,
        [vm()] * 8 if shares else [vm()] * 2 + [hbm()] * 2,
        [pltpu.VMEM((half * length, ff), BF16)] + scratch,
        flops=4 * half * length * enc_width * ff,
        limit=ENCODER_LIMIT if shares else 48 * 1024 * 1024,
    )(pool_rows, normed, *pieces)
    enc = encoded[0]
    if shares:
        projection = encoded[1]
    pool0_own, enc_own = (
        call(
            functools.partial(projected_body, layer),
            [shape((half, length, layer * enc_width + 2 * cols))],
            [vm()] * 3,
            flops=4 * half * length * enc_width * cols,
            deps=before_projected,
        )(enc, *wkvs)[0]
        for layer in (0, 1)
    )
    pool0_other = swap(pool0_own)
    heads = cols // HEAD
    chunk = rows // tracts
    slot_rows = tracts * slots * NT
    wide_scores = pltpu.VMEM((tracts * heads, chunk, slots * NT), F32)
    bf_scores = pltpu.VMEM((tracts * heads, chunk, slots * NT), BF16)
    attention_flops = 2 * rows * slots * NT * cols

    wide_shape = shape((tracts * heads, chunk, slots * NT), F32)
    block_shape = shape((slot_rows, 2 * cols))
    query0 = call(
        functools.partial(query_body, n),
        [shape((rows, cols))],
        [vm()] * (4 + len(row_pieces)),
        flops=2 * rows * width * cols,
        deps=[pool0_own],
    )(*gains, *wqs, *row_pieces)[0]
    att, probs0, blocks0, enc_own = call(
        functools.partial(first_layer_body, tracts, slots),
        [shape((rows, cols)), wide_shape, block_shape],
        [smem(), smem()] + [vm()] * 3,
        flops=2 * attention_flops,
        passing=[enc_own],
    )(ids, counts, query0, pool0_own, pool0_other)
    enc_other = swap(enc_own)
    att_pieces = along_mp(att, n)
    rows1, *messages = call(
        functools.partial(between_body, n),
        [shape((rows, feats))] + [shape((rows + PAD, cols))] * n,
        [vm()] * (6 + n),
        flops=4 * rows * feats * n * cols,
        deps=[enc_other],
    )(*gains, own, *wouts, projection, *att_pieces)
    query_pieces = scattered(messages)
    bf_shape = shape((tracts * heads, chunk, slots * NT))
    blocks1, att1, prob_grads1 = call(
        functools.partial(last_values_body, tracts, slots),
        [block_shape, shape((rows, cols)), wide_shape],
        [smem()] + [vm()] * (len(grad_parts) + 2),
        flops=attention_flops,
    )(ids, *grad_parts, enc_own, enc_other)
    grad_query, scale1, query1, *soft1 = call(
        functools.partial(last_layer_body, n, width, tracts, slots),
        [shape((rows + PAD, cols)), shape((rows, HEAD), F32), shape((rows, cols))] + [bf_shape] * 2,
        [smem()] + [vm()] * (n + 2),
        [pltpu.VMEM((rows, cols), F32), wide_scores],
        flops=3 * attention_flops,
    )(counts, *query_pieces, blocks1, prob_grads1)
    dkv1 = call(
        functools.partial(last_slots_body, tracts, slots),
        [shape((slot_rows, 2 * cols))],
        [vm()] * 4,
        flops=2 * attention_flops,
    )(query1, att1, *soft1)[0]
    query_grads = along_mp(grad_query, n)
    enc_slots, kept1, sent1 = call(
        functools.partial(last_grads_body, tracts, slots),
        [shape((enc_width, slot_rows)), shape((enc_width, cols)), shape((enc_width, cols))],
        [smem(), vm(), vm(), vm()],
        flops=4 * enc_width * slot_rows * cols,
    )(ids, dkv1, enc_own, enc_other)
    *messages, kept1, sent1 = call(
        functools.partial(back_between_body, n, width),
        [shape((rows, cols))] * n,
        [vm()] * (8 + n),
        flops=4 * rows * feats * n * cols,
        passing=[kept1, sent1],
    )(*gains, rows1, out_grad[:, 0], scale1, projection, *wouts, *query_grads)
    grad_pieces0 = scattered(messages)

    def over_dp(parts, order):
        size = len(parts)
        moved = [None] * size
        for by in sorted(set(order)):
            members = [i for i in range(size) if order[i] == by]
            if len(members) == 1:
                moved[members[0]] = xor_move(parts[members[0]], "dp", by)
                continue
            message = xor_move(jnp.concatenate([parts[i] for i in members], axis=0), "dp", by)
            start = 0
            for i in members:
                moved[i] = lax.slice_in_dim(message, start, start + parts[i].shape[0])
                start += parts[i].shape[0]
        shapes = [shape(part.shape) for part in parts]
        return call(functools.partial(add_body, size), shapes, [vm()] * (2 * size))(*parts, *moved)

    def pieces_of(kept, sent, sizes):
        parts = [shape((size, cols)) for size in sizes]
        return call(pieces_body, parts, [vm()] * 2)(kept, swap(sent))

    size = enc_width // 2
    early = size // 2 + 16 if size % 32 == 0 else size // 2
    ax, bx, ay, by = pieces_of(kept1, sent1, [early, size - early] * 2)
    if dp == 4:
        ax, ay = over_dp([ax, ay], (1, 2))
    dkv0 = call(
        functools.partial(first_back_body, n, tracts, slots),
        [shape((slot_rows, 2 * cols))],
        [vm()] * (n + 3),
        [pltpu.VMEM((rows, cols), BF16), wide_scores, bf_scores, bf_scores],
        flops=3 * attention_flops,
    )(query0, probs0, blocks0, *grad_pieces0)[0]
    sent0, kept0 = (
        call(
            functools.partial(part_grads_body, keep),
            [shape((enc_width, cols))],
            [vm()] * 2,
            flops=2 * enc_width * slot_rows * cols,
            deps=[] if keep else [ax, ay],
        )(enc_slots, dkv0)[0]
        for keep in (False, True)
    )
    top, bottom = pieces_of(kept0, sent0, [size] * 2)
    if dp == 4:
        top, bottom, ax, ay, bx, by = over_dp([top, bottom, ax, ay, bx, by], (1, 2, 2, 1, 1, 2))
        top, bottom, bx, by = over_dp([top, bottom, bx, by], (2, 1, 2, 1))
    else:
        top, bottom, ax, ay, bx, by = lax.psum((top, bottom, ax, ay, bx, by), "dp")
    sum0 = jnp.concatenate([top, bottom], axis=0)
    sum1 = jnp.concatenate([ax, bx, ay, by], axis=0)
    received = swap(jnp.where(first, sum1, sum0))
    key_total = jnp.where(first, sum0, received)
    value_total = jnp.where(first, received, sum1)
    return (key_total[None], value_total[None])


def solution(mesh):
    placed = (
        P(None, "dp", None, "mp"),
        P(None, "dp", None, "mp"),
        P("section", "dp", None, None),
        P(None, "dp", None, None),
        P(None, "dp", None),
        P(),
        P(None, "mp"),
        P(None, "mp"),
        P("section", None),
        P("section", None, "mp"),
        P("section", None, "mp"),
        P("section", None, "mp"),
        P("section", None, "mp"),
    )
    return jax.shard_map(
        on_device,
        mesh=mesh,
        in_specs=placed,
        out_specs=(P("section", None, "mp"), P("section", None, "mp")),
        check_vma=False,
    )
```

```python
import functools

import jax
import jax.numpy as jnp
from jax import lax
from jax.experimental import pallas as pl
from jax.experimental.pallas import tpu as pltpu
from jax.sharding import PartitionSpec as P

HEAD = 128
NT = 128
EPSILON = 1e-05
SCALE = HEAD ** (-0.5)
PAD = 16
VMEM_LIMIT = 20 * 1024 * 1024
ENCODER_LIMIT = 32 * 1024 * 1024
FIRST_LIMIT = 60 * 1024 * 1024

BF16 = jnp.bfloat16
F32 = jnp.float32
NN = (((1,), (0,)), ((), ()))
NTR = (((1,), (1,)), ((), ()))
TNR = (((0,), (0,)), ((), ()))


def mm(a, b, dims=NN):
    return lax.dot_general(a, b, dims, preferred_element_type=F32)


def xor_move(value, axis, by):
    count = lax.axis_size(axis)
    return lax.ppermute(value, axis, [(i, i ^ by) for i in range(count)])


def places(n):
    return (0, 2, 3, 1) if n == 4 else tuple(range(n))


def swap(value):
    return xor_move(value, "section", 1)


def vm():
    return pl.BlockSpec(memory_space=pltpu.VMEM)


def hbm():
    return pl.BlockSpec(memory_space=pl.ANY)


def hbm_only():
    return pl.BlockSpec(memory_space=pltpu.HBM)


def smem():
    return pl.BlockSpec(memory_space=pltpu.SMEM)


def call(body, outs, specs, scratch=(), flops=0, limit=VMEM_LIMIT, first=(), deps=(), passing=()):
    count, more, kept, results = len(specs), len(deps), len(passing), len(outs)
    nbytes = sum(o.size * o.dtype.itemsize for o in outs)
    begin = len(first)
    start = begin + count + more + kept

    def kernel(*refs):
        given = refs[begin : begin + count]
        body(*given, *refs[start : start + results], *refs[start + results + kept :])

    def run(*args):
        return pl.pallas_call(
            kernel,
            out_shape=list(outs) + [shape(x.shape, x.dtype) for x in passing],
            in_specs=[hbm()] * begin + list(specs) + [hbm()] * (more + kept),
            out_specs=[vm() for _ in outs] + [hbm()] * kept,
            scratch_shapes=list(scratch),
            input_output_aliases={begin + count + more + i: results + i for i in range(kept)},
            compiler_params=pltpu.CompilerParams(vmem_limit_bytes=limit),
            cost_estimate=pl.CostEstimate(
                flops=flops // 1000, bytes_accessed=nbytes // 1000, transcendentals=0
            ),
        )(*first, *args, *deps, *passing)

    return run


def shape(dims, dtype=BF16):
    return jax.ShapeDtypeStruct(dims, dtype)


def to_row(column):
    rows = column.shape[0]
    here = lax.broadcasted_iota(jnp.int32, (rows, rows), 0)
    there = lax.broadcasted_iota(jnp.int32, (rows, rows), 1)
    return jnp.sum(jnp.where(here == there, column, 0.0), axis=0, keepdims=True)


def to_column(row):
    rows = row.shape[1]
    here = lax.broadcasted_iota(jnp.int32, (rows, rows), 0)
    there = lax.broadcasted_iota(jnp.int32, (rows, rows), 1)
    return jnp.sum(jnp.where(here == there, row, 0.0), axis=1, keepdims=True)


def slot_value(own, other, ids_ref, tract, slot, start, size):
    half = own.shape[0]
    s = lax.axis_index("section")
    place = ids_ref[s, tract, slot]
    mine, theirs = place - s * half, place - (1 - s) * half
    here = jnp.logical_and(mine >= 0, mine < half)
    cols = slice(start, start + size)
    return jnp.where(
        here,
        own[jnp.clip(mine, 0, half - 1), :, cols],
        other[jnp.clip(theirs, 0, half - 1), :, cols],
    )


def fill_slots(own, other, ids_ref, tracts, slots, blocks, start=0):
    for c in range(tracts):
        for k in range(slots):
            here = slice((c * slots + k) * NT, (c * slots + k + 1) * NT)
            blocks[here, :] = slot_value(own, other, ids_ref, c, k, start, blocks.shape[1])


def of_layer(layer, own_ref, other_ref, *index):
    index = index or (Ellipsis,)
    own = lax.axis_index("section") == layer
    return jnp.where(own, own_ref[index], other_ref[index])


def pack(value, cols):
    rows, feats = value.shape
    if feats >= cols:
        return jnp.concatenate([value[:, i : i + cols] for i in range(0, feats, cols)], axis=0)
    share = rows * feats // cols
    return jnp.concatenate([value[i : i + share] for i in range(0, rows, share)], axis=1)


def unpack(value, rows, feats):
    cols = value.shape[1]
    if feats >= cols:
        return jnp.concatenate(
            [value[i : i + rows] for i in range(0, value.shape[0], rows)], axis=1
        )
    return jnp.concatenate([value[:, i : i + feats] for i in range(0, cols, feats)], axis=0)


def share_body(up_ref, down_ref, rows_ref, out_ref, own_ref):
    s = lax.axis_index("section")
    place = s * lax.axis_size("dp") + lax.axis_index("dp")
    tall = out_ref.shape[0] // 2
    cols = pl.ds(pl.multiple_of(place * HEAD, HEAD), HEAD)
    out_ref[:tall, :] = up_ref[pl.ds(pl.multiple_of(place * tall, 16), tall), :]
    for side in range(2):
        there = slice(side * HEAD, (side + 1) * HEAD)
        out_ref[tall:, there] = down_ref[side * tall : (side + 1) * tall, cols]
    own_ref[...] = pack(rows_ref[s], own_ref.shape[1])


def messages_body(n, share_ref, own_ref, wq_own, wq_other, *outs):
    s, m = lax.axis_index("section"), lax.axis_index("mp")
    place = s * lax.axis_size("dp") + lax.axis_index("dp")
    parts = 2 * lax.axis_size("dp")
    above = share_ref.shape[0]
    share = wq_own.shape[0] // (n * parts)
    for i, d in enumerate(places(n)):
        outs[i][:above, :] = share_ref[...]
        start = ((m ^ d) * parts + place) * share
        here = pl.ds(pl.multiple_of(start, share), share)
        outs[i][above : above + share, :] = of_layer(1, wq_own, wq_other, here, slice(None))
    half = own_ref.shape[0] // 2
    outs[n - 1][above + share :, :] = own_ref[:half, :]


def line_body(n, tall, *refs):
    half = (refs[0].shape[0] - 2 * tall) // 2
    own_ref, far_ref = refs[n], refs[n + 1]
    near_ref, message, inner_ref = refs[n + 4 :]
    size = own_ref.shape[0]
    inner_ref[:size, :] = own_ref[...]
    inner_ref[size:, :] = refs[n - 1][2 * (tall + half) :, :]
    near_ref[...] = refs[n - 1][2 * (tall + half) :, :]
    rest = own_ref.shape[0] // 2
    message[:rest, :] = own_ref[rest:, :]
    message[rest:-PAD, :] = far_ref[...]
    message[-PAD:, :] = jnp.zeros((PAD, message.shape[1]), BF16)
    for i in range(1, n):
        for j in range(2):
            start = 2 * tall + j * half
            refs[n + 2 + j][i - 1, :tall] = refs[i][j * tall : (j + 1) * tall, :]
            refs[n + 2 + j][i - 1, tall:] = refs[i][start : start + half, :]


def pair_body(up, up1, down, down2, near1, moved, far2, far3, ups, downs, message, near):
    for here, there, out_ref in ((up, up1, ups), (down, down2, downs)):
        out_ref[0] = here[...]
        out_ref[1] = there[...]
    rest, rows = near1.shape[0], far2.shape[0]
    near[:rest, :] = near1[...]
    near[rest:, :] = moved[:rest, :]
    message[:rest, :] = moved[:rest, :]
    for i, far in enumerate((far3, far2)):
        start = rest + i * rows
        total = moved[start : start + rows, :].astype(F32) + far[...].astype(F32)
        message[start : start + rows, :] = total.astype(BF16)


def gather_body(
    up, up1, up2, down, down2, down1, moved, close, key_ref, value_ref,
    out_ref, message, weight_ref,
):
    tall = key_ref.shape[0]
    weight_ref[:tall, :] = key_ref[...]
    weight_ref[tall:, :] = value_ref[...]
    for base, parts in ((0, (up, up1, up2)), (4, (down, down2, down1))):
        near = 1 if base == 0 else 2
        out_ref[base] = parts[0][...]
        out_ref[base + near] = parts[1][...]
        out_ref[base + 3 - near] = parts[2][0]
        out_ref[base + 3] = parts[2][1]
    rows = close.shape[0]
    rest = message.shape[0] - rows
    message[:rest, :] = moved[:rest, :]
    total = moved[rest + rows :, :].astype(F32) + close[...].astype(F32)
    message[rest:, :] = total.astype(BF16)


def rows_body(cols, rows_ref, own_ref):
    own_ref[...] = pack(rows_ref[lax.axis_index("section")], cols)


def query_shares_body(n, wq_own, wq_other, *outs):
    m = lax.axis_index("mp")
    tall = outs[0].shape[0]
    for i, d in enumerate(places(n)):
        here = pl.ds(pl.multiple_of((m ^ d) * tall, tall), tall)
        outs[i][...] = of_layer(1, wq_own, wq_other, here, slice(None))


def out_grads_body(n, og_ref, wout_own, wout_other, *outs):
    s, m = lax.axis_index("section"), lax.axis_index("mp")
    cols = outs[0].shape[1]
    rows = og_ref.shape[1]
    for i, d in enumerate(places(n)):
        here = pl.ds(pl.multiple_of((m ^ d) * cols, cols), cols)
        weight = of_layer(1, wout_own, wout_other, here, slice(None))
        outs[i][...] = mm(og_ref[s], weight, NTR).astype(BF16)
    for i, out_ref in enumerate(outs[1:3]):
        if len(outs) > n:
            outs[n][i * rows : (i + 1) * rows, :] = out_ref[...]


def add_body(count, *refs):
    for i in range(count):
        total = refs[i][...].astype(F32) + refs[count + i][...].astype(F32)
        refs[2 * count + i][...] = total.astype(BF16)


def pieces_body(kept_ref, other_ref, *outs):
    start = 0
    for out_ref in outs:
        here = slice(start, start + out_ref.shape[0])
        start += out_ref.shape[0]
        total = kept_ref[here, :].astype(F32) + other_ref[here, :].astype(F32)
        out_ref[...] = total.astype(BF16)


def norm_body(pool_ref, gain_ref, out_ref):
    wide = pool_ref[...].astype(F32)
    scale = lax.rsqrt(jnp.mean(wide * wide, axis=-1, keepdims=True) + EPSILON)
    out_ref[...] = (wide * scale * gain_ref[...]).astype(BF16)


def encoder_body(n, parts, gathered, *refs):
    pool_ref, normed_ref = refs[:2]
    if gathered:
        pieces, (enc_ref, hidden, up, down, *sems) = refs[2:4], refs[4:]
    else:
        pieces, (enc_ref, wq_ref, hidden, up, down) = refs[2:4], refs[8:]
        up_ref, down_ref, wq_own, wq_other = refs[4:8]
    m = lax.axis_index("mp")
    if gathered:
        copies = [[pltpu.make_async_copy(pieces[i], (up, down)[i], sems[0].at[i])] for i in range(2)]
        downs = copies[1]
        ups = copies[:1] + [[]] * (n - 1)
        ups[0][0].start()
        downs[0].start()
    else:
        s, g = lax.axis_index("section"), lax.axis_index("dp")
        dp, tall, wide = parts // 2, up.shape[2], HEAD
        share = pieces[0].shape[2] - tall
        ups, downs = [[] for _ in range(n)], []
        up[m] = up_ref[...].reshape(up.shape[1:])
        down[m] = down_ref[...]
        here = pl.ds(pl.multiple_of(m * wq_ref.shape[1], wq_ref.shape[1]), wq_ref.shape[1])
        wq_ref[0] = of_layer(1, wq_own, wq_other, here, slice(None))
        for j, dz in enumerate(places(n)[1:]):
            for i in range(parts):
                half, dg = divmod(i, dp)
                place = (s ^ half) * dp + (g ^ dg)
                for k in range(2):
                    start = pl.multiple_of((2 * place + k) * share, share)
                    wq_ref[j + 1, pl.ds(start, share)] = pieces[half][k * dp + dg, j, tall:]
                up[m ^ dz, place] = pieces[half][dg, j, :tall]
                where = pl.ds(pl.multiple_of(place * wide, wide), wide)
                for side in range(2):
                    rows_of = slice(side * tall, (side + 1) * tall)
                    down[m ^ dz, rows_of, where] = pieces[half][
                        dp + dg, j, :tall, side * wide : (side + 1) * wide
                    ]
    rows, width = normed_ref.shape
    cols = up.shape[-1]
    chunk = rows // 4
    for dz in range(n):
        for copy in ups[dz]:
            copy.wait()
        k = dz if gathered else m ^ dz
        there = pl.ds(pl.multiple_of(k * cols, cols), cols)
        weight = up[k].reshape(width, cols)
        for r in range(0, rows, chunk):
            product = mm(normed_ref[r : r + chunk, :], weight)
            hidden[r : r + chunk, there] = jax.nn.gelu(product).astype(BF16)
    for copy in downs:
        copy.wait()
    for r in range(0, rows, chunk):
        weight = down[...].reshape(width, hidden.shape[1])
        enc = pool_ref[r : r + chunk, :].astype(F32) + mm(hidden[r : r + chunk, :], weight, NTR)
        enc_ref[r : r + chunk, :] = enc.astype(BF16)


def projected_body(layer, enc_ref, wkv_own, wkv_other, out_ref):
    count, length, total = out_ref.shape
    cols, width = wkv_own.shape[1], wkv_own.shape[0] // 2
    enc = enc_ref[...]
    start = total - 2 * cols
    if start:
        out_ref[:, :, :start] = enc.reshape(count, length, width)
    for kind in range(2):
        weight = of_layer(layer, wkv_own, wkv_other, slice(kind * width, (kind + 1) * width))
        out = mm(enc, weight).astype(BF16).reshape(count, length, cols)
        out_ref[:, :, start + kind * cols : start + (kind + 1) * cols] = out


def slot_slice(c, slots):
    return slice(c * slots * NT, (c + 1) * slots * NT)


def softmax_used(scores, used):
    lane = lax.broadcasted_iota(jnp.int32, scores.shape, scores.ndim - 1)
    scores = jnp.where(lane < used * NT, scores, -1e30)
    powers = jnp.exp(scores - jnp.max(scores, axis=-1, keepdims=True))
    return powers / jnp.sum(powers, axis=-1, keepdims=True)


def query_body(n, gain_own, gain_other, wq_own, wq_other, *refs):
    pieces, query_ref = refs[:-1], refs[-1]
    m = lax.axis_index("mp")
    rows, cols = query_ref.shape
    feats = gain_own.shape[-1]

    def piece(k):
        if len(pieces) == n or k < 2:
            return unpack(pieces[k][...], rows, feats).astype(F32)
        far_inner, next_outer, late_inner, late_outer = (ref[...] for ref in pieces[2:])
        size = rows * feats // cols
        rest = size // 2
        inner = jnp.logical_or(m == 1, m == 2)
        if k == 2:
            inside = jnp.concatenate([far_inner[size:], late_inner[:rest]], axis=0)
            value = jnp.where(inner, inside, next_outer[:size])
        else:
            outside = jnp.concatenate([next_outer[size:], late_outer[:rest]], axis=0)
            value = jnp.where(inner, far_inner[:size], outside)
        return unpack(value, rows, feats).astype(F32)

    total = jnp.zeros((rows, 1), F32)
    for k in range(n):
        wide = piece(k)
        total = total + jnp.sum(wide * wide, axis=-1, keepdims=True)
    scale = lax.rsqrt(total / (n * feats) + EPSILON)
    raw = jnp.zeros((rows, cols), F32)
    for k in range(n):
        gain = of_layer(0, gain_own, gain_other, m ^ k)
        normed = (piece(k) * scale * gain).astype(BF16)
        here = pl.ds(pl.multiple_of((m ^ k) * feats, feats), feats)
        raw = raw + mm(normed, of_layer(0, wq_own, wq_other, here, slice(None)))
    query_ref[...] = (raw * SCALE).astype(BF16)


def scores_of(tracts, slots, heads, query_ref, counts_ref, blocks, probs_ref):
    s = lax.axis_index("section")
    length = query_ref.shape[0] // tracts
    for c in range(tracts):
        here, span = slice(c * length, (c + 1) * length), slot_slice(c, slots)
        for h in range(heads):
            there = slice(h * HEAD, (h + 1) * HEAD)
            probs_ref[c * heads + h] = mm(query_ref[here, there], blocks[span, there], NTR)
    for c in range(tracts):
        both = slice(c * heads, (c + 1) * heads)
        probs_ref[both] = softmax_used(probs_ref[both], counts_ref[s, c])


def first_layer_body(
    tracts, slots, ids_ref, counts_ref, query_ref, own, other, att_ref, probs_ref, blocks
):
    fill_slots(own, other, ids_ref, tracts, slots, blocks)
    rows, cols = query_ref.shape
    heads, length = cols // HEAD, rows // tracts
    scores_of(tracts, slots, heads, query_ref, counts_ref, blocks, probs_ref)
    for c in range(tracts):
        here, span = slice(c * length, (c + 1) * length), slot_slice(c, slots)
        for h in range(heads):
            there = slice(h * HEAD, (h + 1) * HEAD)
            beyond = slice(cols + h * HEAD, cols + (h + 1) * HEAD)
            probs = probs_ref[c * heads + h].astype(BF16)
            att_ref[here, there] = mm(probs, blocks[span, beyond]).astype(BF16)


def between_body(n, *refs):
    gain_own, gain_other, own_ref, wout_own, wout_other, wq_ref = refs[:6]
    pieces = refs[6 : 6 + n]
    rows_ref, messages = refs[6 + n], refs[7 + n :]
    m = lax.axis_index("mp")
    rows, cols = pieces[0].shape
    feats = rows_ref.shape[1]
    wide = unpack(own_ref[...], rows, feats).astype(F32)
    for i, d in enumerate(places(n)):
        here = pl.ds(pl.multiple_of((m ^ d) * cols, cols), cols)
        wide = wide + mm(pieces[i][...], of_layer(0, wout_own, wout_other, here, slice(None)))
    rounded = wide.astype(BF16)
    rows_ref[...] = rounded
    wide = rounded.astype(F32)
    square = to_row(jnp.sum(wide * wide, axis=-1, keepdims=True))
    high = square.astype(BF16).astype(F32)
    index = lax.broadcasted_iota(jnp.int32, (PAD, rows), 0)
    extra = jnp.where(index == 0, high, jnp.where(index == 1, square - high, 0.0)).astype(BF16)
    gained = (wide * of_layer(1, gain_own, gain_other, m)).astype(BF16)
    for i in range(n):
        messages[i][:rows, :] = mm(gained, wq_ref[i]).astype(BF16)
        messages[i][rows:, :] = extra


def prob_grads(tracts, slots, heads, att_ref, blocks, grads_ref):
    rows, cols = att_ref.shape
    length = rows // tracts
    for c in range(tracts):
        here, span = slice(c * length, (c + 1) * length), slot_slice(c, slots)
        for h in range(heads):
            there = slice(h * HEAD, (h + 1) * HEAD)
            beyond = slice(cols + h * HEAD, cols + (h + 1) * HEAD)
            grads_ref[c * heads + h] = mm(att_ref[here, there], blocks[span, beyond], NTR)


def score_grads(tracts, heads, probs_ref, grads_ref, scores_ref, soft_ref):
    for c in range(tracts):
        both = slice(c * heads, (c + 1) * heads)
        probs, grads = probs_ref[both], grads_ref[both]
        inner = jnp.sum(probs * grads, axis=-1, keepdims=True)
        scores_ref[both] = (probs * (grads - inner)).astype(BF16)
        soft_ref[both] = probs.astype(BF16)


def slot_grads(tracts, slots, heads, cols, query_ref, att_ref, scores_ref, soft_ref, dkv_ref):
    length = att_ref.shape[0] // tracts
    for c in range(tracts):
        here, span = slice(c * length, (c + 1) * length), slot_slice(c, slots)
        for h in range(heads):
            there = slice(h * HEAD, (h + 1) * HEAD)
            beyond = slice(cols + h * HEAD, cols + (h + 1) * HEAD)
            dkv_ref[span, there] = mm(
                scores_ref[c * heads + h], query_ref[here, there], TNR
            ).astype(BF16)
            dkv_ref[span, beyond] = mm(
                soft_ref[c * heads + h], att_ref[here, there], TNR
            ).astype(BF16)


def last_values_body(tracts, slots, ids_ref, *refs):
    grads, (own, other, blocks, att_ref, grads_ref) = refs[:-5], refs[-5:]
    fill_slots(own, other, ids_ref, tracts, slots, blocks, own.shape[2] - blocks.shape[1])
    rows, cols = att_ref.shape
    grad = jnp.zeros((rows, cols), F32)
    for part in grads:
        start = grads[1].shape[0] - 2 * rows if part.shape[0] > rows else 0
        grad = grad + part[start : start + rows, :].astype(F32)
    att_ref[...] = grad.astype(BF16)
    prob_grads(tracts, slots, cols // HEAD, att_ref, blocks, grads_ref)


def last_layer_body(n, width, tracts, slots, counts_ref, *refs):
    messages, (blocks, grads_ref) = refs[:n], refs[n : n + 2]
    out_ref, scale_ref, query_ref, scores_ref, soft_ref, raw_ref, probs_ref = refs[n + 2 :]
    rows, cols = raw_ref.shape
    raw = jnp.zeros((rows, cols), F32)
    square = jnp.zeros((1, rows), F32)
    for d in range(n):
        raw = raw + messages[d][:rows, :].astype(F32)
        extra = messages[d][rows:, :].astype(F32)
        square = square + extra[0:1, :] + extra[1:2, :]
    scale = lax.rsqrt(to_column(square) / width + EPSILON)
    scale_ref[...] = jnp.broadcast_to(scale, scale_ref.shape)
    raw = raw * scale
    raw_ref[...] = raw
    query_ref[...] = (raw * SCALE).astype(BF16)
    length = rows // tracts
    heads = cols // HEAD
    scores_of(tracts, slots, heads, query_ref, counts_ref, blocks, probs_ref)
    score_grads(tracts, heads, probs_ref, grads_ref, scores_ref, soft_ref)
    for c in range(tracts):
        here, span = slice(c * length, (c + 1) * length), slot_slice(c, slots)
        for h in range(heads):
            there = slice(h * HEAD, (h + 1) * HEAD)
            grad_query = mm(scores_ref[c * heads + h], blocks[span, there]) * SCALE
            out_ref[here, there] = grad_query.astype(BF16)
    part = jnp.sum(out_ref[:rows, :].astype(F32) * raw_ref[...], axis=-1, keepdims=True)
    index = lax.broadcasted_iota(jnp.int32, (PAD, rows), 0)
    out_ref[rows:, :] = jnp.where(index == 0, to_row(part), 0.0).astype(BF16)


def last_slots_body(tracts, slots, query_ref, att_ref, scores_ref, soft_ref, dkv_ref):
    cols = query_ref.shape[1]
    slot_grads(
        tracts, slots, cols // HEAD, cols, query_ref, att_ref, scores_ref, soft_ref, dkv_ref
    )


def weight_grads(enc_ref, dkv_ref, kept_ref, sent_ref):
    cols = kept_ref.shape[1]
    first = lax.axis_index("section") == 0
    chunk = enc_ref.shape[0] // 2
    for r in range(0, enc_ref.shape[0], chunk):
        total = mm(enc_ref[r : r + chunk, :], dkv_ref[...])
        keys, values = total[:, :cols], total[:, cols:]
        kept_ref[r : r + chunk, :] = jnp.where(first, keys, values).astype(BF16)
        sent_ref[r : r + chunk, :] = jnp.where(first, values, keys).astype(BF16)


def part_grads_body(keep, enc_ref, dkv_ref, out_ref):
    cols = out_ref.shape[1]
    kind = lax.axis_index("section") if keep else 1 - lax.axis_index("section")
    here = pl.ds(pl.multiple_of(kind * cols, cols), cols)
    out_ref[...] = mm(enc_ref[...], dkv_ref[:, here]).astype(BF16)


def last_grads_body(
    tracts, slots, ids_ref, dkv_ref, own, other, enc_ref, kept_ref, sent_ref
):
    for c in range(tracts):
        for k in range(slots):
            here = slice((c * slots + k) * NT, (c * slots + k + 1) * NT)
            enc_ref[:, here] = slot_value(own, other, ids_ref, c, k, 0, enc_ref.shape[0]).T
    weight_grads(enc_ref, dkv_ref, kept_ref, sent_ref)


def back_between_body(n, width, *refs):
    gain_own, gain_other, rows_ref, og_ref, scale_ref, wq_ref = refs[:6]
    wout_own, wout_other = refs[6:8]
    pieces, messages = refs[8 : 8 + n], refs[8 + n :]
    s, m = lax.axis_index("section"), lax.axis_index("mp")
    rows, feats = rows_ref.shape
    cols = pieces[0].shape[1]
    normed = jnp.zeros((rows, feats), F32)
    total = jnp.zeros((1, rows), F32)
    for d in range(n):
        normed = normed + mm(pieces[d][:rows, :], wq_ref[d], NTR)
        total = total + pieces[d][rows:, :].astype(F32)[0:1, :]
    scale = scale_ref[:, 0:1]
    wide = rows_ref[...].astype(F32)
    gain = of_layer(1, gain_own, gain_other, m)
    grad = og_ref[s].astype(F32) + scale * gain * normed
    grad = grad - wide * (scale * scale * (to_column(total) / width))
    grad = grad.astype(BF16)
    for i, d in enumerate(places(n)):
        here = pl.ds(pl.multiple_of((m ^ d) * cols, cols), cols)
        weight = of_layer(0, wout_own, wout_other, here, slice(None))
        messages[i][...] = mm(grad, weight, NTR).astype(BF16)


def first_back_body(n, tracts, slots, query_ref, probs_ref, blocks, *refs):
    grads, (dkv_ref, att_ref, grads_ref, scores_ref, soft_ref) = refs[:n], refs[n:]
    rows, cols = query_ref.shape
    grad = jnp.zeros((rows, cols), F32)
    for d in range(n):
        grad = grad + grads[d][...].astype(F32)
    att_ref[...] = grad.astype(BF16)
    heads = cols // HEAD
    prob_grads(tracts, slots, heads, att_ref, blocks, grads_ref)
    score_grads(tracts, heads, probs_ref, grads_ref, scores_ref, soft_ref)
    slot_grads(tracts, slots, heads, cols, query_ref, att_ref, scores_ref, soft_ref, dkv_ref)


def along_mp(value, n):
    return [value] + [xor_move(value, "mp", d) for d in places(n)[1:]]


def scattered(messages):
    order = places(len(messages))
    return [messages[0]] + [xor_move(messages[i], "mp", order[i]) for i in range(1, len(messages))]


def on_device(
    segment_input,
    out_grad,
    pool_tokens,
    neighbour_ids,
    neighbour_counts,
    enc_gain,
    enc_up,
    enc_down,
    norm_gain,
    w_query,
    w_key,
    w_value,
    w_out,
):
    n, dp = lax.axis_size("mp"), lax.axis_size("dp")
    s = lax.axis_index("section")
    _, _, rows, feats = segment_input.shape
    width = n * feats
    cols = w_query.shape[2]
    half, _, length, enc_width = pool_tokens.shape
    tracts, slots = neighbour_ids.shape[2:]
    ids, counts = neighbour_ids[:, 0], neighbour_counts[:, 0]
    ff = enc_down.shape[0]
    first = s == 0
    gain = norm_gain.reshape(n, 1, feats)
    wq, wk, wv, wout = w_query[0], w_key[0], w_value[0], w_out[0]
    gains, wqs, wouts = ((w, swap(w)) for w in (gain, wq, wout))

    pool_rows = pool_tokens[:, 0].reshape(half * length, enc_width)
    normed = call(
        norm_body, [shape((half * length, enc_width))], [vm(), vm()], flops=half * length * enc_width
    )(pool_rows, enc_gain[None, :])[0]
    down_t = enc_down.T
    parts = 2 * dp
    up_rows, down_cols = enc_width // parts, ff // parts
    shares = up_rows % 16 == 0 and enc_width // n == 2 * up_rows and down_cols == HEAD
    shares = shares and enc_up.shape[1] == 2 * down_cols and dp == 4 and n == 4
    shares = shares and feats % (32 * parts) == 0 and cols == enc_up.shape[1]
    if shares:
        own_shape = shape((rows * feats // cols, cols))
        messages = [shape((2 * up_rows + feats // parts, 2 * down_cols))] * (n - 1)
        rest = own_shape.shape[0] // 2
        longer = shape((messages[0].shape[0] + rest, cols))
        share, own = call(
            share_body, [shape((2 * up_rows, 2 * down_cols)), own_shape], [vm()] * 3
        )(enc_up, down_t, segment_input[:, 0])
        messages = call(
            functools.partial(messages_body, n), messages + [longer], [vm()] * 4
        )(share, own, *wqs)
        line = scattered(messages)
        *grads, far_grads = call(
            functools.partial(out_grads_body, n),
            [shape((rows, cols))] * n + [shape((2 * rows, cols))],
            [vm()] * 3,
            flops=2 * rows * width * cols,
        )(out_grad[:, 0], *wouts)
        piece = (n - 1, up_rows + feats // (2 * parts), 2 * down_cols)
        up, down, near, message, inner_rows = call(
            functools.partial(line_body, n, up_rows),
            [shape(piece)] * 2
            + [shape((rest + size, cols)) for size in (0, 2 * rows + PAD, own_shape.shape[0])],
            [vm()] * (n + 2),
            deps=[gains[1]],
        )(*line, own, far_grads)
        inner, outer = [(1, 2), (2, 1)], [(1, 0), (2, 3)]
        up1, down2 = xor_move(up, "dp", 1), xor_move(down, "dp", 2)
        far_inner = lax.ppermute(inner_rows, "mp", inner)
        message = xor_move(message, "mp", 1)
        ups, downs, message, near = call(
            pair_body,
            [shape((2,) + piece)] * 2 + [shape((rest + 2 * rows, cols)), own_shape],
            [vm()] * 8,
            deps=[far_inner],
        )(up, up1, down, down2, near, message, grads[1], grads[2])
        up2, down1 = xor_move(ups, "dp", 2), xor_move(downs, "dp", 1)
        next_outer = lax.ppermute(far_inner, "mp", outer)
        message = lax.ppermute(message, "mp", inner)
        gathered, close, wkv = call(
            gather_body,
            [shape((parts,) + piece), shape((rest + rows, cols)), shape((2 * enc_width, cols))],
            [vm()] * 10,
            deps=[next_outer, normed],
        )(up, up1, up2, down, down2, down1, message, grads[3], wk, wv)
        pieces = [gathered, swap(gathered), enc_up, down_t, *wqs]
        close = xor_move(close, "mp", 1)
        grad_parts = [grads[0], message, close]
        row_pieces = [own, near, far_inner, next_outer, message, close]
        before_projected = [close]
        scratch = [
            pltpu.VMEM((n, parts, up_rows, enc_up.shape[1]), BF16),
            pltpu.VMEM((n, enc_width // n, ff), BF16),
        ]
    else:
        own = call(
            functools.partial(rows_body, cols), [shape((rows * feats // cols, cols))], [vm()]
        )(segment_input[:, 0])[0]
        grad_parts = call(
            functools.partial(out_grads_body, n),
            [shape((rows, cols))] * n,
            [vm()] * 3,
            flops=2 * rows * width * cols,
        )(out_grad[:, 0], *wouts)
        row_pieces, grad_parts = along_mp(own, n), scattered(list(grad_parts))
        query_shares = call(
            functools.partial(query_shares_body, n), [shape((feats, cols))] * n, [vm()] * 2
        )(*wqs)
        projection = jnp.stack(scattered(query_shares))
        wkv = jnp.concatenate([wk, wv], axis=0)
        before_projected = []
        pieces = [
            lax.all_gather(enc_up, "mp", axis=0),
            lax.all_gather(down_t, "mp", axis=0, tiled=True),
        ]
        scratch = [
            pltpu.VMEM((n, enc_width, enc_up.shape[1]), BF16),
            pltpu.VMEM((enc_width, ff), BF16),
            pltpu.SemaphoreType.DMA((2,)),
        ]

    wkvs = (wkv, swap(wkv))

    encoded = call(
        functools.partial(encoder_body, n, parts, not shares),
        [shape((half * length, enc_width))] + [shape((n, feats, cols))] * shares,
        [vm()] * 8 if shares else [vm()] * 2 + [hbm()] * 2,
        [pltpu.VMEM((half * length, ff), BF16)] + scratch,
        flops=4 * half * length * enc_width * ff,
        limit=ENCODER_LIMIT if shares else 48 * 1024 * 1024,
    )(pool_rows, normed, *pieces)
    enc = encoded[0]
    if shares:
        projection = encoded[1]
    pool0_own, enc_own = (
        call(
            functools.partial(projected_body, layer),
            [shape((half, length, layer * enc_width + 2 * cols))],
            [vm()] * 3,
            flops=4 * half * length * enc_width * cols,
            deps=before_projected,
        )(enc, *wkvs)[0]
        for layer in (0, 1)
    )
    pool0_other = swap(pool0_own)
    heads = cols // HEAD
    chunk = rows // tracts
    slot_rows = tracts * slots * NT
    wide_scores = pltpu.VMEM((tracts * heads, chunk, slots * NT), F32)
    bf_scores = pltpu.VMEM((tracts * heads, chunk, slots * NT), BF16)
    attention_flops = 2 * rows * slots * NT * cols

    wide_shape = shape((tracts * heads, chunk, slots * NT), F32)
    block_shape = shape((slot_rows, 2 * cols))
    query0 = call(
        functools.partial(query_body, n),
        [shape((rows, cols))],
        [vm()] * (4 + len(row_pieces)),
        flops=2 * rows * width * cols,
        deps=[pool0_own],
    )(*gains, *wqs, *row_pieces)[0]
    att, probs0, blocks0, enc_own = call(
        functools.partial(first_layer_body, tracts, slots),
        [shape((rows, cols)), wide_shape, block_shape],
        [smem(), smem()] + [vm()] * 3,
        flops=2 * attention_flops,
        passing=[enc_own],
    )(ids, counts, query0, pool0_own, pool0_other)
    enc_other = swap(enc_own)
    att_pieces = along_mp(att, n)
    rows1, *messages = call(
        functools.partial(between_body, n),
        [shape((rows, feats))] + [shape((rows + PAD, cols))] * n,
        [vm()] * (6 + n),
        flops=4 * rows * feats * n * cols,
        deps=[enc_other],
    )(*gains, own, *wouts, projection, *att_pieces)
    query_pieces = scattered(messages)
    bf_shape = shape((tracts * heads, chunk, slots * NT))
    blocks1, att1, prob_grads1 = call(
        functools.partial(last_values_body, tracts, slots),
        [block_shape, shape((rows, cols)), wide_shape],
        [smem()] + [vm()] * (len(grad_parts) + 2),
        flops=attention_flops,
    )(ids, *grad_parts, enc_own, enc_other)
    grad_query, scale1, query1, *soft1 = call(
        functools.partial(last_layer_body, n, width, tracts, slots),
        [shape((rows + PAD, cols)), shape((rows, HEAD), F32), shape((rows, cols))] + [bf_shape] * 2,
        [smem()] + [vm()] * (n + 2),
        [pltpu.VMEM((rows, cols), F32), wide_scores],
        flops=3 * attention_flops,
    )(counts, *query_pieces, blocks1, prob_grads1)
    dkv1 = call(
        functools.partial(last_slots_body, tracts, slots),
        [shape((slot_rows, 2 * cols))],
        [vm()] * 4,
        flops=2 * attention_flops,
    )(query1, att1, *soft1)[0]
    query_grads = along_mp(grad_query, n)
    enc_slots, kept1, sent1 = call(
        functools.partial(last_grads_body, tracts, slots),
        [shape((enc_width, slot_rows)), shape((enc_width, cols)), shape((enc_width, cols))],
        [smem(), vm(), vm(), vm()],
        flops=4 * enc_width * slot_rows * cols,
    )(ids, dkv1, enc_own, enc_other)
    *messages, kept1, sent1 = call(
        functools.partial(back_between_body, n, width),
        [shape((rows, cols))] * n,
        [vm()] * (8 + n),
        flops=4 * rows * feats * n * cols,
        passing=[kept1, sent1],
    )(*gains, rows1, out_grad[:, 0], scale1, projection, *wouts, *query_grads)
    grad_pieces0 = scattered(messages)

    def over_dp(parts, order):
        size = len(parts)
        moved = [None] * size
        for by in sorted(set(order)):
            members = [i for i in range(size) if order[i] == by]
            if len(members) == 1:
                moved[members[0]] = xor_move(parts[members[0]], "dp", by)
                continue
            message = xor_move(jnp.concatenate([parts[i] for i in members], axis=0), "dp", by)
            start = 0
            for i in members:
                moved[i] = lax.slice_in_dim(message, start, start + parts[i].shape[0])
                start += parts[i].shape[0]
        shapes = [shape(part.shape) for part in parts]
        return call(functools.partial(add_body, size), shapes, [vm()] * (2 * size))(*parts, *moved)

    def pieces_of(kept, sent, sizes):
        parts = [shape((size, cols)) for size in sizes]
        return call(pieces_body, parts, [vm()] * 2)(kept, swap(sent))

    size = enc_width // 2
    early = size // 2 + 16 if size % 32 == 0 else size // 2
    ax, bx, ay, by = pieces_of(kept1, sent1, [early, size - early] * 2)
    if dp == 4:
        ax, ay = over_dp([ax, ay], (1, 2))
    dkv0 = call(
        functools.partial(first_back_body, n, tracts, slots),
        [shape((slot_rows, 2 * cols))],
        [vm()] * (n + 3),
        [pltpu.VMEM((rows, cols), BF16), wide_scores, bf_scores, bf_scores],
        flops=3 * attention_flops,
    )(query0, probs0, blocks0, *grad_pieces0)[0]
    sent0, kept0 = (
        call(
            functools.partial(part_grads_body, keep),
            [shape((enc_width, cols))],
            [vm()] * 2,
            flops=2 * enc_width * slot_rows * cols,
            deps=[] if keep else [ax, ay],
        )(enc_slots, dkv0)[0]
        for keep in (False, True)
    )
    top, bottom = pieces_of(kept0, sent0, [size] * 2)
    if dp == 4:
        top, bottom, ax, ay, bx, by = over_dp([top, bottom, ax, ay, bx, by], (1, 2, 2, 1, 1, 2))
        top, bottom, bx, by = over_dp([top, bottom, bx, by], (2, 1, 2, 1))
    else:
        top, bottom, ax, ay, bx, by = lax.psum((top, bottom, ax, ay, bx, by), "dp")
    sum0 = jnp.concatenate([top, bottom], axis=0)
    sum1 = jnp.concatenate([ax, bx, ay, by], axis=0)
    received = swap(jnp.where(first, sum1, sum0))
    key_total = jnp.where(first, sum0, received)
    value_total = jnp.where(first, received, sum1)
    return (key_total[None], value_total[None])


def solution(mesh):
    placed = (
        P(None, "dp", None, "mp"),
        P(None, "dp", None, "mp"),
        P("section", "dp", None, None),
        P(None, "dp", None, None),
        P(None, "dp", None),
        P(),
        P(None, "mp"),
        P(None, "mp"),
        P("section", None),
        P("section", None, "mp"),
        P("section", None, "mp"),
        P("section", None, "mp"),
        P("section", None, "mp"),
    )
    return jax.shard_map(
        on_device,
        mesh=mesh,
        in_specs=placed,
        out_specs=(P("section", None, "mp"), P("section", None, "mp")),
        check_vma=False,
    )
```

```python
import functools

import jax
import jax.numpy as jnp
from jax import lax
from jax.experimental import pallas as pl
from jax.experimental.pallas import tpu as pltpu
from jax.sharding import PartitionSpec as P

HEAD = 128
NT = 128
EPSILON = 1e-05
SCALE = HEAD ** (-0.5)
PAD = 16
VMEM_LIMIT = 20 * 1024 * 1024
ENCODER_LIMIT = 32 * 1024 * 1024
FIRST_LIMIT = 60 * 1024 * 1024

BF16 = jnp.bfloat16
F32 = jnp.float32
NN = (((1,), (0,)), ((), ()))
NTR = (((1,), (1,)), ((), ()))
TNR = (((0,), (0,)), ((), ()))


def mm(a, b, dims=NN):
    return lax.dot_general(a, b, dims, preferred_element_type=F32)


def xor_move(value, axis, by):
    count = lax.axis_size(axis)
    return lax.ppermute(value, axis, [(i, i ^ by) for i in range(count)])


def places(n):
    return (0, 2, 3, 1) if n == 4 else tuple(range(n))


def swap(value):
    return xor_move(value, "section", 1)


def vm():
    return pl.BlockSpec(memory_space=pltpu.VMEM)


def hbm():
    return pl.BlockSpec(memory_space=pl.ANY)


def hbm_only():
    return pl.BlockSpec(memory_space=pltpu.HBM)


def smem():
    return pl.BlockSpec(memory_space=pltpu.SMEM)


def call(body, outs, specs, scratch=(), flops=0, limit=VMEM_LIMIT, first=(), deps=(), passing=()):
    count, more, kept, results = len(specs), len(deps), len(passing), len(outs)
    nbytes = sum(o.size * o.dtype.itemsize for o in outs)
    begin = len(first)
    start = begin + count + more + kept

    def kernel(*refs):
        given = refs[begin : begin + count]
        body(*given, *refs[start : start + results], *refs[start + results + kept :])

    def run(*args):
        return pl.pallas_call(
            kernel,
            out_shape=list(outs) + [shape(x.shape, x.dtype) for x in passing],
            in_specs=[hbm()] * begin + list(specs) + [hbm()] * (more + kept),
            out_specs=[vm() for _ in outs] + [hbm()] * kept,
            scratch_shapes=list(scratch),
            input_output_aliases={begin + count + more + i: results + i for i in range(kept)},
            compiler_params=pltpu.CompilerParams(vmem_limit_bytes=limit),
            cost_estimate=pl.CostEstimate(
                flops=flops // 1000, bytes_accessed=nbytes // 1000, transcendentals=0
            ),
        )(*first, *args, *deps, *passing)

    return run


def shape(dims, dtype=BF16):
    return jax.ShapeDtypeStruct(dims, dtype)


def to_row(column):
    rows = column.shape[0]
    here = lax.broadcasted_iota(jnp.int32, (rows, rows), 0)
    there = lax.broadcasted_iota(jnp.int32, (rows, rows), 1)
    return jnp.sum(jnp.where(here == there, column, 0.0), axis=0, keepdims=True)


def to_column(row):
    rows = row.shape[1]
    here = lax.broadcasted_iota(jnp.int32, (rows, rows), 0)
    there = lax.broadcasted_iota(jnp.int32, (rows, rows), 1)
    return jnp.sum(jnp.where(here == there, row, 0.0), axis=1, keepdims=True)


def slot_value(own, other, ids_ref, tract, slot, start, size):
    half = own.shape[0]
    s = lax.axis_index("section")
    place = ids_ref[s, tract, slot]
    mine, theirs = place - s * half, place - (1 - s) * half
    here = jnp.logical_and(mine >= 0, mine < half)
    cols = slice(start, start + size)
    return jnp.where(
        here,
        own[jnp.clip(mine, 0, half - 1), :, cols],
        other[jnp.clip(theirs, 0, half - 1), :, cols],
    )


def fill_slots(own, other, ids_ref, tracts, slots, blocks, start=0):
    for c in range(tracts):
        for k in range(slots):
            here = slice((c * slots + k) * NT, (c * slots + k + 1) * NT)
            blocks[here, :] = slot_value(own, other, ids_ref, c, k, start, blocks.shape[1])


def of_layer(layer, own_ref, other_ref, *index):
    index = index or (Ellipsis,)
    own = lax.axis_index("section") == layer
    return jnp.where(own, own_ref[index], other_ref[index])


def pack(value, cols):
    rows, feats = value.shape
    if feats >= cols:
        return jnp.concatenate([value[:, i : i + cols] for i in range(0, feats, cols)], axis=0)
    share = rows * feats // cols
    return jnp.concatenate([value[i : i + share] for i in range(0, rows, share)], axis=1)


def unpack(value, rows, feats):
    cols = value.shape[1]
    if feats >= cols:
        return jnp.concatenate(
            [value[i : i + rows] for i in range(0, value.shape[0], rows)], axis=1
        )
    return jnp.concatenate([value[:, i : i + feats] for i in range(0, cols, feats)], axis=0)


def share_body(up_ref, down_ref, rows_ref, out_ref, own_ref, sems):
    s = lax.axis_index("section")
    place = s * lax.axis_size("dp") + lax.axis_index("dp")
    total, length = rows_ref.shape[1], own_ref.shape[1]
    copies = []
    for i in range(own_ref.shape[0] // total):
        source = rows_ref.at[s, :, pl.ds(i * length, length)]
        target = own_ref.at[pl.ds(i * total, total)]
        copies.append(pltpu.make_async_copy(source, target, sems.at[i]))
        copies[-1].start()
    tall = out_ref.shape[0] // 2
    cols = pl.ds(pl.multiple_of(place * HEAD, HEAD), HEAD)
    out_ref[:tall, :] = up_ref[pl.ds(pl.multiple_of(place * tall, 16), tall), :]
    for side in range(2):
        there = slice(side * HEAD, (side + 1) * HEAD)
        out_ref[tall:, there] = down_ref[side * tall : (side + 1) * tall, cols]
    for copy in copies:
        copy.wait()


def messages_body(n, share_ref, own_ref, wq_own, wq_other, *outs):
    s, m = lax.axis_index("section"), lax.axis_index("mp")
    place = s * lax.axis_size("dp") + lax.axis_index("dp")
    parts = 2 * lax.axis_size("dp")
    above = share_ref.shape[0]
    share = wq_own.shape[0] // (n * parts)
    for i, d in enumerate(places(n)):
        outs[i][:above, :] = share_ref[...]
        start = ((m ^ d) * parts + place) * share
        here = pl.ds(pl.multiple_of(start, share), share)
        outs[i][above : above + share, :] = of_layer(1, wq_own, wq_other, here, slice(None))
    half = own_ref.shape[0] // 2
    outs[n - 1][above + share :, :] = own_ref[:half, :]


def line_body(n, tall, *refs):
    half = (refs[0].shape[0] - 2 * tall) // 2
    own_ref, far_ref = refs[n], refs[n + 1]
    near_ref, message, inner_ref = refs[n + 4 :]
    size = own_ref.shape[0]
    inner_ref[:size, :] = own_ref[...]
    inner_ref[size:, :] = refs[n - 1][2 * (tall + half) :, :]
    near_ref[...] = refs[n - 1][2 * (tall + half) :, :]
    rest = own_ref.shape[0] // 2
    message[:rest, :] = own_ref[rest:, :]
    message[rest:-PAD, :] = far_ref[...]
    message[-PAD:, :] = jnp.zeros((PAD, message.shape[1]), BF16)
    for i in range(1, n):
        for j in range(2):
            start = 2 * tall + j * half
            refs[n + 2 + j][i - 1, :tall] = refs[i][j * tall : (j + 1) * tall, :]
            refs[n + 2 + j][i - 1, tall:] = refs[i][start : start + half, :]


def pair_body(up, up1, down, down2, near1, moved, far2, far3, ups, downs, message, near):
    for here, there, out_ref in ((up, up1, ups), (down, down2, downs)):
        out_ref[0] = here[...]
        out_ref[1] = there[...]
    rest, rows = near1.shape[0], far2.shape[0]
    near[:rest, :] = near1[...]
    near[rest:, :] = moved[:rest, :]
    message[:rest, :] = moved[:rest, :]
    for i, far in enumerate((far3, far2)):
        start = rest + i * rows
        total = moved[start : start + rows, :].astype(F32) + far[...].astype(F32)
        message[start : start + rows, :] = total.astype(BF16)


def gather_body(
    up, up1, up2, down, down2, down1, moved, close, key_ref, value_ref,
    out_ref, message, weight_ref,
):
    tall = key_ref.shape[0]
    weight_ref[:tall, :] = key_ref[...]
    weight_ref[tall:, :] = value_ref[...]
    for base, parts in ((0, (up, up1, up2)), (4, (down, down2, down1))):
        near = 1 if base == 0 else 2
        out_ref[base] = parts[0][...]
        out_ref[base + near] = parts[1][...]
        out_ref[base + 3 - near] = parts[2][0]
        out_ref[base + 3] = parts[2][1]
    rows = close.shape[0]
    rest = message.shape[0] - rows
    message[:rest, :] = moved[:rest, :]
    total = moved[rest + rows :, :].astype(F32) + close[...].astype(F32)
    message[rest:, :] = total.astype(BF16)


def rows_body(cols, rows_ref, own_ref):
    own_ref[...] = pack(rows_ref[lax.axis_index("section")], cols)


def query_shares_body(n, wq_own, wq_other, *outs):
    m = lax.axis_index("mp")
    tall = outs[0].shape[0]
    for i, d in enumerate(places(n)):
        here = pl.ds(pl.multiple_of((m ^ d) * tall, tall), tall)
        outs[i][...] = of_layer(1, wq_own, wq_other, here, slice(None))


def out_grads_body(n, og_ref, wout_own, wout_other, *outs):
    s, m = lax.axis_index("section"), lax.axis_index("mp")
    cols = outs[0].shape[1]
    rows = og_ref.shape[1]
    for i, d in enumerate(places(n)):
        here = pl.ds(pl.multiple_of((m ^ d) * cols, cols), cols)
        weight = of_layer(1, wout_own, wout_other, here, slice(None))
        outs[i][...] = mm(og_ref[s], weight, NTR).astype(BF16)
    for i, out_ref in enumerate(outs[1:3]):
        if len(outs) > n:
            outs[n][i * rows : (i + 1) * rows, :] = out_ref[...]


def add_body(count, *refs):
    for i in range(count):
        total = refs[i][...].astype(F32) + refs[count + i][...].astype(F32)
        refs[2 * count + i][...] = total.astype(BF16)


def pieces_body(kept_ref, other_ref, *outs):
    start = 0
    for out_ref in outs:
        here = slice(start, start + out_ref.shape[0])
        start += out_ref.shape[0]
        total = kept_ref[here, :].astype(F32) + other_ref[here, :].astype(F32)
        out_ref[...] = total.astype(BF16)


def norm_body(pool_ref, gain_ref, out_ref):
    wide = pool_ref[...].astype(F32)
    scale = lax.rsqrt(jnp.mean(wide * wide, axis=-1, keepdims=True) + EPSILON)
    out_ref[...] = (wide * scale * gain_ref[...]).astype(BF16)


def encoder_body(n, parts, gathered, *refs):
    pool_ref, normed_ref = refs[:2]
    if gathered:
        pieces, (enc_ref, hidden, up, down, *sems) = refs[2:4], refs[4:]
    else:
        pieces, (enc_ref, wq_ref, hidden, up, down) = refs[2:4], refs[8:]
        up_ref, down_ref, wq_own, wq_other = refs[4:8]
    m = lax.axis_index("mp")
    if gathered:
        copies = [[pltpu.make_async_copy(pieces[i], (up, down)[i], sems[0].at[i])] for i in range(2)]
        downs = copies[1]
        ups = copies[:1] + [[]] * (n - 1)
        ups[0][0].start()
        downs[0].start()
    else:
        s, g = lax.axis_index("section"), lax.axis_index("dp")
        dp, tall, wide = parts // 2, up.shape[2], HEAD
        share = pieces[0].shape[2] - tall
        ups, downs = [[] for _ in range(n)], []
        up[m] = up_ref[...].reshape(up.shape[1:])
        down[m] = down_ref[...]
        here = pl.ds(pl.multiple_of(m * wq_ref.shape[1], wq_ref.shape[1]), wq_ref.shape[1])
        wq_ref[0] = of_layer(1, wq_own, wq_other, here, slice(None))
        for j, dz in enumerate(places(n)[1:]):
            for i in range(parts):
                half, dg = divmod(i, dp)
                place = (s ^ half) * dp + (g ^ dg)
                for k in range(2):
                    start = pl.multiple_of((2 * place + k) * share, share)
                    wq_ref[j + 1, pl.ds(start, share)] = pieces[half][k * dp + dg, j, tall:]
                up[m ^ dz, place] = pieces[half][dg, j, :tall]
                where = pl.ds(pl.multiple_of(place * wide, wide), wide)
                for side in range(2):
                    rows_of = slice(side * tall, (side + 1) * tall)
                    down[m ^ dz, rows_of, where] = pieces[half][
                        dp + dg, j, :tall, side * wide : (side + 1) * wide
                    ]
    rows, width = normed_ref.shape
    cols = up.shape[-1]
    chunk = rows // 4
    for dz in range(n):
        for copy in ups[dz]:
            copy.wait()
        k = dz if gathered else m ^ dz
        there = pl.ds(pl.multiple_of(k * cols, cols), cols)
        weight = up[k].reshape(width, cols)
        for r in range(0, rows, chunk):
            product = mm(normed_ref[r : r + chunk, :], weight)
            hidden[r : r + chunk, there] = jax.nn.gelu(product).astype(BF16)
    for copy in downs:
        copy.wait()
    for r in range(0, rows, chunk):
        weight = down[...].reshape(width, hidden.shape[1])
        enc = pool_ref[r : r + chunk, :].astype(F32) + mm(hidden[r : r + chunk, :], weight, NTR)
        enc_ref[r : r + chunk, :] = enc.astype(BF16)


def projected_body(layer, enc_ref, wkv_own, wkv_other, out_ref):
    count, length, total = out_ref.shape
    cols, width = wkv_own.shape[1], wkv_own.shape[0] // 2
    enc = enc_ref[...]
    start = total - 2 * cols
    if start:
        out_ref[:, :, :start] = enc.reshape(count, length, width)
    for kind in range(2):
        weight = of_layer(layer, wkv_own, wkv_other, slice(kind * width, (kind + 1) * width))
        out = mm(enc, weight).astype(BF16).reshape(count, length, cols)
        out_ref[:, :, start + kind * cols : start + (kind + 1) * cols] = out


def slot_slice(c, slots):
    return slice(c * slots * NT, (c + 1) * slots * NT)


def softmax_used(scores, used):
    lane = lax.broadcasted_iota(jnp.int32, scores.shape, scores.ndim - 1)
    scores = jnp.where(lane < used * NT, scores, -1e30)
    powers = jnp.exp(scores - jnp.max(scores, axis=-1, keepdims=True))
    return powers / jnp.sum(powers, axis=-1, keepdims=True)


def query_body(n, gain_own, gain_other, wq_own, wq_other, *refs):
    pieces, query_ref = refs[:-1], refs[-1]
    m = lax.axis_index("mp")
    rows, cols = query_ref.shape
    feats = gain_own.shape[-1]

    def piece(k):
        if len(pieces) == n or k < 2:
            return unpack(pieces[k][...], rows, feats).astype(F32)
        far_inner, next_outer, late_inner, late_outer = (ref[...] for ref in pieces[2:])
        size = rows * feats // cols
        rest = size // 2
        inner = jnp.logical_or(m == 1, m == 2)
        if k == 2:
            inside = jnp.concatenate([far_inner[size:], late_inner[:rest]], axis=0)
            value = jnp.where(inner, inside, next_outer[:size])
        else:
            outside = jnp.concatenate([next_outer[size:], late_outer[:rest]], axis=0)
            value = jnp.where(inner, far_inner[:size], outside)
        return unpack(value, rows, feats).astype(F32)

    total = jnp.zeros((rows, 1), F32)
    for k in range(n):
        wide = piece(k)
        total = total + jnp.sum(wide * wide, axis=-1, keepdims=True)
    scale = lax.rsqrt(total / (n * feats) + EPSILON)
    raw = jnp.zeros((rows, cols), F32)
    for k in range(n):
        gain = of_layer(0, gain_own, gain_other, m ^ k)
        normed = (piece(k) * scale * gain).astype(BF16)
        here = pl.ds(pl.multiple_of((m ^ k) * feats, feats), feats)
        raw = raw + mm(normed, of_layer(0, wq_own, wq_other, here, slice(None)))
    query_ref[...] = (raw * SCALE).astype(BF16)


def scores_of(tracts, slots, heads, query_ref, counts_ref, blocks, probs_ref):
    s = lax.axis_index("section")
    length = query_ref.shape[0] // tracts
    for c in range(tracts):
        here, span = slice(c * length, (c + 1) * length), slot_slice(c, slots)
        for h in range(heads):
            there = slice(h * HEAD, (h + 1) * HEAD)
            probs_ref[c * heads + h] = mm(query_ref[here, there], blocks[span, there], NTR)
    for c in range(tracts):
        both = slice(c * heads, (c + 1) * heads)
        probs_ref[both] = softmax_used(probs_ref[both], counts_ref[s, c])


def first_layer_body(
    tracts, slots, ids_ref, counts_ref, query_ref, own, other, att_ref, probs_ref, blocks
):
    fill_slots(own, other, ids_ref, tracts, slots, blocks)
    rows, cols = query_ref.shape
    heads, length = cols // HEAD, rows // tracts
    scores_of(tracts, slots, heads, query_ref, counts_ref, blocks, probs_ref)
    for c in range(tracts):
        here, span = slice(c * length, (c + 1) * length), slot_slice(c, slots)
        for h in range(heads):
            there = slice(h * HEAD, (h + 1) * HEAD)
            beyond = slice(cols + h * HEAD, cols + (h + 1) * HEAD)
            probs = probs_ref[c * heads + h].astype(BF16)
            att_ref[here, there] = mm(probs, blocks[span, beyond]).astype(BF16)


def between_body(n, *refs):
    gain_own, gain_other, own_ref, wout_own, wout_other, wq_ref = refs[:6]
    pieces = refs[6 : 6 + n]
    rows_ref, messages = refs[6 + n], refs[7 + n :]
    m = lax.axis_index("mp")
    rows, cols = pieces[0].shape
    feats = rows_ref.shape[1]
    wide = unpack(own_ref[...], rows, feats).astype(F32)
    for i, d in enumerate(places(n)):
        here = pl.ds(pl.multiple_of((m ^ d) * cols, cols), cols)
        wide = wide + mm(pieces[i][...], of_layer(0, wout_own, wout_other, here, slice(None)))
    rounded = wide.astype(BF16)
    rows_ref[...] = rounded
    wide = rounded.astype(F32)
    square = to_row(jnp.sum(wide * wide, axis=-1, keepdims=True))
    high = square.astype(BF16).astype(F32)
    index = lax.broadcasted_iota(jnp.int32, (PAD, rows), 0)
    extra = jnp.where(index == 0, high, jnp.where(index == 1, square - high, 0.0)).astype(BF16)
    gained = (wide * of_layer(1, gain_own, gain_other, m)).astype(BF16)
    for i in range(n):
        messages[i][:rows, :] = mm(gained, wq_ref[i]).astype(BF16)
        messages[i][rows:, :] = extra


def prob_grads(tracts, slots, heads, att_ref, blocks, grads_ref):
    rows, cols = att_ref.shape
    length = rows // tracts
    for c in range(tracts):
        here, span = slice(c * length, (c + 1) * length), slot_slice(c, slots)
        for h in range(heads):
            there = slice(h * HEAD, (h + 1) * HEAD)
            beyond = slice(cols + h * HEAD, cols + (h + 1) * HEAD)
            grads_ref[c * heads + h] = mm(att_ref[here, there], blocks[span, beyond], NTR)


def score_grads(tracts, heads, probs_ref, grads_ref, scores_ref, soft_ref):
    for c in range(tracts):
        both = slice(c * heads, (c + 1) * heads)
        probs, grads = probs_ref[both], grads_ref[both]
        inner = jnp.sum(probs * grads, axis=-1, keepdims=True)
        scores_ref[both] = (probs * (grads - inner)).astype(BF16)
        soft_ref[both] = probs.astype(BF16)


def slot_grads(tracts, slots, heads, cols, query_ref, att_ref, scores_ref, soft_ref, dkv_ref):
    length = att_ref.shape[0] // tracts
    for c in range(tracts):
        here, span = slice(c * length, (c + 1) * length), slot_slice(c, slots)
        for h in range(heads):
            there = slice(h * HEAD, (h + 1) * HEAD)
            beyond = slice(cols + h * HEAD, cols + (h + 1) * HEAD)
            dkv_ref[span, there] = mm(
                scores_ref[c * heads + h], query_ref[here, there], TNR
            ).astype(BF16)
            dkv_ref[span, beyond] = mm(
                soft_ref[c * heads + h], att_ref[here, there], TNR
            ).astype(BF16)


def last_values_body(tracts, slots, ids_ref, *refs):
    grads, (own, other, blocks, att_ref, grads_ref) = refs[:-5], refs[-5:]
    fill_slots(own, other, ids_ref, tracts, slots, blocks, own.shape[2] - blocks.shape[1])
    rows, cols = att_ref.shape
    grad = jnp.zeros((rows, cols), F32)
    for part in grads:
        start = grads[1].shape[0] - 2 * rows if part.shape[0] > rows else 0
        grad = grad + part[start : start + rows, :].astype(F32)
    att_ref[...] = grad.astype(BF16)
    prob_grads(tracts, slots, cols // HEAD, att_ref, blocks, grads_ref)


def last_layer_body(n, width, tracts, slots, counts_ref, *refs):
    messages, (blocks, grads_ref) = refs[:n], refs[n : n + 2]
    out_ref, scale_ref, query_ref, scores_ref, soft_ref, raw_ref, probs_ref = refs[n + 2 :]
    rows, cols = raw_ref.shape
    raw = jnp.zeros((rows, cols), F32)
    square = jnp.zeros((1, rows), F32)
    for d in range(n):
        raw = raw + messages[d][:rows, :].astype(F32)
        extra = messages[d][rows:, :].astype(F32)
        square = square + extra[0:1, :] + extra[1:2, :]
    scale = lax.rsqrt(to_column(square) / width + EPSILON)
    scale_ref[...] = jnp.broadcast_to(scale, scale_ref.shape)
    raw = raw * scale
    raw_ref[...] = raw
    query_ref[...] = (raw * SCALE).astype(BF16)
    length = rows // tracts
    heads = cols // HEAD
    scores_of(tracts, slots, heads, query_ref, counts_ref, blocks, probs_ref)
    score_grads(tracts, heads, probs_ref, grads_ref, scores_ref, soft_ref)
    for c in range(tracts):
        here, span = slice(c * length, (c + 1) * length), slot_slice(c, slots)
        for h in range(heads):
            there = slice(h * HEAD, (h + 1) * HEAD)
            grad_query = mm(scores_ref[c * heads + h], blocks[span, there]) * SCALE
            out_ref[here, there] = grad_query.astype(BF16)
    part = jnp.sum(out_ref[:rows, :].astype(F32) * raw_ref[...], axis=-1, keepdims=True)
    index = lax.broadcasted_iota(jnp.int32, (PAD, rows), 0)
    out_ref[rows:, :] = jnp.where(index == 0, to_row(part), 0.0).astype(BF16)


def last_slots_body(tracts, slots, query_ref, att_ref, scores_ref, soft_ref, dkv_ref):
    cols = query_ref.shape[1]
    slot_grads(
        tracts, slots, cols // HEAD, cols, query_ref, att_ref, scores_ref, soft_ref, dkv_ref
    )


def weight_grads(enc_ref, dkv_ref, kept_ref, sent_ref):
    cols = kept_ref.shape[1]
    first = lax.axis_index("section") == 0
    chunk = enc_ref.shape[0] // 2
    for r in range(0, enc_ref.shape[0], chunk):
        total = mm(enc_ref[r : r + chunk, :], dkv_ref[...])
        keys, values = total[:, :cols], total[:, cols:]
        kept_ref[r : r + chunk, :] = jnp.where(first, keys, values).astype(BF16)
        sent_ref[r : r + chunk, :] = jnp.where(first, values, keys).astype(BF16)


def part_grads_body(keep, enc_ref, dkv_ref, out_ref):
    cols = out_ref.shape[1]
    kind = lax.axis_index("section") if keep else 1 - lax.axis_index("section")
    here = pl.ds(pl.multiple_of(kind * cols, cols), cols)
    out_ref[...] = mm(enc_ref[...], dkv_ref[:, here]).astype(BF16)


def last_grads_body(
    tracts, slots, ids_ref, dkv_ref, own, other, enc_ref, kept_ref, sent_ref
):
    for c in range(tracts):
        for k in range(slots):
            here = slice((c * slots + k) * NT, (c * slots + k + 1) * NT)
            enc_ref[:, here] = slot_value(own, other, ids_ref, c, k, 0, enc_ref.shape[0]).T
    weight_grads(enc_ref, dkv_ref, kept_ref, sent_ref)


def back_between_body(n, width, *refs):
    gain_own, gain_other, rows_ref, og_ref, scale_ref, wq_ref = refs[:6]
    wout_own, wout_other = refs[6:8]
    pieces, messages = refs[8 : 8 + n], refs[8 + n :]
    s, m = lax.axis_index("section"), lax.axis_index("mp")
    rows, feats = rows_ref.shape
    cols = pieces[0].shape[1]
    normed = jnp.zeros((rows, feats), F32)
    total = jnp.zeros((1, rows), F32)
    for d in range(n):
        normed = normed + mm(pieces[d][:rows, :], wq_ref[d], NTR)
        total = total + pieces[d][rows:, :].astype(F32)[0:1, :]
    scale = scale_ref[:, 0:1]
    wide = rows_ref[...].astype(F32)
    gain = of_layer(1, gain_own, gain_other, m)
    grad = og_ref[s].astype(F32) + scale * gain * normed
    grad = grad - wide * (scale * scale * (to_column(total) / width))
    grad = grad.astype(BF16)
    for i, d in enumerate(places(n)):
        here = pl.ds(pl.multiple_of((m ^ d) * cols, cols), cols)
        weight = of_layer(0, wout_own, wout_other, here, slice(None))
        messages[i][...] = mm(grad, weight, NTR).astype(BF16)


def first_back_body(n, tracts, slots, query_ref, probs_ref, blocks, *refs):
    grads, (dkv_ref, att_ref, grads_ref, scores_ref, soft_ref) = refs[:n], refs[n:]
    rows, cols = query_ref.shape
    grad = jnp.zeros((rows, cols), F32)
    for d in range(n):
        grad = grad + grads[d][...].astype(F32)
    att_ref[...] = grad.astype(BF16)
    heads = cols // HEAD
    prob_grads(tracts, slots, heads, att_ref, blocks, grads_ref)
    score_grads(tracts, heads, probs_ref, grads_ref, scores_ref, soft_ref)
    slot_grads(tracts, slots, heads, cols, query_ref, att_ref, scores_ref, soft_ref, dkv_ref)


def along_mp(value, n):
    return [value] + [xor_move(value, "mp", d) for d in places(n)[1:]]


def scattered(messages):
    order = places(len(messages))
    return [messages[0]] + [xor_move(messages[i], "mp", order[i]) for i in range(1, len(messages))]


def on_device(
    segment_input,
    out_grad,
    pool_tokens,
    neighbour_ids,
    neighbour_counts,
    enc_gain,
    enc_up,
    enc_down,
    norm_gain,
    w_query,
    w_key,
    w_value,
    w_out,
):
    n, dp = lax.axis_size("mp"), lax.axis_size("dp")
    s = lax.axis_index("section")
    _, _, rows, feats = segment_input.shape
    width = n * feats
    cols = w_query.shape[2]
    half, _, length, enc_width = pool_tokens.shape
    tracts, slots = neighbour_ids.shape[2:]
    ids, counts = neighbour_ids[:, 0], neighbour_counts[:, 0]
    ff = enc_down.shape[0]
    first = s == 0
    gain = norm_gain.reshape(n, 1, feats)
    wq, wk, wv, wout = w_query[0], w_key[0], w_value[0], w_out[0]
    gains, wqs, wouts = ((w, swap(w)) for w in (gain, wq, wout))

    pool_rows = pool_tokens[:, 0].reshape(half * length, enc_width)
    normed = call(
        norm_body, [shape((half * length, enc_width))], [vm(), vm()], flops=half * length * enc_width
    )(pool_rows, enc_gain[None, :])[0]
    down_t = enc_down.T
    parts = 2 * dp
    up_rows, down_cols = enc_width // parts, ff // parts
    shares = up_rows % 16 == 0 and enc_width // n == 2 * up_rows and down_cols == HEAD
    shares = shares and enc_up.shape[1] == 2 * down_cols and dp == 4 and n == 4
    shares = shares and feats % (32 * parts) == 0 and cols == enc_up.shape[1]
    if shares:
        own_shape = shape((rows * feats // cols, cols))
        messages = [shape((2 * up_rows + feats // parts, 2 * down_cols))] * (n - 1)
        rest = own_shape.shape[0] // 2
        longer = shape((messages[0].shape[0] + rest, cols))
        share, own = call(
            share_body,
            [shape((2 * up_rows, 2 * down_cols)), own_shape],
            [vm(), vm(), hbm()],
            [pltpu.SemaphoreType.DMA((feats // cols,))],
        )(enc_up, down_t, segment_input[:, 0])
        messages = call(
            functools.partial(messages_body, n), messages + [longer], [vm()] * 4
        )(share, own, *wqs)
        line = scattered(messages)
        *grads, far_grads = call(
            functools.partial(out_grads_body, n),
            [shape((rows, cols))] * n + [shape((2 * rows, cols))],
            [vm()] * 3,
            flops=2 * rows * width * cols,
        )(out_grad[:, 0], *wouts)
        piece = (n - 1, up_rows + feats // (2 * parts), 2 * down_cols)
        up, down, near, message, inner_rows = call(
            functools.partial(line_body, n, up_rows),
            [shape(piece)] * 2
            + [shape((rest + size, cols)) for size in (0, 2 * rows + PAD, own_shape.shape[0])],
            [vm()] * (n + 2),
            deps=[gains[1]],
        )(*line, own, far_grads)
        inner, outer = [(1, 2), (2, 1)], [(1, 0), (2, 3)]
        up1, down2 = xor_move(up, "dp", 1), xor_move(down, "dp", 2)
        far_inner = lax.ppermute(inner_rows, "mp", inner)
        message = xor_move(message, "mp", 1)
        ups, downs, message, near = call(
            pair_body,
            [shape((2,) + piece)] * 2 + [shape((rest + 2 * rows, cols)), own_shape],
            [vm()] * 8,
            deps=[far_inner],
        )(up, up1, down, down2, near, message, grads[1], grads[2])
        up2, down1 = xor_move(ups, "dp", 2), xor_move(downs, "dp", 1)
        next_outer = lax.ppermute(far_inner, "mp", outer)
        message = lax.ppermute(message, "mp", inner)
        gathered, close, wkv = call(
            gather_body,
            [shape((parts,) + piece), shape((rest + rows, cols)), shape((2 * enc_width, cols))],
            [vm()] * 10,
            deps=[next_outer, normed],
        )(up, up1, up2, down, down2, down1, message, grads[3], wk, wv)
        pieces = [gathered, swap(gathered), enc_up, down_t, *wqs]
        close = xor_move(close, "mp", 1)
        grad_parts = [grads[0], message, close]
        row_pieces = [own, near, far_inner, next_outer, message, close]
        before_projected = [close]
        scratch = [
            pltpu.VMEM((n, parts, up_rows, enc_up.shape[1]), BF16),
            pltpu.VMEM((n, enc_width // n, ff), BF16),
        ]
    else:
        own = call(
            functools.partial(rows_body, cols), [shape((rows * feats // cols, cols))], [vm()]
        )(segment_input[:, 0])[0]
        grad_parts = call(
            functools.partial(out_grads_body, n),
            [shape((rows, cols))] * n,
            [vm()] * 3,
            flops=2 * rows * width * cols,
        )(out_grad[:, 0], *wouts)
        row_pieces, grad_parts = along_mp(own, n), scattered(list(grad_parts))
        query_shares = call(
            functools.partial(query_shares_body, n), [shape((feats, cols))] * n, [vm()] * 2
        )(*wqs)
        projection = jnp.stack(scattered(query_shares))
        wkv = jnp.concatenate([wk, wv], axis=0)
        before_projected = []
        pieces = [
            lax.all_gather(enc_up, "mp", axis=0),
            lax.all_gather(down_t, "mp", axis=0, tiled=True),
        ]
        scratch = [
            pltpu.VMEM((n, enc_width, enc_up.shape[1]), BF16),
            pltpu.VMEM((enc_width, ff), BF16),
            pltpu.SemaphoreType.DMA((2,)),
        ]

    wkvs = (wkv, swap(wkv))

    encoded = call(
        functools.partial(encoder_body, n, parts, not shares),
        [shape((half * length, enc_width))] + [shape((n, feats, cols))] * shares,
        [vm()] * 8 if shares else [vm()] * 2 + [hbm()] * 2,
        [pltpu.VMEM((half * length, ff), BF16)] + scratch,
        flops=4 * half * length * enc_width * ff,
        limit=ENCODER_LIMIT if shares else 48 * 1024 * 1024,
    )(pool_rows, normed, *pieces)
    enc = encoded[0]
    if shares:
        projection = encoded[1]
    pool0_own, enc_own = (
        call(
            functools.partial(projected_body, layer),
            [shape((half, length, layer * enc_width + 2 * cols))],
            [vm()] * 3,
            flops=4 * half * length * enc_width * cols,
            deps=before_projected,
        )(enc, *wkvs)[0]
        for layer in (0, 1)
    )
    pool0_other = swap(pool0_own)
    heads = cols // HEAD
    chunk = rows // tracts
    slot_rows = tracts * slots * NT
    wide_scores = pltpu.VMEM((tracts * heads, chunk, slots * NT), F32)
    bf_scores = pltpu.VMEM((tracts * heads, chunk, slots * NT), BF16)
    attention_flops = 2 * rows * slots * NT * cols

    wide_shape = shape((tracts * heads, chunk, slots * NT), F32)
    block_shape = shape((slot_rows, 2 * cols))
    query0 = call(
        functools.partial(query_body, n),
        [shape((rows, cols))],
        [vm()] * (4 + len(row_pieces)),
        flops=2 * rows * width * cols,
        deps=[pool0_own],
    )(*gains, *wqs, *row_pieces)[0]
    att, probs0, blocks0, enc_own = call(
        functools.partial(first_layer_body, tracts, slots),
        [shape((rows, cols)), wide_shape, block_shape],
        [smem(), smem()] + [vm()] * 3,
        flops=2 * attention_flops,
        passing=[enc_own],
    )(ids, counts, query0, pool0_own, pool0_other)
    enc_other = swap(enc_own)
    att_pieces = along_mp(att, n)
    rows1, *messages = call(
        functools.partial(between_body, n),
        [shape((rows, feats))] + [shape((rows + PAD, cols))] * n,
        [vm()] * (6 + n),
        flops=4 * rows * feats * n * cols,
        deps=[enc_other],
    )(*gains, own, *wouts, projection, *att_pieces)
    query_pieces = scattered(messages)
    bf_shape = shape((tracts * heads, chunk, slots * NT))
    blocks1, att1, prob_grads1 = call(
        functools.partial(last_values_body, tracts, slots),
        [block_shape, shape((rows, cols)), wide_shape],
        [smem()] + [vm()] * (len(grad_parts) + 2),
        flops=attention_flops,
    )(ids, *grad_parts, enc_own, enc_other)
    grad_query, scale1, query1, *soft1 = call(
        functools.partial(last_layer_body, n, width, tracts, slots),
        [shape((rows + PAD, cols)), shape((rows, HEAD), F32), shape((rows, cols))] + [bf_shape] * 2,
        [smem()] + [vm()] * (n + 2),
        [pltpu.VMEM((rows, cols), F32), wide_scores],
        flops=3 * attention_flops,
    )(counts, *query_pieces, blocks1, prob_grads1)
    dkv1 = call(
        functools.partial(last_slots_body, tracts, slots),
        [shape((slot_rows, 2 * cols))],
        [vm()] * 4,
        flops=2 * attention_flops,
    )(query1, att1, *soft1)[0]
    query_grads = along_mp(grad_query, n)
    enc_slots, kept1, sent1 = call(
        functools.partial(last_grads_body, tracts, slots),
        [shape((enc_width, slot_rows)), shape((enc_width, cols)), shape((enc_width, cols))],
        [smem(), vm(), vm(), vm()],
        flops=4 * enc_width * slot_rows * cols,
    )(ids, dkv1, enc_own, enc_other)
    *messages, kept1, sent1 = call(
        functools.partial(back_between_body, n, width),
        [shape((rows, cols))] * n,
        [vm()] * (8 + n),
        flops=4 * rows * feats * n * cols,
        passing=[kept1, sent1],
    )(*gains, rows1, out_grad[:, 0], scale1, projection, *wouts, *query_grads)
    grad_pieces0 = scattered(messages)

    def over_dp(parts, order):
        size = len(parts)
        moved = [None] * size
        for by in sorted(set(order)):
            members = [i for i in range(size) if order[i] == by]
            if len(members) == 1:
                moved[members[0]] = xor_move(parts[members[0]], "dp", by)
                continue
            message = xor_move(jnp.concatenate([parts[i] for i in members], axis=0), "dp", by)
            start = 0
            for i in members:
                moved[i] = lax.slice_in_dim(message, start, start + parts[i].shape[0])
                start += parts[i].shape[0]
        shapes = [shape(part.shape) for part in parts]
        return call(functools.partial(add_body, size), shapes, [vm()] * (2 * size))(*parts, *moved)

    def pieces_of(kept, sent, sizes):
        parts = [shape((size, cols)) for size in sizes]
        return call(pieces_body, parts, [vm()] * 2)(kept, swap(sent))

    size = enc_width // 2
    early = size // 2 + 32 if size % 64 == 0 else size // 2
    ax, bx, ay, by = pieces_of(kept1, sent1, [early, size - early] * 2)
    if dp == 4:
        ax, ay = over_dp([ax, ay], (1, 2))
    dkv0 = call(
        functools.partial(first_back_body, n, tracts, slots),
        [shape((slot_rows, 2 * cols))],
        [vm()] * (n + 3),
        [pltpu.VMEM((rows, cols), BF16), wide_scores, bf_scores, bf_scores],
        flops=3 * attention_flops,
    )(query0, probs0, blocks0, *grad_pieces0)[0]
    sent0, kept0 = (
        call(
            functools.partial(part_grads_body, keep),
            [shape((enc_width, cols))],
            [vm()] * 2,
            flops=2 * enc_width * slot_rows * cols,
            deps=[] if keep else [ax, ay],
        )(enc_slots, dkv0)[0]
        for keep in (False, True)
    )
    top, bottom = pieces_of(kept0, sent0, [size] * 2)
    if dp == 4:
        top, bottom, ax, ay, bx, by = over_dp([top, bottom, ax, ay, bx, by], (1, 2, 2, 1, 1, 2))
        top, bottom, bx, by = over_dp([top, bottom, bx, by], (2, 1, 2, 1))
    else:
        top, bottom, ax, ay, bx, by = lax.psum((top, bottom, ax, ay, bx, by), "dp")
    sum0 = jnp.concatenate([top, bottom], axis=0)
    sum1 = jnp.concatenate([ax, bx, ay, by], axis=0)
    received = swap(jnp.where(first, sum1, sum0))
    key_total = jnp.where(first, sum0, received)
    value_total = jnp.where(first, received, sum1)
    return (key_total[None], value_total[None])


def solution(mesh):
    placed = (
        P(None, "dp", None, "mp"),
        P(None, "dp", None, "mp"),
        P("section", "dp", None, None),
        P(None, "dp", None, None),
        P(None, "dp", None),
        P(),
        P(None, "mp"),
        P(None, "mp"),
        P("section", None),
        P("section", None, "mp"),
        P("section", None, "mp"),
        P("section", None, "mp"),
        P("section", None, "mp"),
    )
    return jax.shard_map(
        on_device,
        mesh=mesh,
        in_specs=placed,
        out_specs=(P("section", None, "mp"), P("section", None, "mp")),
        check_vma=False,
    )
```
